32 devices in a mesh: sec: 4 (over x, core), tile: 8 (over z, y).
Axes of the slice: x: 2, y: 2, z: 4, core: 2. Of those that a mesh axis runs over, the one named last changes fastest.
Arguments:
- state: float32 [4, 128, 4096], P('sec', None, 'tile'), may hold values from -6 to 6
- tendency: bfloat16 [4, 128, 4096], P('sec', None, 'tile'), may hold values from -4 to 4
- diffusion: bfloat16 [4, 128, 4096], P('sec', None, 'tile'), may hold values from 0.019897461 to 0.23925781
- mixing: float32 [4, 128, 128], P('sec')
- coupling: float32 [4, 128], P('sec'), may hold values from 0.05 to 0.4
- remap_index: int32 [4, 4, 4096], P('sec', None, 'tile'), may hold values from 0 to 1535, as said below
- remap_weight: float32 [4, 4, 4096], P('sec', None, 'tile'), may hold values from 0.1 to 0.4
- active_cols: int32 [4], replicated, may hold values from 256 to 512
- send_cols: int32 [2, 4, 8, 8, 4], P(None, 'sec', 'tile'), may hold values from 0 to 511
- occ_slot: int32 [2, 4, 8, 512], P(None, 'sec', None, 'tile'), may hold values from 0 to 31
- occ_weight: float32 [2, 4, 8, 512], P(None, 'sec', None, 'tile'), may hold values from 0.2 to 0.6
- occ_count: int32 [2, 4, 512], P(None, 'sec', 'tile'), may hold values from 1 to 8
- refraction: float32 [4, 128, 128], P('sec'), may hold values from -0.5 to 0.5
- abel_matrix: float32 [128, 256], replicated
- observed: float32 [2, 512, 256], P(None, ('sec', 'tile')), may hold values from -6 to 6
Outputs:
- final_state: float32 [4, 128, 4096], P('sec', None, 'tile')
- departures: float32 [2, 512, 256], P(None, ('sec', 'tile'))
The draws below stay inside these ranges and needn't reach their ends.
Inputs may be any that keep to these rules, and one draw needn't show every extreme that they name: `remap_index`: for an atmosphere section the value is a column within the tile of the ocean section; for the last section, value // 512 is the atmosphere section and value % 512 the column within the tile.
All inputs are finite; a program needn't handle non-finite values.
Results may differ from the reference program's by a relative error of at most 0.00035.
Values sent between devices are 32-bit elements; how exact they have to be, the bound alone decides.
A program may use at most 64 MiB of HBM per device.

```python
import math
import jax
import jax.numpy as jnp
from jax import lax

LEV = 128
COLS = 512
SUBS = 4
STEPS = 2
RK = 4
CAP = 4
TPMAX = 8
NB = 256
OQ = 16
SECTIONS = 4
TILES = 8
NCOL = 4096
OCC_TILE = 64
OCCS = 512


def draw_mixing(key, part):
    key_diag, key_rest = jax.random.split(key)
    diagonal = jax.random.uniform(key_diag, (SECTIONS, LEV), jnp.float32, 0.5, 0.65)
    spread = jax.random.uniform(key_rest, (SECTIONS, LEV, LEV), jnp.float32, -1.0, 1.0) * (0.35 / (LEV - 1))
    unit_diag = jnp.eye(LEV, dtype=jnp.float32)[None]
    return spread * (1.0 - unit_diag) + unit_diag * diagonal[:, :, None]


def draw_remap_index(key, part):
    drawn = jax.random.randint(key, (SECTIONS, RK, NCOL), 0, (SECTIONS - 1) * COLS)
    ocean_rows = (jnp.arange(SECTIONS) == SECTIONS - 1)[:, None, None]
    return jnp.where(ocean_rows, drawn, drawn % COLS).astype(jnp.int32)


def draw_active_cols(key, part):
    mixed_key = jax.random.fold_in(key, part)
    key_order, key_value = jax.random.split(mixed_key)
    drawn = jax.random.randint(key_value, (SECTIONS,), COLS // 2, COLS + 1)
    order = jax.random.permutation(key_order, SECTIONS)
    drawn = jnp.where(order == 0, COLS, drawn)
    drawn = jnp.where(order == 1, COLS // 2, drawn)
    return drawn.astype(jnp.int32)


def draw_abel_matrix(key, part):
    entries = jax.random.uniform(key, (LEV, NB), jnp.float32, 0.5, 1.5)
    level_index = jnp.arange(LEV)[:, None]
    height_index = jnp.arange(NB)[None, :]
    above_height = level_index * NB <= (NB - 1 - height_index) * LEV
    return jnp.where(above_height, entries, 0.0) * (1.0 / math.sqrt(LEV))


def place_ends(values, key, least, high):
    place = [jax.random.randint(jax.random.fold_in(key, axis), (), 0, length) for axis, length in enumerate(values.shape)]
    widest = values.shape.index(max(values.shape))
    neighbour = place[:widest] + [(place[widest] + 1) % values.shape[widest]] + place[widest + 1:]
    return values.at[tuple(place)].set(least).at[tuple(neighbour)].set(high)


def levels(own_key, shape, shards, smallest, top_value):
    def one(axis_at, blocks):
        heights = jax.random.uniform(jax.random.fold_in(jax.random.fold_in(own_key, 6), axis_at), (blocks,), jnp.float32, smallest / len(shards), top_value / len(shards))
        return jnp.repeat(jnp.exp(heights), shape[axis_at] // blocks).reshape((-1,) + (1,) * (len(shape) - axis_at - 1))

    level = one(*shards[0])
    for cut in shards[1:]:
        level = level * one(*cut)
    return level


def bell_draw(rng, extent, deviation, most, cuts=(), kind=jnp.bfloat16):
    values = deviation * jax.random.normal(rng, extent, jnp.float32)
    if cuts:
        values = values * levels(rng, extent, cuts, -0.22, 0.18)
    return jnp.clip(values, -most, most).astype(kind)


def setup_inputs(seed: int = 0) -> dict:
    seeds = jax.random.split(jax.random.key(seed), 16)
    state = bell_draw(seeds[0], (SECTIONS, LEV, NCOL), 1.0, 6.0, ((0, 4), (2, 8)), jnp.float32)
    tendency = bell_draw(seeds[1], (SECTIONS, LEV, NCOL), 0.3, 4.0, ((0, 4), (2, 8)))
    diffusion = jnp.clip(0.019897461 + 0.21936035 * jax.random.uniform(seeds[2], (SECTIONS, LEV, NCOL), jnp.float32) ** levels(seeds[2], (SECTIONS, LEV, NCOL), ((0, 4), (2, 8)), -0.2, 0.2), 0.019897461, 0.23925781).astype(jnp.bfloat16)
    mixing = draw_mixing(jax.random.fold_in(seeds[15], 71), 0)
    coupling = jnp.clip(0.05 + 0.35 * jax.random.uniform(seeds[4], (SECTIONS, LEV), jnp.float32) ** levels(seeds[4], (SECTIONS, LEV), ((0, 4),), -0.2, 0.2), 0.05, 0.4)
    remap_index = draw_remap_index(jax.random.fold_in(seeds[15], 71), 0)
    remap_weight = jnp.clip(0.1 + 0.3 * jax.random.uniform(seeds[6], (SECTIONS, RK, NCOL), jnp.float32) ** levels(seeds[6], (SECTIONS, RK, NCOL), ((0, 4), (2, 8)), -0.2, 0.2), 0.1, 0.4)
    active_cols = draw_active_cols(jax.random.fold_in(seeds[15], 71), 0)
    send_cols = place_ends(jax.random.randint(seeds[8], (STEPS, SECTIONS, TILES, TILES, CAP), 0, COLS), jax.random.fold_in(seeds[8], 1), 0, COLS - 1).astype(jnp.int32)
    occ_slot = place_ends(jax.random.randint(seeds[9], (STEPS, SECTIONS, TPMAX, TILES * OCC_TILE), 0, TILES * CAP), jax.random.fold_in(seeds[9], 1), 0, (TILES * CAP) - 1).astype(jnp.int32)
    occ_weight = jnp.clip(0.2 + 0.400000021 * jax.random.uniform(seeds[10], (STEPS, SECTIONS, TPMAX, TILES * OCC_TILE), jnp.float32) ** levels(seeds[10], (STEPS, SECTIONS, TPMAX, TILES * OCC_TILE), ((1, 4), (3, 8)), -0.2, 0.2), 0.2, 0.6)
    occ_count = place_ends(jax.random.randint(seeds[11], (STEPS, SECTIONS, TILES * OCC_TILE), 1, TPMAX + 1), jax.random.fold_in(seeds[11], 1), 1, TPMAX).astype(jnp.int32)
    refraction = bell_draw(seeds[12], (SECTIONS, LEV, LEV), LEV ** -0.5, 0.5, ((0, 4),), jnp.float32)
    abel_matrix = draw_abel_matrix(jax.random.fold_in(seeds[15], 71), 0)
    observed = bell_draw(seeds[14], (STEPS, OCCS, NB), 1.0, 6.0, ((1, 32),), jnp.float32)
    return dict(state=state, tendency=tendency, diffusion=diffusion, mixing=mixing, coupling=coupling, remap_index=remap_index, remap_weight=remap_weight, active_cols=active_cols, send_cols=send_cols, occ_slot=occ_slot, occ_weight=occ_weight, occ_count=occ_count, refraction=refraction, abel_matrix=abel_matrix, observed=observed)


def observe(field, sent, slots, weights, counts, refraction, abel_matrix, observed_step):
    highest = lax.Precision.HIGHEST
    owner_tile = jnp.arange(TILES * OCC_TILE, dtype=jnp.int32) // OCC_TILE
    source_tile = slots // CAP
    slot_index = slots % CAP
    section_ids = jnp.arange(SECTIONS, dtype=jnp.int32)[:, None, None]
    column_ids = source_tile * COLS + sent[section_ids, source_tile, owner_tile[None, None, :], slot_index]
    values = field[section_ids, :, column_ids]
    tangent_live = jnp.arange(TPMAX, dtype=jnp.int32)[None, :, None] < counts[:, None, :]
    live_weight = jnp.where(tangent_live, weights, 0.0)
    profile = jnp.sum(live_weight[..., None] * values, axis=1)
    projected = jnp.einsum('snl,slm->snm', profile, refraction, precision=highest)
    bending = jnp.einsum('snm,mb->nb', projected, abel_matrix, precision=highest)
    bending = bending.reshape(TILES, SECTIONS, OQ, NB).transpose(1, 0, 2, 3).reshape(OCCS, NB)
    return observed_step - bending


def reference(state, tendency, diffusion, mixing, coupling, remap_index, remap_weight, active_cols, send_cols, occ_slot, occ_weight, occ_count, refraction, abel_matrix, observed):
    highest = lax.Precision.HIGHEST
    column_ids = jnp.arange(NCOL, dtype=jnp.int32)
    local_index = column_ids % COLS
    tile_base = (column_ids // COLS) * COLS
    live_mask = local_index[None, :] < active_cols[:, None]
    section_ids = jnp.arange(SECTIONS, dtype=jnp.int32)
    ocean_rows = (section_ids == SECTIONS - 1)[:, None, None]
    source_section = jnp.where(ocean_rows, remap_index // COLS, SECTIONS - 1).astype(jnp.int32)
    source_column = (tile_base[None, None, :] + jnp.where(ocean_rows, remap_index % COLS, remap_index)).astype(jnp.int32)
    rates = diffusion.astype(jnp.float32)
    forcing = tendency.astype(jnp.float32)
    field = state
    results = []
    for period in range(STEPS):
        surface = field[:, LEV - 1, :]
        picked = surface[source_section, source_column]
        boundary = jnp.sum(remap_weight * picked, axis=1) - surface
        for substep in range(SUBS):
            spread = field + rates * (jnp.roll(field, 1, 2) + jnp.roll(field, -1, 2) - 2.0 * field)
            stepped = jnp.einsum('sij,sjc->sic', mixing, spread, precision=highest)
            stepped = stepped + coupling[:, :, None] * boundary[:, None, :] + forcing
            field = jnp.where(live_mask[:, None, :], stepped, field)
        results.append(observe(field, send_cols[period], occ_slot[period], occ_weight[period], occ_count[period], refraction, abel_matrix, observed[period]))
    return field, jnp.stack(results)
```

```python
import functools

import jax
import jax.numpy as jnp
from jax import lax
from jax.experimental import pallas as pl
from jax.experimental.pallas import tpu as pltpu
from jax.sharding import PartitionSpec as P

SUBS = 4
STEPS = 2
HALO = SUBS * STEPS
LANES = 128
PACK = 3 * HALO + 8
F32 = jnp.float32
BF16 = jnp.bfloat16
MESH = pl.DeviceIdType.MESH


def split(x):
    high = x.astype(BF16)
    low = (x - high.astype(F32)).astype(BF16)
    return high, low


def mm(a, b, dims):
    return lax.dot_general(a, b, (dims, ((), ())), preferred_element_type=F32)


NN = ((1,), (0,))
NT = ((1,), (1,))
TN = ((0,), (0,))


def dot3(a, b, dims=NN):
    ah, al = split(a)
    bh, bl = split(b)
    return mm(ah, bh, dims) + (mm(ah, bl, dims) + mm(al, bh, dims))


def kernel(
    sections,
    tiles,
    state,
    tendency,
    diffusion,
    mixing,
    coupling,
    remap_index,
    remap_weight,
    active_cols,
    send_cols,
    occ_slot,
    occ_weight,
    occ_count,
    refraction,
    abel_matrix,
    observed,
    out_state,
    out_departures,
    field,
    rates,
    forcing,
    tend_v,
    diff_v,
    mix_v,
    coup_v,
    ridx_v,
    rw_v,
    cols_v,
    slot_v,
    ow_v,
    oc_v,
    refr_v,
    abel_v,
    obs_v,
    dep_v,
    mix_a,
    mix_b,
    gain,
    position,
    weight,
    picked,
    surf,
    tab,
    pack_out,
    pack_in,
    chosen_out,
    chosen_in,
    parts_out,
    parts_in,
    load_sem,
    store_sem,
    pack_send,
    pack_recv,
    surf_send,
    surf_recv,
    col_send,
    col_recv,
    red_send,
    red_recv,
):
    levels, columns = tend_v.shape
    ext = field.shape[1]
    blocks = columns // LANES
    rk = ridx_v.shape[0]
    s = lax.axis_index("sec")
    t = lax.axis_index("tile")
    ocean = sections - 1
    is_ocean = s == ocean
    right = lax.rem(t + 1, tiles)
    left = lax.rem(t + tiles - 1, tiles)
    near = ((t, 0), (left, 1), (right, 2))

    loads = [
        (state.at[0], field.at[:, 0:columns]),
        (diffusion.at[0], diff_v),
        (tendency.at[0], tend_v),
        (remap_index.at[0], ridx_v),
        (remap_weight.at[0], rw_v),
        (mixing.at[0], mix_v),
        (coupling, coup_v),
        (send_cols, cols_v),
        (occ_slot, slot_v),
        (occ_weight, ow_v),
        (occ_count, oc_v),
        (refraction.at[0], refr_v),
        (abel_matrix, abel_v),
        (observed, obs_v),
    ]
    loads = [pltpu.make_async_copy(a, b, load_sem.at[i]) for i, (a, b) in enumerate(loads)]
    for load in loads:
        load.start()

    def over_tiles(body):
        if tiles <= 8:
            for d in range(1, tiles):
                body(lax.rem(t + d, tiles))
        else:
            lax.fori_loop(1, tiles, lambda d, c: (body(lax.rem(t + d, tiles)), c)[1], 0)

    barrier = pltpu.get_barrier_semaphore()

    def greet(sec, tile):
        pl.semaphore_signal(barrier, inc=1, device_id=(sec, tile), device_id_type=MESH)

    over_tiles(lambda other: greet(s, other))
    for d in range(1, sections):
        greet(lax.rem(s + d, sections), t)

    @pl.when(is_ocean)
    def _():
        for a in range(ocean):
            greet(a, left)
            greet(a, right)

    @pl.when(jnp.logical_not(is_ocean))
    def _():
        greet(ocean, left)
        greet(ocean, right)

    lane = lax.broadcasted_iota(jnp.int32, (levels, LANES), 1)
    row_lane = lax.broadcasted_iota(jnp.int32, (1, LANES), 1)

    for load in loads[:5]:
        load.wait()
    surf[0] = field[levels - 1 : levels, 0:columns]

    tail = columns - LANES
    idx_f = ridx_v[...].astype(F32)

    def pack(slot, lo, shift):
        a = field[:, lo : lo + LANES]
        b = diff_v[:, lo : lo + LANES].astype(F32)
        c = tend_v[:, lo : lo + LANES].astype(F32)
        if shift:
            a = pltpu.roll(a, shift, 1)
        b = pltpu.roll(b, shift + HALO, 1)
        c = pltpu.roll(c, shift + 2 * HALO, 1)
        mixed = jnp.where(lane < HALO, a, jnp.where(lane < 2 * HALO, b, c))
        pack_out[slot, 0 : 3 * HALO, :] = mixed.T[0 : 3 * HALO]
        pack_out[slot, 3 * HALO : 3 * HALO + rk, :] = idx_f[:, lo : lo + LANES]
        pack_out[slot, 3 * HALO + rk : PACK, :] = rw_v[:, lo : lo + LANES]

    pack(0, 0, 0)
    pack(1, tail, HALO)

    meet = (tiles - 1) + (sections - 1) + jnp.where(is_ocean, 2 * ocean, 2)
    pl.semaphore_wait(barrier, meet)

    def pack_copy(slot, tile):
        return pltpu.make_async_remote_copy(
            src_ref=pack_out.at[slot],
            dst_ref=pack_in.at[slot],
            send_sem=pack_send.at[slot],
            recv_sem=pack_recv.at[slot],
            device_id=(s, tile),
            device_id_type=MESH,
        )

    def surf_copy(p, d, a, sec, tile, mark):
        return pltpu.make_async_remote_copy(
            src_ref=surf.at[p],
            dst_ref=tab.at[p, d, a],
            send_sem=surf_send.at[p, d, mark],
            recv_sem=surf_recv.at[p, d, a],
            device_id=(sec, tile),
            device_id_type=MESH,
        )

    def surf_each(p, act):
        @pl.when(is_ocean)
        def _():
            for tile, d in near:
                for a in range(ocean):
                    act(surf_copy(p, d, 0, a, tile, a))

        @pl.when(jnp.logical_not(is_ocean))
        def _():
            for tile, d in near:
                act(surf_copy(p, d, s, ocean, tile, 0))

    packs = (pack_copy(0, left), pack_copy(1, right))
    for copy in packs:
        copy.start()
    surf_each(0, lambda copy: copy.start())

    for load in loads[5:]:
        load.wait()
    mh, ml = split(mix_v[...])
    mix_a[:, 0:levels] = mh
    mix_a[:, levels : 2 * levels] = mh
    mix_b[...] = ml
    gain[...] = jnp.broadcast_to(coup_v[...], (LANES, levels)).T
    rates[:, 0:columns] = diff_v[...].astype(F32)
    forcing[:, 0:columns] = tend_v[...].astype(F32)
    for b in range(blocks):
        position[b * rk : (b + 1) * rk, :] = ridx_v[:, b * LANES : (b + 1) * LANES]
        weight[b * rk : (b + 1) * rk, :] = rw_v[:, b * LANES : (b + 1) * LANES]

    limit = active_cols[s]
    number = lax.broadcasted_iota(jnp.int32, (1, ext), 1)
    number = jnp.where(
        number < columns, number, jnp.where(number < columns + LANES // 2, number - columns, number - LANES)
    )
    live = number < limit

    cap = cols_v.shape[4]
    rows = tiles * 8

    def selector(p):
        which = lax.broadcasted_iota(jnp.int32, (rows, tiles), 0)
        owner = lax.broadcasted_iota(jnp.int32, (rows, tiles), 1)
        expand = jnp.where(lax.shift_right_logical(which, 3) == owner, 1.0, 0.0)
        listed = jnp.dot(
            expand, cols_v[p, 0, 0].astype(F32), precision=lax.Precision.HIGHEST, preferred_element_type=F32
        )
        r = lax.broadcasted_iota(jnp.int32, (rows, cap), 0)
        c = lax.broadcasted_iota(jnp.int32, (rows, cap), 1)
        column = jnp.sum(jnp.where((r & 7) == c, listed, 0.0), axis=1, keepdims=True)
        rr = lax.broadcasted_iota(jnp.int32, (rows, columns), 0)
        cc = lax.broadcasted_iota(jnp.int32, (rows, columns), 1)
        hit = jnp.logical_and(cc == column.astype(jnp.int32), (rr & 7) < cap)
        return jnp.where(hit, 1.0, 0.0).astype(BF16)

    def occultation_weights(p):
        shape = (rows, slot_v.shape[3])
        m = lax.broadcasted_iota(jnp.int32, shape, 0)
        key = jnp.where((m & 7) < cap, lax.shift_right_logical(m, 3) * cap + (m & 7), -1)
        counts = oc_v[p]
        total = jnp.zeros(shape, F32)
        for k in range(slot_v.shape[2]):
            w = jnp.where(counts > k, ow_v[p, 0, k : k + 1, :], 0.0)
            total = total + jnp.where(key == slot_v[p, 0, k : k + 1, :], w, 0.0)
        return total

    def mixed_spread():
        f = field[...]
        around = pltpu.roll(f, 1, 1) + pltpu.roll(f, ext - 1, 1)
        spread = f + rates[...] * (around - 2.0 * f)
        xh, xl = split(spread)
        return mm(mix_a[...], jnp.concatenate([xh, xl], axis=0), NN) + mm(mix_b[...], xh, NN)

    def boundary_of(p):
        pos = position[...]
        inner = pos & (LANES - 1)
        outer = lax.shift_right_logical(pos, 7)

        def look(a):
            for d in range(3):
                pltpu.make_async_remote_copy(
                    src_ref=surf.at[p],
                    dst_ref=tab.at[p, d, a],
                    send_sem=surf_send.at[p, d, 0],
                    recv_sem=surf_recv.at[p, d, a],
                    device_id=(s, right),
                    device_id_type=MESH,
                ).wait_recv()
            found = picked[...]
            for b in range(blocks):
                at = slice(b * LANES, (b + 1) * LANES)
                table = jnp.concatenate(
                    [
                        jnp.broadcast_to(tab[p, 0, a, :, at], (blocks * rk, LANES)),
                        jnp.broadcast_to(tab[p, 1, a, :, at], (rk, LANES)),
                        jnp.broadcast_to(tab[p, 2, a, :, at], (rk, LANES)),
                    ],
                    axis=0,
                )
                got = jnp.take_along_axis(table, inner, axis=1, mode="promise_in_bounds")
                found = jnp.where(outer == a * blocks + b, got, found)
            picked[...] = found

        picked[...] = jnp.zeros(picked.shape, F32)
        look(0)

        @pl.when(is_ocean)
        def _():
            for a in range(1, ocean):
                look(a)

        terms = picked[...] * weight[...]
        sums = [jnp.sum(terms[b * rk : (b + 1) * rk], axis=0, keepdims=True) for b in range(blocks + 2)]
        sums[blocks] = jnp.where(row_lane < LANES // 2, sums[blocks], sums[blocks + 1])
        return [
            sums[b] - field[levels - 1 : levels, b * LANES : (b + 1) * LANES] for b in range(blocks + 1)
        ]

    def coupling_step(p):
        product = mixed_spread()
        boundary = boundary_of(p)
        push = jnp.concatenate([gain[...] * row for row in boundary], axis=1)
        push = push + forcing[...]
        field[...] = jnp.where(live, product + push, field[...])
        for _ in range(SUBS - 1):
            field[...] = jnp.where(live, mixed_spread() + push, field[...])

    def column_copy(p, other, source):
        return pltpu.make_async_remote_copy(
            src_ref=chosen_out.at[p, other],
            dst_ref=chosen_in.at[p, source],
            send_sem=col_send.at[p, other],
            recv_sem=col_recv.at[p, source],
            device_id=(s, other),
            device_id_type=MESH,
        )

    def send_columns(p, pick):
        fh, fl = split(field[:, 0:columns])
        taken = mm(pick, fh, NT) + mm(pick, fl, NT)
        projected = dot3(taken, refr_v[...]).reshape(tiles, 8, levels)
        chosen_out[p] = projected
        over_tiles(lambda other: column_copy(p, other, t).start())
        chosen_in[p, t] = chosen_out[p, t]

    own = parts_out.shape[2]

    def part_copy(p, other, source):
        return pltpu.make_async_remote_copy(
            src_ref=parts_out.at[p, other],
            dst_ref=parts_in.at[p, source],
            send_sem=red_send.at[p, other],
            recv_sem=red_recv.at[p, source],
            device_id=(other, t),
            device_id_type=MESH,
        )

    def others():
        return [lax.rem(s + d, sections) for d in range(1, sections)]

    def send_parts(p, w):
        over_tiles(lambda other: column_copy(p, other, other).wait_recv())
        part = dot3(w, chosen_in[p].reshape(rows, levels), TN)
        parts_out[p] = part.reshape(sections, own, levels)
        for other in others():
            part_copy(p, other, s).start()
        parts_in[p, s] = parts_out[p, s]

    def depart(p):
        for other in others():
            part_copy(p, other, other).wait_recv()
        total = parts_in[p, 0]
        for a in range(1, sections):
            total = total + parts_in[p, a]
        dep_v[p] = obs_v[p] - dot3(total, abel_v[...])

    picks = [selector(p) for p in range(STEPS)]
    occ = [occultation_weights(p) for p in range(STEPS)]

    for copy in packs:
        copy.wait_recv()
    gap = jnp.zeros((LANES - 2 * HALO, levels), F32)

    def pad(i):
        at = slice(i * HALO, (i + 1) * HALO)
        return jnp.concatenate([pack_in[0, at, :], gap, pack_in[1, at, :]], axis=0).T

    field[:, columns:ext] = pad(0)
    rates[:, columns:ext] = pad(1)
    forcing[:, columns:ext] = pad(2)
    for i in range(2):
        at = slice((blocks + i) * rk, (blocks + i + 1) * rk)
        position[at, :] = pack_in[i, 3 * HALO : 3 * HALO + rk, :].astype(jnp.int32)
        weight[at, :] = pack_in[i, 3 * HALO + rk : PACK, :]

    coupling_step(0)
    surf[1] = field[levels - 1 : levels, 0:columns]
    surf_each(1, lambda copy: copy.start())
    send_columns(0, picks[0])
    coupling_step(1)
    stores = [pltpu.make_async_copy(field.at[:, 0:columns], out_state.at[0], store_sem.at[0])]
    stores[0].start()
    send_columns(1, picks[1])
    send_parts(0, occ[0])
    send_parts(1, occ[1])
    depart(0)
    depart(1)
    stores.append(pltpu.make_async_copy(dep_v, out_departures, store_sem.at[1]))
    stores[1].start()

    for copy in packs:
        copy.wait_send()
    for p in range(STEPS):
        surf_each(p, lambda copy: copy.wait_send())
        over_tiles(lambda other: column_copy(p, other, t).wait_send())
        for other in others():
            part_copy(p, other, s).wait_send()
    for store in stores:
        store.wait()


def shards(sections, tiles, *args):
    (state, tendency, diffusion, mixing, coupling, remap_index, remap_weight, active_cols, send_cols) = args[:9]
    (occ_slot, occ_weight, occ_count, refraction, abel_matrix, observed) = args[9:]
    levels, columns = state.shape[1:]
    rk = remap_index.shape[1]
    ext = columns + LANES
    slots = (columns // LANES + 2) * rk
    own = observed.shape[1]
    heights = abel_matrix.shape[1]
    dma = pltpu.SemaphoreType.DMA
    any_spec = pl.BlockSpec(memory_space=pl.ANY)
    smem = pl.BlockSpec(memory_space=pltpu.SMEM)
    specs = [any_spec] * len(args)
    specs[7] = smem
    scratch = [
        pltpu.VMEM((levels, ext), F32),
        pltpu.VMEM((levels, ext), F32),
        pltpu.VMEM((levels, ext), F32),
        pltpu.VMEM((levels, columns), BF16),
        pltpu.VMEM((levels, columns), BF16),
        pltpu.VMEM((levels, levels), F32),
        pltpu.VMEM(coupling.shape, F32),
        pltpu.VMEM((rk, columns), jnp.int32),
        pltpu.VMEM((rk, columns), F32),
        pltpu.VMEM(send_cols.shape, jnp.int32),
        pltpu.VMEM(occ_slot.shape, jnp.int32),
        pltpu.VMEM(occ_weight.shape, F32),
        pltpu.VMEM(occ_count.shape, jnp.int32),
        pltpu.VMEM((levels, levels), F32),
        pltpu.VMEM(abel_matrix.shape, F32),
        pltpu.VMEM(observed.shape, F32),
        pltpu.VMEM(observed.shape, F32),
        pltpu.VMEM((levels, 2 * levels), BF16),
        pltpu.VMEM((levels, levels), BF16),
        pltpu.VMEM((levels, LANES), F32),
        pltpu.VMEM((slots, LANES), jnp.int32),
        pltpu.VMEM((slots, LANES), F32),
        pltpu.VMEM((slots, LANES), F32),
        pltpu.VMEM((STEPS, 1, columns), F32),
        pltpu.VMEM((STEPS, 3, sections - 1, 1, columns), F32),
        pltpu.VMEM((2, PACK, LANES), F32),
        pltpu.VMEM((2, PACK, LANES), F32),
        pltpu.VMEM((STEPS, tiles, 8, levels), F32),
        pltpu.VMEM((STEPS, tiles, 8, levels), F32),
        pltpu.VMEM((STEPS, sections, own, levels), F32),
        pltpu.VMEM((STEPS, sections, own, levels), F32),
        dma((14,)),
        dma((2,)),
        dma((2,)),
        dma((2,)),
        dma((STEPS, 3, sections - 1)),
        dma((STEPS, 3, sections - 1)),
        dma((STEPS, tiles)),
        dma((STEPS, tiles)),
        dma((STEPS, sections)),
        dma((STEPS, sections)),
    ]
    return pl.pallas_call(
        functools.partial(kernel, sections, tiles),
        out_shape=(
            jax.ShapeDtypeStruct(state.shape, F32),
            jax.ShapeDtypeStruct((STEPS, own, heights), F32),
        ),
        in_specs=specs,
        out_specs=(any_spec, any_spec),
        scratch_shapes=scratch,
        compiler_params=pltpu.CompilerParams(
            collective_id=0, has_side_effects=True, vmem_limit_bytes=32 * 1024 * 1024
        ),
        cost_estimate=pl.CostEstimate(flops=700_000_000, bytes_accessed=1_500_000, transcendentals=0),
    )(*args)


def solution(mesh):
    return jax.shard_map(
        functools.partial(shards, mesh.shape["sec"], mesh.shape["tile"]),
        mesh=mesh,
        in_specs=(
            P("sec", None, "tile"),
            P("sec", None, "tile"),
            P("sec", None, "tile"),
            P("sec", None, None),
            P("sec", None),
            P("sec", None, "tile"),
            P("sec", None, "tile"),
            P(),
            P(None, "sec", "tile", None, None),
            P(None, "sec", None, "tile"),
            P(None, "sec", None, "tile"),
            P(None, "sec", "tile"),
            P("sec", None, None),
            P(),
            P(None, ("sec", "tile"), None),
        ),
        out_specs=(P("sec", None, "tile"), P(None, ("sec", "tile"), None)),
        check_vma=False,
    )
```

```python
import functools

import jax
import jax.numpy as jnp
from jax import lax
from jax.experimental import pallas as pl
from jax.experimental.pallas import tpu as pltpu
from jax.sharding import PartitionSpec as P

SUBS = 4
STEPS = 2
HALO = SUBS * STEPS
LANES = 128
PACK = 3 * HALO + 8
F32 = jnp.float32
BF16 = jnp.bfloat16
MESH = pl.DeviceIdType.MESH


def split(x):
    high = x.astype(BF16)
    low = (x - high.astype(F32)).astype(BF16)
    return high, low


def mm(a, b, dims):
    return lax.dot_general(a, b, (dims, ((), ())), preferred_element_type=F32)


NN = ((1,), (0,))
NT = ((1,), (1,))
TN = ((0,), (0,))


def dot3(a, b, dims=NN):
    ah, al = split(a)
    bh, bl = split(b)
    return mm(ah, bh, dims) + (mm(ah, bl, dims) + mm(al, bh, dims))


def kernel(
    sections,
    tiles,
    state,
    tendency,
    diffusion,
    mixing,
    coupling,
    remap_index,
    remap_weight,
    active_cols,
    send_cols,
    occ_slot,
    occ_weight,
    occ_count,
    refraction,
    abel_matrix,
    observed,
    out_state,
    out_departures,
    field,
    rates,
    forcing,
    drive,
    tend_v,
    diff_v,
    mix_v,
    coup_v,
    ridx_v,
    rw_v,
    cols_v,
    slot_v,
    ow_v,
    oc_v,
    refr_v,
    abel_v,
    obs_v,
    dep_v,
    mix_a,
    mix_b,
    gain,
    position,
    weight,
    picked,
    surf,
    tab,
    pack_out,
    pack_in,
    chosen_out,
    chosen_in,
    parts_out,
    parts_in,
    load_sem,
    store_sem,
    pack_send,
    pack_recv,
    surf_send,
    surf_recv,
    col_send,
    col_recv,
    red_send,
    red_recv,
):
    levels, columns = tend_v.shape
    ext = field.shape[1]
    blocks = columns // LANES
    rk = ridx_v.shape[0]
    s = lax.axis_index("sec")
    t = lax.axis_index("tile")
    ocean = sections - 1
    is_ocean = s == ocean
    right = lax.rem(t + 1, tiles)
    left = lax.rem(t + tiles - 1, tiles)
    near = ((t, 0), (left, 1), (right, 2))

    loads = [
        (state.at[0], field.at[:, 0:columns]),
        (diffusion.at[0], diff_v),
        (tendency.at[0], tend_v),
        (remap_index.at[0], ridx_v),
        (remap_weight.at[0], rw_v),
        (mixing.at[0], mix_v),
        (coupling, coup_v),
        (send_cols, cols_v),
        (occ_slot, slot_v),
        (occ_weight, ow_v),
        (occ_count, oc_v),
        (refraction.at[0], refr_v),
        (abel_matrix, abel_v),
        (observed, obs_v),
    ]
    loads = [pltpu.make_async_copy(a, b, load_sem.at[i]) for i, (a, b) in enumerate(loads)]
    for load in loads:
        load.start()

    def over_tiles(body):
        if tiles <= 8:
            for d in range(1, tiles):
                body(lax.rem(t + d, tiles))
        else:
            lax.fori_loop(1, tiles, lambda d, c: (body(lax.rem(t + d, tiles)), c)[1], 0)

    barrier = pltpu.get_barrier_semaphore()

    def greet(sec, tile):
        pl.semaphore_signal(barrier, inc=1, device_id=(sec, tile), device_id_type=MESH)

    over_tiles(lambda other: greet(s, other))
    for d in range(1, sections):
        greet(lax.rem(s + d, sections), t)

    @pl.when(is_ocean)
    def _():
        for a in range(ocean):
            greet(a, left)
            greet(a, right)

    @pl.when(jnp.logical_not(is_ocean))
    def _():
        greet(ocean, left)
        greet(ocean, right)

    lane = lax.broadcasted_iota(jnp.int32, (levels, LANES), 1)
    row_lane = lax.broadcasted_iota(jnp.int32, (1, LANES), 1)

    for load in loads[:5]:
        load.wait()
    surf[0] = field[levels - 1 : levels, 0:columns]

    tail = columns - LANES
    idx_f = ridx_v[...].astype(F32)

    def pack(slot, lo, shift):
        a = field[:, lo : lo + LANES]
        b = diff_v[:, lo : lo + LANES].astype(F32)
        c = tend_v[:, lo : lo + LANES].astype(F32)
        if shift:
            a = pltpu.roll(a, shift, 1)
        b = pltpu.roll(b, shift + HALO, 1)
        c = pltpu.roll(c, shift + 2 * HALO, 1)
        mixed = jnp.where(lane < HALO, a, jnp.where(lane < 2 * HALO, b, c))
        pack_out[slot, 0 : 3 * HALO, :] = mixed.T[0 : 3 * HALO]
        pack_out[slot, 3 * HALO : 3 * HALO + rk, :] = idx_f[:, lo : lo + LANES]
        pack_out[slot, 3 * HALO + rk : PACK, :] = rw_v[:, lo : lo + LANES]

    pack(0, 0, 0)
    pack(1, tail, HALO)

    meet = (tiles - 1) + (sections - 1) + jnp.where(is_ocean, 2 * ocean, 2)
    pl.semaphore_wait(barrier, meet)

    def pack_copy(slot, tile):
        return pltpu.make_async_remote_copy(
            src_ref=pack_out.at[slot],
            dst_ref=pack_in.at[slot],
            send_sem=pack_send.at[slot],
            recv_sem=pack_recv.at[slot],
            device_id=(s, tile),
            device_id_type=MESH,
        )

    def surf_copy(p, d, a, sec, tile, mark):
        return pltpu.make_async_remote_copy(
            src_ref=surf.at[p],
            dst_ref=tab.at[p, d, a],
            send_sem=surf_send.at[p, d, mark],
            recv_sem=surf_recv.at[p, d, a],
            device_id=(sec, tile),
            device_id_type=MESH,
        )

    def surf_each(p, act):
        @pl.when(is_ocean)
        def _():
            for tile, d in near:
                for a in range(ocean):
                    act(surf_copy(p, d, 0, a, tile, a))

        @pl.when(jnp.logical_not(is_ocean))
        def _():
            for tile, d in near:
                act(surf_copy(p, d, s, ocean, tile, 0))

    packs = (pack_copy(0, left), pack_copy(1, right))
    for copy in packs:
        copy.start()
    surf_each(0, lambda copy: copy.start())

    for load in loads[5:]:
        load.wait()
    mh, ml = split(mix_v[...])
    mix_a[:, 0:levels] = mh
    mix_a[:, levels : 2 * levels] = mh
    mix_b[...] = ml
    gain[...] = jnp.broadcast_to(coup_v[...], (LANES, levels)).T
    rates[:, 0:columns] = diff_v[...].astype(F32)
    forcing[:, 0:columns] = tend_v[...].astype(F32)
    for b in range(blocks):
        position[b * rk : (b + 1) * rk, :] = ridx_v[:, b * LANES : (b + 1) * LANES]
        weight[b * rk : (b + 1) * rk, :] = rw_v[:, b * LANES : (b + 1) * LANES]

    limit = active_cols[s]
    number = lax.broadcasted_iota(jnp.int32, (1, ext), 1)
    number = jnp.where(
        number < columns, number, jnp.where(number < columns + LANES // 2, number - columns, number - LANES)
    )
    live = number < limit

    cap = cols_v.shape[3]
    rows = tiles * 8

    def selector(p):
        which = lax.broadcasted_iota(jnp.int32, (rows, tiles), 0)
        owner = lax.broadcasted_iota(jnp.int32, (rows, tiles), 1)
        expand = jnp.where(lax.shift_right_logical(which, 3) == owner, 1.0, 0.0)
        listed = lax.dot_general(
            expand,
            cols_v[p, 0, 0].astype(F32),
            (NT, ((), ())),
            precision=lax.Precision.HIGHEST,
            preferred_element_type=F32,
        )
        r = lax.broadcasted_iota(jnp.int32, (rows, cap), 0)
        c = lax.broadcasted_iota(jnp.int32, (rows, cap), 1)
        column = jnp.sum(jnp.where((r & 7) == c, listed, 0.0), axis=1, keepdims=True)
        rr = lax.broadcasted_iota(jnp.int32, (rows, columns), 0)
        cc = lax.broadcasted_iota(jnp.int32, (rows, columns), 1)
        hit = jnp.logical_and(cc == column.astype(jnp.int32), (rr & 7) < cap)
        return jnp.where(hit, 1.0, 0.0).astype(BF16)

    def occultation_weights(p):
        shape = (rows, slot_v.shape[3])
        m = lax.broadcasted_iota(jnp.int32, shape, 0)
        key = jnp.where((m & 7) < cap, lax.shift_right_logical(m, 3) * cap + (m & 7), -1)
        counts = oc_v[p]
        total = jnp.zeros(shape, F32)
        for k in range(slot_v.shape[2]):
            w = jnp.where(counts > k, ow_v[p, 0, k : k + 1, :], 0.0)
            total = total + jnp.where(key == slot_v[p, 0, k : k + 1, :], w, 0.0)
        return total

    def mixed_spread():
        f = field[...]
        around = pltpu.roll(f, 1, 1) + pltpu.roll(f, ext - 1, 1)
        spread = f + rates[...] * (around - 2.0 * f)
        xh, xl = split(spread)
        return mm(mix_a[...], jnp.concatenate([xh, xl], axis=0), NN) + mm(mix_b[...], xh, NN)

    def boundary_of(p):
        pos = position[...]
        inner = pos & (LANES - 1)
        outer = lax.shift_right_logical(pos, 7)

        def look(a):
            for d in range(3):
                pltpu.make_async_remote_copy(
                    src_ref=surf.at[p],
                    dst_ref=tab.at[p, d, a],
                    send_sem=surf_send.at[p, d, 0],
                    recv_sem=surf_recv.at[p, d, a],
                    device_id=(s, right),
                    device_id_type=MESH,
                ).wait_recv()
            found = picked[...]
            for b in range(blocks):
                at = slice(b * LANES, (b + 1) * LANES)
                table = jnp.concatenate(
                    [
                        jnp.broadcast_to(tab[p, 0, a, :, at], (blocks * rk, LANES)),
                        jnp.broadcast_to(tab[p, 1, a, :, at], (rk, LANES)),
                        jnp.broadcast_to(tab[p, 2, a, :, at], (rk, LANES)),
                    ],
                    axis=0,
                )
                got = jnp.take_along_axis(table, inner, axis=1, mode="promise_in_bounds")
                found = jnp.where(outer == a * blocks + b, got, found)
            picked[...] = found

        picked[...] = jnp.zeros(picked.shape, F32)
        look(0)

        @pl.when(is_ocean)
        def _():
            for a in range(1, ocean):
                look(a)

        terms = picked[...] * weight[...]
        sums = [jnp.sum(terms[b * rk : (b + 1) * rk], axis=0, keepdims=True) for b in range(blocks + 2)]
        sums[blocks] = jnp.where(row_lane < LANES // 2, sums[blocks], sums[blocks + 1])
        return [
            sums[b] - field[levels - 1 : levels, b * LANES : (b + 1) * LANES] for b in range(blocks + 1)
        ]

    def coupling_step(p):
        product = mixed_spread()
        boundary = boundary_of(p)
        push = jnp.concatenate([gain[...] * row for row in boundary], axis=1)
        push = push + forcing[...]
        field[...] = jnp.where(live, product + push, field[...])
        drive[...] = push

        def substep(_, carry):
            field[...] = jnp.where(live, mixed_spread() + drive[...], field[...])
            return carry

        lax.fori_loop(0, SUBS - 1, substep, 0)

    def column_copy(p, other, source):
        return pltpu.make_async_remote_copy(
            src_ref=chosen_out.at[p, other],
            dst_ref=chosen_in.at[p, source],
            send_sem=col_send.at[p, other],
            recv_sem=col_recv.at[p, source],
            device_id=(s, other),
            device_id_type=MESH,
        )

    def send_columns(p, pick):
        fh, fl = split(field[:, 0:columns])
        taken = mm(pick, fh, NT) + mm(pick, fl, NT)
        projected = dot3(taken, refr_v[...]).reshape(tiles, 8, levels)
        chosen_out[p] = projected
        over_tiles(lambda other: column_copy(p, other, t).start())
        chosen_in[p, t] = chosen_out[p, t]

    own = parts_out.shape[2]

    def part_copy(p, other, source):
        return pltpu.make_async_remote_copy(
            src_ref=parts_out.at[p, other],
            dst_ref=parts_in.at[p, source],
            send_sem=red_send.at[p, other],
            recv_sem=red_recv.at[p, source],
            device_id=(other, t),
            device_id_type=MESH,
        )

    def others():
        return [lax.rem(s + d, sections) for d in range(1, sections)]

    def send_parts(p, w):
        over_tiles(lambda other: column_copy(p, other, other).wait_recv())
        part = dot3(w, chosen_in[p].reshape(rows, levels), TN)
        parts_out[p] = part.reshape(sections, own, levels)
        for other in others():
            part_copy(p, other, s).start()
        parts_in[p, s] = parts_out[p, s]

    def depart(p):
        for other in others():
            part_copy(p, other, other).wait_recv()
        total = parts_in[p, 0]
        for a in range(1, sections):
            total = total + parts_in[p, a]
        dep_v[p] = obs_v[p] - dot3(total, abel_v[...])

    for copy in packs:
        copy.wait_recv()
    gap = jnp.zeros((LANES - 2 * HALO, levels), F32)

    def pad(i):
        at = slice(i * HALO, (i + 1) * HALO)
        return jnp.concatenate([pack_in[0, at, :], gap, pack_in[1, at, :]], axis=0).T

    field[:, columns:ext] = pad(0)
    rates[:, columns:ext] = pad(1)
    forcing[:, columns:ext] = pad(2)
    for i in range(2):
        at = slice((blocks + i) * rk, (blocks + i + 1) * rk)
        position[at, :] = pack_in[i, 3 * HALO : 3 * HALO + rk, :].astype(jnp.int32)
        weight[at, :] = pack_in[i, 3 * HALO + rk : PACK, :]

    coupling_step(0)
    surf[1] = field[levels - 1 : levels, 0:columns]
    surf_each(1, lambda copy: copy.start())
    send_columns(0, selector(0))
    coupling_step(1)
    stores = [pltpu.make_async_copy(field.at[:, 0:columns], out_state.at[0], store_sem.at[0])]
    stores[0].start()
    send_columns(1, selector(1))
    send_parts(0, occultation_weights(0))
    send_parts(1, occultation_weights(1))
    depart(0)
    depart(1)
    stores.append(pltpu.make_async_copy(dep_v, out_departures, store_sem.at[1]))
    stores[1].start()

    for copy in packs:
        copy.wait_send()
    for p in range(STEPS):
        surf_each(p, lambda copy: copy.wait_send())
        over_tiles(lambda other: column_copy(p, other, t).wait_send())
        for other in others():
            part_copy(p, other, s).wait_send()
    for store in stores:
        store.wait()


def shards(sections, tiles, *args):
    (state, tendency, diffusion, mixing, coupling, remap_index, remap_weight, active_cols, send_cols) = args[:9]
    (occ_slot, occ_weight, occ_count, refraction, abel_matrix, observed) = args[9:]
    send_cols = jnp.swapaxes(send_cols, 3, 4)
    args = args[:8] + (send_cols,) + args[9:]
    levels, columns = state.shape[1:]
    rk = remap_index.shape[1]
    ext = columns + LANES
    slots = (columns // LANES + 2) * rk
    own = observed.shape[1]
    heights = abel_matrix.shape[1]
    dma = pltpu.SemaphoreType.DMA
    any_spec = pl.BlockSpec(memory_space=pltpu.HBM)
    smem = pl.BlockSpec(memory_space=pltpu.SMEM)
    specs = [any_spec] * len(args)
    specs[7] = smem
    scratch = [
        pltpu.VMEM((levels, ext), F32),
        pltpu.VMEM((levels, ext), F32),
        pltpu.VMEM((levels, ext), F32),
        pltpu.VMEM((levels, ext), F32),
        pltpu.VMEM((levels, columns), BF16),
        pltpu.VMEM((levels, columns), BF16),
        pltpu.VMEM((levels, levels), F32),
        pltpu.VMEM(coupling.shape, F32),
        pltpu.VMEM((rk, columns), jnp.int32),
        pltpu.VMEM((rk, columns), F32),
        pltpu.VMEM(send_cols.shape, jnp.int32),
        pltpu.VMEM(occ_slot.shape, jnp.int32),
        pltpu.VMEM(occ_weight.shape, F32),
        pltpu.VMEM(occ_count.shape, jnp.int32),
        pltpu.VMEM((levels, levels), F32),
        pltpu.VMEM(abel_matrix.shape, F32),
        pltpu.VMEM(observed.shape, F32),
        pltpu.VMEM(observed.shape, F32),
        pltpu.VMEM((levels, 2 * levels), BF16),
        pltpu.VMEM((levels, levels), BF16),
        pltpu.VMEM((levels, LANES), F32),
        pltpu.VMEM((slots, LANES), jnp.int32),
        pltpu.VMEM((slots, LANES), F32),
        pltpu.VMEM((slots, LANES), F32),
        pltpu.VMEM((STEPS, 1, columns), F32),
        pltpu.VMEM((STEPS, 3, sections - 1, 1, columns), F32),
        pltpu.VMEM((2, PACK, LANES), F32),
        pltpu.VMEM((2, PACK, LANES), F32),
        pltpu.VMEM((STEPS, tiles, 8, levels), F32),
        pltpu.VMEM((STEPS, tiles, 8, levels), F32),
        pltpu.VMEM((STEPS, sections, own, levels), F32),
        pltpu.VMEM((STEPS, sections, own, levels), F32),
        dma((14,)),
        dma((2,)),
        dma((2,)),
        dma((2,)),
        dma((STEPS, 3, sections - 1)),
        dma((STEPS, 3, sections - 1)),
        dma((STEPS, tiles)),
        dma((STEPS, tiles)),
        dma((STEPS, sections)),
        dma((STEPS, sections)),
    ]
    return pl.pallas_call(
        functools.partial(kernel, sections, tiles),
        out_shape=(
            jax.ShapeDtypeStruct(state.shape, F32),
            jax.ShapeDtypeStruct((STEPS, own, heights), F32),
        ),
        in_specs=specs,
        out_specs=(any_spec, any_spec),
        scratch_shapes=scratch,
        compiler_params=pltpu.CompilerParams(
            collective_id=0, has_side_effects=True, vmem_limit_bytes=64 * 1024 * 1024 - 64 * 1024
        ),
        cost_estimate=pl.CostEstimate(flops=700_000_000, bytes_accessed=1_500_000, transcendentals=0),
    )(*args)


def solution(mesh):
    return jax.shard_map(
        functools.partial(shards, mesh.shape["sec"], mesh.shape["tile"]),
        mesh=mesh,
        in_specs=(
            P("sec", None, "tile"),
            P("sec", None, "tile"),
            P("sec", None, "tile"),
            P("sec", None, None),
            P("sec", None),
            P("sec", None, "tile"),
            P("sec", None, "tile"),
            P(),
            P(None, "sec", "tile", None, None),
            P(None, "sec", None, "tile"),
            P(None, "sec", None, "tile"),
            P(None, "sec", "tile"),
            P("sec", None, None),
            P(),
            P(None, ("sec", "tile"), None),
        ),
        out_specs=(P("sec", None, "tile"), P(None, ("sec", "tile"), None)),
        check_vma=False,
    )
```

```python
import functools

import jax
import jax.numpy as jnp
from jax import lax
from jax.experimental import pallas as pl
from jax.experimental.pallas import tpu as pltpu
from jax.sharding import PartitionSpec as P

SUBS = 4
STEPS = 2
HALO = SUBS * STEPS
LANES = 128
PACK = 3 * HALO + 8
F32 = jnp.float32
BF16 = jnp.bfloat16
MESH = pl.DeviceIdType.MESH


def split(x):
    high = x.astype(BF16)
    low = (x - high.astype(F32)).astype(BF16)
    return high, low


def mm(a, b, dims):
    return lax.dot_general(a, b, (dims, ((), ())), preferred_element_type=F32)


NN = ((1,), (0,))
NT = ((1,), (1,))
TN = ((0,), (0,))


def dot3(a, b, dims=NN):
    ah, al = split(a)
    bh, bl = split(b)
    return mm(ah, bh, dims) + (mm(ah, bl, dims) + mm(al, bh, dims))


def kernel(
    sections,
    tiles,
    state,
    tendency,
    diffusion,
    mixing,
    coupling,
    remap_index,
    remap_weight,
    active_cols,
    send_cols,
    occ_slot,
    occ_weight,
    occ_count,
    refraction,
    abel_matrix,
    observed,
    out_state,
    out_departures,
    field,
    rates,
    forcing,
    drive,
    tend_v,
    diff_v,
    mix_v,
    coup_v,
    ridx_v,
    rw_v,
    cols_v,
    slot_v,
    ow_v,
    oc_v,
    refr_v,
    abel_v,
    obs_v,
    dep_v,
    mix_a,
    mix_b,
    pick_v,
    gain,
    position,
    weight,
    picked,
    surf,
    tab,
    pack_out,
    pack_in,
    chosen_out,
    chosen_in,
    parts_out,
    parts_in,
    load_sem,
    store_sem,
    pack_send,
    pack_recv,
    surf_send,
    surf_recv,
    col_send,
    col_recv,
    red_send,
    red_recv,
):
    levels, columns = tend_v.shape
    ext = field.shape[1]
    blocks = columns // LANES
    rk = ridx_v.shape[0]
    s = lax.axis_index("sec")
    t = lax.axis_index("tile")
    ocean = sections - 1
    is_ocean = s == ocean
    right = lax.rem(t + 1, tiles)
    left = lax.rem(t + tiles - 1, tiles)
    near = ((t, 0), (left, 1), (right, 2))

    loads = [
        (state.at[0], field.at[:, 0:columns]),
        (diffusion.at[0], diff_v),
        (tendency.at[0], tend_v),
        (remap_index.at[0], ridx_v),
        (remap_weight.at[0], rw_v),
        (mixing.at[0], mix_v),
        (coupling, coup_v),
        (send_cols, cols_v),
        (occ_slot, slot_v),
        (occ_weight, ow_v),
        (occ_count, oc_v),
        (refraction.at[0], refr_v),
        (abel_matrix, abel_v),
        (observed, obs_v),
    ]
    loads = [pltpu.make_async_copy(a, b, load_sem.at[i]) for i, (a, b) in enumerate(loads)]
    def over_tiles(body):
        if tiles <= 8:
            for d in range(1, tiles):
                body(lax.rem(t + d, tiles))
        else:
            lax.fori_loop(1, tiles, lambda d, c: (body(lax.rem(t + d, tiles)), c)[1], 0)

    barrier = pltpu.get_barrier_semaphore()

    def greet(sec, tile):
        pl.semaphore_signal(barrier, inc=1, device_id=(sec, tile), device_id_type=MESH)

    over_tiles(lambda other: greet(s, other))
    for d in range(1, sections):
        greet(lax.rem(s + d, sections), t)

    @pl.when(is_ocean)
    def _():
        for a in range(ocean):
            greet(a, left)
            greet(a, right)

    @pl.when(jnp.logical_not(is_ocean))
    def _():
        greet(ocean, left)
        greet(ocean, right)

    for load in loads:
        load.start()

    lane = lax.broadcasted_iota(jnp.int32, (levels, LANES), 1)
    row_lane = lax.broadcasted_iota(jnp.int32, (1, LANES), 1)

    for load in loads[:5]:
        load.wait()
    surf[0] = field[levels - 1 : levels, 0:columns]

    tail = columns - LANES
    idx_f = ridx_v[...].astype(F32)

    def pack(slot, lo, shift):
        a = field[:, lo : lo + LANES]
        b = diff_v[:, lo : lo + LANES].astype(F32)
        c = tend_v[:, lo : lo + LANES].astype(F32)
        if shift:
            a = pltpu.roll(a, shift, 1)
        b = pltpu.roll(b, shift + HALO, 1)
        c = pltpu.roll(c, shift + 2 * HALO, 1)
        mixed = jnp.where(lane < HALO, a, jnp.where(lane < 2 * HALO, b, c))
        pack_out[slot, 0 : 3 * HALO, :] = mixed.T[0 : 3 * HALO]
        pack_out[slot, 3 * HALO : 3 * HALO + rk, :] = idx_f[:, lo : lo + LANES]
        pack_out[slot, 3 * HALO + rk : PACK, :] = rw_v[:, lo : lo + LANES]

    pack(0, 0, 0)
    pack(1, tail, HALO)

    meet = (tiles - 1) + (sections - 1) + jnp.where(is_ocean, 2 * ocean, 2)
    pl.semaphore_wait(barrier, meet)

    def pack_copy(slot, tile):
        return pltpu.make_async_remote_copy(
            src_ref=pack_out.at[slot],
            dst_ref=pack_in.at[slot],
            send_sem=pack_send.at[slot],
            recv_sem=pack_recv.at[slot],
            device_id=(s, tile),
            device_id_type=MESH,
        )

    def surf_copy(p, d, a, sec, tile, mark):
        return pltpu.make_async_remote_copy(
            src_ref=surf.at[p],
            dst_ref=tab.at[p, d, a],
            send_sem=surf_send.at[p, d, mark],
            recv_sem=surf_recv.at[p, d, a],
            device_id=(sec, tile),
            device_id_type=MESH,
        )

    def surf_each(p, act):
        @pl.when(is_ocean)
        def _():
            for tile, d in near:
                for a in range(ocean):
                    act(surf_copy(p, d, 0, a, tile, a))

        @pl.when(jnp.logical_not(is_ocean))
        def _():
            for tile, d in near:
                act(surf_copy(p, d, s, ocean, tile, 0))

    packs = (pack_copy(0, left), pack_copy(1, right))
    for copy in packs:
        copy.start()
    surf_each(0, lambda copy: copy.start())

    for load in loads[5:]:
        load.wait()
    mh, ml = split(mix_v[...])
    mix_a[:, 0:levels] = mh
    mix_a[:, levels : 2 * levels] = mh
    mix_b[...] = ml
    gain[...] = jnp.broadcast_to(coup_v[...], (LANES, levels)).T
    rates[:, 0:columns] = diff_v[...].astype(F32)
    forcing[:, 0:columns] = tend_v[...].astype(F32)
    for b in range(blocks):
        position[b * rk : (b + 1) * rk, :] = ridx_v[:, b * LANES : (b + 1) * LANES]
        weight[b * rk : (b + 1) * rk, :] = rw_v[:, b * LANES : (b + 1) * LANES]

    limit = active_cols[s]
    number = lax.broadcasted_iota(jnp.int32, (1, ext), 1)
    number = jnp.where(
        number < columns, number, jnp.where(number < columns + LANES // 2, number - columns, number - LANES)
    )
    live = number < limit

    cap = cols_v.shape[3]
    rows = tiles * 8

    def selector(p):
        which = lax.broadcasted_iota(jnp.int32, (rows, tiles), 0)
        owner = lax.broadcasted_iota(jnp.int32, (rows, tiles), 1)
        expand = jnp.where(lax.shift_right_logical(which, 3) == owner, 1.0, 0.0)
        listed = lax.dot_general(
            expand,
            cols_v[p, 0, 0].astype(F32),
            (NT, ((), ())),
            precision=lax.Precision.HIGHEST,
            preferred_element_type=F32,
        )
        r = lax.broadcasted_iota(jnp.int32, (rows, cap), 0)
        c = lax.broadcasted_iota(jnp.int32, (rows, cap), 1)
        column = jnp.sum(jnp.where((r & 7) == c, listed, 0.0), axis=1, keepdims=True)
        rr = lax.broadcasted_iota(jnp.int32, (rows, columns), 0)
        cc = lax.broadcasted_iota(jnp.int32, (rows, columns), 1)
        hit = jnp.logical_and(cc == column.astype(jnp.int32), (rr & 7) < cap)
        return jnp.where(hit, 1.0, 0.0).astype(BF16)

    def occultation_weights(p):
        shape = (rows, slot_v.shape[3])
        m = lax.broadcasted_iota(jnp.int32, shape, 0)
        key = jnp.where((m & 7) < cap, lax.shift_right_logical(m, 3) * cap + (m & 7), -1)
        counts = oc_v[p]
        total = jnp.zeros(shape, F32)
        for k in range(slot_v.shape[2]):
            w = jnp.where(counts > k, ow_v[p, 0, k : k + 1, :], 0.0)
            total = total + jnp.where(key == slot_v[p, 0, k : k + 1, :], w, 0.0)
        return total

    def spread_halves():
        f = field[...]
        around = pltpu.roll(f, 1, 1) + pltpu.roll(f, ext - 1, 1)
        spread = f + rates[...] * (around - 2.0 * f)
        xh, xl = split(spread)
        return jnp.concatenate([xh, xl], axis=0), xh

    def mixed_spread():
        xx, xh = spread_halves()
        return mm(mix_a[...], xx, NN) + mm(mix_b[...], xh, NN)

    def boundary_of(p):
        pos = position[...]
        inner = pos & (LANES - 1)
        outer = lax.shift_right_logical(pos, 7)

        def look(a):
            for d in range(3):
                pltpu.make_async_remote_copy(
                    src_ref=surf.at[p],
                    dst_ref=tab.at[p, d, a],
                    send_sem=surf_send.at[p, d, 0],
                    recv_sem=surf_recv.at[p, d, a],
                    device_id=(s, right),
                    device_id_type=MESH,
                ).wait_recv()
            found = picked[...]
            for b in range(blocks):
                at = slice(b * LANES, (b + 1) * LANES)
                table = jnp.concatenate(
                    [
                        jnp.broadcast_to(tab[p, 0, a, :, at], (blocks * rk, LANES)),
                        jnp.broadcast_to(tab[p, 1, a, :, at], (rk, LANES)),
                        jnp.broadcast_to(tab[p, 2, a, :, at], (rk, LANES)),
                    ],
                    axis=0,
                )
                got = jnp.take_along_axis(table, inner, axis=1, mode="promise_in_bounds")
                found = jnp.where(outer == a * blocks + b, got, found)
            picked[...] = found

        picked[...] = jnp.zeros(picked.shape, F32)
        look(0)

        @pl.when(is_ocean)
        def _():
            for a in range(1, ocean):
                look(a)

        terms = picked[...] * weight[...]
        sums = [jnp.sum(terms[b * rk : (b + 1) * rk], axis=0, keepdims=True) for b in range(blocks + 2)]
        sums[blocks] = jnp.where(row_lane < LANES // 2, sums[blocks], sums[blocks + 1])
        return [
            sums[b] - field[levels - 1 : levels, b * LANES : (b + 1) * LANES] for b in range(blocks + 1)
        ]

    def coupling_step(p):
        product = mixed_spread()
        boundary = boundary_of(p)
        push = jnp.concatenate([gain[...] * row for row in boundary], axis=1)
        push = push + forcing[...]
        field[...] = jnp.where(live, product + push, field[...])
        drive[...] = push

        def substep(_, carry):
            field[...] = jnp.where(live, mixed_spread() + drive[...], field[...])
            return carry

        if p == STEPS - 1:
            lax.fori_loop(0, SUBS - 1, substep, 0)
            return
        lax.fori_loop(0, SUBS - 2, substep, 0)
        xx, xh = spread_halves()
        low = slice(levels - 8, levels)
        row = mm(mix_a[low, :], xx, NN) + mm(mix_b[low, :], xh, NN) + drive[low, :]
        row = jnp.where(live, row, field[low, :])
        surf[p + 1] = row[7:8, 0:columns]
        surf_each(p + 1, lambda copy: copy.start())
        product = mm(mix_a[...], xx, NN) + mm(mix_b[...], xh, NN)
        field[...] = jnp.where(live, product + drive[...], field[...])

    def column_copy(p, other, source):
        return pltpu.make_async_remote_copy(
            src_ref=chosen_out.at[p, other],
            dst_ref=chosen_in.at[p, source],
            send_sem=col_send.at[p, other],
            recv_sem=col_recv.at[p, source],
            device_id=(s, other),
            device_id_type=MESH,
        )

    def send_columns(p):
        pick = pick_v[p]
        fh, fl = split(field[:, 0:columns])
        taken = mm(pick, fh, NT) + mm(pick, fl, NT)
        projected = dot3(taken, refr_v[...]).reshape(tiles, 8, levels)
        chosen_out[p] = projected
        over_tiles(lambda other: column_copy(p, other, t).start())
        chosen_in[p, t] = chosen_out[p, t]

    own = parts_out.shape[2]

    def part_copy(p, other, source):
        return pltpu.make_async_remote_copy(
            src_ref=parts_out.at[p, other],
            dst_ref=parts_in.at[p, source],
            send_sem=red_send.at[p, other],
            recv_sem=red_recv.at[p, source],
            device_id=(other, t),
            device_id_type=MESH,
        )

    def others():
        return [lax.rem(s + d, sections) for d in range(1, sections)]

    def send_parts(p, w):
        over_tiles(lambda other: column_copy(p, other, other).wait_recv())
        part = dot3(w, chosen_in[p].reshape(rows, levels), TN)
        parts_out[p] = part.reshape(sections, own, levels)
        for other in others():
            part_copy(p, other, s).start()
        parts_in[p, s] = parts_out[p, s]

    def depart(p):
        for other in others():
            part_copy(p, other, other).wait_recv()
        total = parts_in[p, 0]
        for a in range(1, sections):
            total = total + parts_in[p, a]
        dep_v[p] = obs_v[p] - dot3(total, abel_v[...])

    for p in range(STEPS):
        pick_v[p] = selector(p)

    for copy in packs:
        copy.wait_recv()
    gap = jnp.zeros((LANES - 2 * HALO, levels), F32)

    def pad(i):
        at = slice(i * HALO, (i + 1) * HALO)
        return jnp.concatenate([pack_in[0, at, :], gap, pack_in[1, at, :]], axis=0).T

    field[:, columns:ext] = pad(0)
    rates[:, columns:ext] = pad(1)
    forcing[:, columns:ext] = pad(2)
    for i in range(2):
        at = slice((blocks + i) * rk, (blocks + i + 1) * rk)
        position[at, :] = pack_in[i, 3 * HALO : 3 * HALO + rk, :].astype(jnp.int32)
        weight[at, :] = pack_in[i, 3 * HALO + rk : PACK, :]

    coupling_step(0)
    send_columns(0)
    coupling_step(1)
    store = pltpu.make_async_copy(field.at[:, 0:columns], out_state.at[0], store_sem.at[0])
    store.start()
    send_columns(1)
    occ = [occultation_weights(p) for p in range(STEPS)]
    send_parts(0, occ[0])
    for copy in packs:
        copy.wait_send()
    for p in range(STEPS):
        surf_each(p, lambda copy: copy.wait_send())
    over_tiles(lambda other: column_copy(0, other, t).wait_send())
    depart(0)
    send_parts(1, occ[1])
    over_tiles(lambda other: column_copy(1, other, t).wait_send())
    for p in range(STEPS):
        for other in others():
            part_copy(p, other, s).wait_send()
    store.wait()
    depart(1)
    last = pltpu.make_async_copy(dep_v, out_departures, store_sem.at[1])
    last.start()
    last.wait()


def hand_over(state, departures, out_state, out_departures, sem):
    rows = state.shape[1] // 4
    copies = [pltpu.make_async_copy(departures, out_departures, sem.at[4])]
    for i in range(4):
        at = pl.ds(i * rows, rows)
        copies.append(pltpu.make_async_copy(state.at[:, at], out_state.at[:, at], sem.at[i]))
    for copy in copies:
        copy.start()
    for copy in copies:
        copy.wait()


def shards(sections, tiles, *args):
    (state, tendency, diffusion, mixing, coupling, remap_index, remap_weight, active_cols, send_cols) = args[:9]
    (occ_slot, occ_weight, occ_count, refraction, abel_matrix, observed) = args[9:]
    send_cols = jnp.swapaxes(send_cols, 3, 4)
    args = args[:8] + (send_cols,) + args[9:]
    levels, columns = state.shape[1:]
    rk = remap_index.shape[1]
    ext = columns + LANES
    slots = (columns // LANES + 2) * rk
    own = observed.shape[1]
    heights = abel_matrix.shape[1]
    dma = pltpu.SemaphoreType.DMA
    any_spec = pl.BlockSpec(memory_space=pltpu.HBM)
    smem = pl.BlockSpec(memory_space=pltpu.SMEM)
    specs = [any_spec] * len(args)
    specs[7] = smem
    scratch = [
        pltpu.VMEM((levels, ext), F32),
        pltpu.VMEM((levels, ext), F32),
        pltpu.VMEM((levels, ext), F32),
        pltpu.VMEM((levels, ext), F32),
        pltpu.VMEM((levels, columns), BF16),
        pltpu.VMEM((levels, columns), BF16),
        pltpu.VMEM((levels, levels), F32),
        pltpu.VMEM(coupling.shape, F32),
        pltpu.VMEM((rk, columns), jnp.int32),
        pltpu.VMEM((rk, columns), F32),
        pltpu.VMEM(send_cols.shape, jnp.int32),
        pltpu.VMEM(occ_slot.shape, jnp.int32),
        pltpu.VMEM(occ_weight.shape, F32),
        pltpu.VMEM(occ_count.shape, jnp.int32),
        pltpu.VMEM((levels, levels), F32),
        pltpu.VMEM(abel_matrix.shape, F32),
        pltpu.VMEM(observed.shape, F32),
        pltpu.VMEM(observed.shape, F32),
        pltpu.VMEM((levels, 2 * levels), BF16),
        pltpu.VMEM((levels, levels), BF16),
        pltpu.VMEM((STEPS, tiles * 8, columns), BF16),
        pltpu.VMEM((levels, LANES), F32),
        pltpu.VMEM((slots, LANES), jnp.int32),
        pltpu.VMEM((slots, LANES), F32),
        pltpu.VMEM((slots, LANES), F32),
        pltpu.VMEM((STEPS, 1, columns), F32),
        pltpu.VMEM((STEPS, 3, sections - 1, 1, columns), F32),
        pltpu.VMEM((2, PACK, LANES), F32),
        pltpu.VMEM((2, PACK, LANES), F32),
        pltpu.VMEM((STEPS, tiles, 8, levels), F32),
        pltpu.VMEM((STEPS, tiles, 8, levels), F32),
        pltpu.VMEM((STEPS, sections, own, levels), F32),
        pltpu.VMEM((STEPS, sections, own, levels), F32),
        dma((14,)),
        dma((2,)),
        dma((2,)),
        dma((2,)),
        dma((STEPS, 3, sections - 1)),
        dma((STEPS, 3, sections - 1)),
        dma((STEPS, tiles)),
        dma((STEPS, tiles)),
        dma((STEPS, sections)),
        dma((STEPS, sections)),
    ]
    made = pl.pallas_call(
        functools.partial(kernel, sections, tiles),
        out_shape=(
            jax.ShapeDtypeStruct(state.shape, F32),
            jax.ShapeDtypeStruct((STEPS, own, heights), F32),
        ),
        in_specs=specs,
        out_specs=(any_spec, any_spec),
        scratch_shapes=scratch,
        compiler_params=pltpu.CompilerParams(
            collective_id=0, has_side_effects=True, vmem_limit_bytes=64 * 1024 * 1024 - 64 * 1024
        ),
        cost_estimate=pl.CostEstimate(flops=700_000_000, bytes_accessed=1_500_000, transcendentals=0),
    )(*args)
    return pl.pallas_call(
        hand_over,
        out_shape=tuple(jax.ShapeDtypeStruct(x.shape, x.dtype) for x in made),
        in_specs=[any_spec] * 2,
        out_specs=(any_spec, any_spec),
        scratch_shapes=[dma((5,))],
        cost_estimate=pl.CostEstimate(flops=0, bytes_accessed=600_000, transcendentals=0),
        compiler_params=pltpu.CompilerParams(vmem_limit_bytes=64 * 1024 * 1024 - 64 * 1024),
    )(*made)


def solution(mesh):
    return jax.shard_map(
        functools.partial(shards, mesh.shape["sec"], mesh.shape["tile"]),
        mesh=mesh,
        in_specs=(
            P("sec", None, "tile"),
            P("sec", None, "tile"),
            P("sec", None, "tile"),
            P("sec", None, None),
            P("sec", None),
            P("sec", None, "tile"),
            P("sec", None, "tile"),
            P(),
            P(None, "sec", "tile", None, None),
            P(None, "sec", None, "tile"),
            P(None, "sec", None, "tile"),
            P(None, "sec", "tile"),
            P("sec", None, None),
            P(),
            P(None, ("sec", "tile"), None),
        ),
        out_specs=(P("sec", None, "tile"), P(None, ("sec", "tile"), None)),
        check_vma=False,
    )
```

```python
import functools

import jax
import jax.numpy as jnp
from jax import lax
from jax.experimental import pallas as pl
from jax.experimental.pallas import tpu as pltpu
from jax.sharding import PartitionSpec as P

SUBS = 4
STEPS = 2
HALO = SUBS * STEPS
LANES = 128
PACK = 3 * HALO + 8
F32 = jnp.float32
BF16 = jnp.bfloat16
MESH = pl.DeviceIdType.MESH


def split(x):
    high = x.astype(BF16)
    low = (x - high.astype(F32)).astype(BF16)
    return high, low


def mm(a, b, dims):
    return lax.dot_general(a, b, (dims, ((), ())), preferred_element_type=F32)


NN = ((1,), (0,))
NT = ((1,), (1,))
TN = ((0,), (0,))


def dot3(a, b, dims=NN):
    ah, al = split(a)
    bh, bl = split(b)
    return mm(ah, bh, dims) + (mm(ah, bl, dims) + mm(al, bh, dims))


def kernel(
    sections,
    tiles,
    state,
    tendency,
    diffusion,
    mixing,
    coupling,
    remap_index,
    remap_weight,
    active_cols,
    send_cols,
    occ_slot,
    occ_weight,
    occ_count,
    refraction,
    abel_matrix,
    observed,
    out_state,
    out_departures,
    field,
    rates,
    forcing,
    drive,
    tend_v,
    diff_v,
    mix_v,
    coup_v,
    ridx_v,
    rw_v,
    cols_v,
    slot_v,
    ow_v,
    oc_v,
    refr_v,
    abel_v,
    obs_v,
    dep_v,
    mix_a,
    mix_b,
    pick_v,
    occ_v,
    gain,
    position,
    weight,
    picked,
    surf,
    tab,
    pack_out,
    pack_in,
    chosen_out,
    chosen_in,
    parts_out,
    parts_in,
    load_sem,
    store_sem,
    pack_send,
    pack_recv,
    surf_send,
    surf_recv,
    col_send,
    col_recv,
    red_send,
    red_recv,
):
    levels, columns = tend_v.shape
    ext = field.shape[1]
    blocks = columns // LANES
    rk = ridx_v.shape[0]
    s = lax.axis_index("sec")
    t = lax.axis_index("tile")
    ocean = sections - 1
    is_ocean = s == ocean
    right = lax.rem(t + 1, tiles)
    left = lax.rem(t + tiles - 1, tiles)
    near = ((t, 0), (left, 1), (right, 2))

    loads = [
        (state.at[0], field.at[:, 0:columns]),
        (diffusion.at[0], diff_v),
        (tendency.at[0], tend_v),
        (remap_index.at[0], ridx_v),
        (remap_weight.at[0], rw_v),
        (mixing.at[0], mix_v),
        (coupling, coup_v),
        (send_cols, cols_v),
        (occ_slot, slot_v),
        (occ_weight, ow_v),
        (occ_count, oc_v),
        (refraction.at[0], refr_v),
        (abel_matrix, abel_v),
        (observed, obs_v),
    ]
    loads = [pltpu.make_async_copy(a, b, load_sem.at[i]) for i, (a, b) in enumerate(loads)]
    def over_tiles(body):
        if tiles <= 8:
            for d in range(1, tiles):
                body(lax.rem(t + d, tiles))
        else:
            lax.fori_loop(1, tiles, lambda d, c: (body(lax.rem(t + d, tiles)), c)[1], 0)

    barrier = pltpu.get_barrier_semaphore()

    def greet(sec, tile):
        pl.semaphore_signal(barrier, inc=1, device_id=(sec, tile), device_id_type=MESH)

    over_tiles(lambda other: greet(s, other))
    for d in range(1, sections):
        greet(lax.rem(s + d, sections), t)

    @pl.when(is_ocean)
    def _():
        for a in range(ocean):
            greet(a, left)
            greet(a, right)

    @pl.when(jnp.logical_not(is_ocean))
    def _():
        greet(ocean, left)
        greet(ocean, right)

    for load in loads:
        load.start()

    lane = lax.broadcasted_iota(jnp.int32, (levels, LANES), 1)
    row_lane = lax.broadcasted_iota(jnp.int32, (1, LANES), 1)

    for load in loads[:5]:
        load.wait()
    surf[0] = field[levels - 1 : levels, 0:columns]

    tail = columns - LANES
    idx_f = ridx_v[...].astype(F32)

    def pack(slot, lo, shift):
        a = field[:, lo : lo + LANES]
        b = diff_v[:, lo : lo + LANES].astype(F32)
        c = tend_v[:, lo : lo + LANES].astype(F32)
        if shift:
            a = pltpu.roll(a, shift, 1)
        b = pltpu.roll(b, shift + HALO, 1)
        c = pltpu.roll(c, shift + 2 * HALO, 1)
        mixed = jnp.where(lane < HALO, a, jnp.where(lane < 2 * HALO, b, c))
        pack_out[slot, 0 : 3 * HALO, :] = mixed.T[0 : 3 * HALO]
        pack_out[slot, 3 * HALO : 3 * HALO + rk, :] = idx_f[:, lo : lo + LANES]
        pack_out[slot, 3 * HALO + rk : PACK, :] = rw_v[:, lo : lo + LANES]

    pack(0, 0, 0)
    pack(1, tail, HALO)

    meet = (tiles - 1) + (sections - 1) + jnp.where(is_ocean, 2 * ocean, 2)
    pl.semaphore_wait(barrier, meet)

    def pack_copy(slot, tile):
        return pltpu.make_async_remote_copy(
            src_ref=pack_out.at[slot],
            dst_ref=pack_in.at[slot],
            send_sem=pack_send.at[slot],
            recv_sem=pack_recv.at[slot],
            device_id=(s, tile),
            device_id_type=MESH,
        )

    def surf_copy(p, d, a, sec, tile, mark):
        return pltpu.make_async_remote_copy(
            src_ref=surf.at[p],
            dst_ref=tab.at[p, d, a],
            send_sem=surf_send.at[p, d, mark],
            recv_sem=surf_recv.at[p, d, a],
            device_id=(sec, tile),
            device_id_type=MESH,
        )

    def surf_each(p, act):
        @pl.when(is_ocean)
        def _():
            for tile, d in near:
                for a in range(ocean):
                    act(surf_copy(p, d, 0, a, tile, a))

        @pl.when(jnp.logical_not(is_ocean))
        def _():
            for tile, d in near:
                act(surf_copy(p, d, s, ocean, tile, 0))

    packs = (pack_copy(0, left), pack_copy(1, right))
    for copy in packs:
        copy.start()
    surf_each(0, lambda copy: copy.start())

    for load in loads[5:]:
        load.wait()
    mh, ml = split(mix_v[...])
    mix_a[:, 0:levels] = mh
    mix_a[:, levels : 2 * levels] = mh
    mix_b[...] = ml
    gain[...] = jnp.broadcast_to(coup_v[...], (LANES, levels)).T
    rates[:, 0:columns] = diff_v[...].astype(F32)
    forcing[:, 0:columns] = tend_v[...].astype(F32)
    for b in range(blocks):
        position[b * rk : (b + 1) * rk, :] = ridx_v[:, b * LANES : (b + 1) * LANES]
        weight[b * rk : (b + 1) * rk, :] = rw_v[:, b * LANES : (b + 1) * LANES]

    limit = active_cols[s]
    number = lax.broadcasted_iota(jnp.int32, (1, ext), 1)
    number = jnp.where(
        number < columns, number, jnp.where(number < columns + LANES // 2, number - columns, number - LANES)
    )
    live = number < limit

    cap = cols_v.shape[3]
    rows = tiles * 8

    def selector(p):
        which = lax.broadcasted_iota(jnp.int32, (rows, tiles), 0)
        owner = lax.broadcasted_iota(jnp.int32, (rows, tiles), 1)
        expand = jnp.where(lax.shift_right_logical(which, 3) == owner, 1.0, 0.0)
        listed = lax.dot_general(
            expand,
            cols_v[p, 0, 0].astype(F32),
            (NT, ((), ())),
            precision=lax.Precision.HIGHEST,
            preferred_element_type=F32,
        )
        r = lax.broadcasted_iota(jnp.int32, (rows, cap), 0)
        c = lax.broadcasted_iota(jnp.int32, (rows, cap), 1)
        column = jnp.sum(jnp.where((r & 7) == c, listed, 0.0), axis=1, keepdims=True)
        rr = lax.broadcasted_iota(jnp.int32, (rows, columns), 0)
        cc = lax.broadcasted_iota(jnp.int32, (rows, columns), 1)
        hit = jnp.logical_and(cc == column.astype(jnp.int32), (rr & 7) < cap)
        return jnp.where(hit, 1.0, 0.0).astype(BF16)

    def occultation_weights(p):
        shape = (rows, slot_v.shape[3])
        m = lax.broadcasted_iota(jnp.int32, shape, 0)
        key = jnp.where((m & 7) < cap, lax.shift_right_logical(m, 3) * cap + (m & 7), -1)
        counts = oc_v[p]
        total = jnp.zeros(shape, F32)
        for k in range(slot_v.shape[2]):
            w = jnp.where(counts > k, ow_v[p, 0, k : k + 1, :], 0.0)
            total = total + jnp.where(key == slot_v[p, 0, k : k + 1, :], w, 0.0)
        return total

    def spread_halves():
        f = field[...]
        around = pltpu.roll(f, 1, 1) + pltpu.roll(f, ext - 1, 1)
        spread = f + rates[...] * (around - 2.0 * f)
        xh, xl = split(spread)
        return jnp.concatenate([xh, xl], axis=0), xh

    def mixed_spread():
        xx, xh = spread_halves()
        return mm(mix_a[...], xx, NN) + mm(mix_b[...], xh, NN)

    def boundary_of(p):
        pos = position[...]
        inner = pos & (LANES - 1)
        outer = lax.shift_right_logical(pos, 7)

        def look(a):
            for d in range(3):
                pltpu.make_async_remote_copy(
                    src_ref=surf.at[p],
                    dst_ref=tab.at[p, d, a],
                    send_sem=surf_send.at[p, d, 0],
                    recv_sem=surf_recv.at[p, d, a],
                    device_id=(s, right),
                    device_id_type=MESH,
                ).wait_recv()
            found = picked[...]
            for b in range(blocks):
                at = slice(b * LANES, (b + 1) * LANES)
                table = jnp.concatenate(
                    [
                        jnp.broadcast_to(tab[p, 0, a, :, at], (blocks * rk, LANES)),
                        jnp.broadcast_to(tab[p, 1, a, :, at], (rk, LANES)),
                        jnp.broadcast_to(tab[p, 2, a, :, at], (rk, LANES)),
                    ],
                    axis=0,
                )
                got = jnp.take_along_axis(table, inner, axis=1, mode="promise_in_bounds")
                found = jnp.where(outer == a * blocks + b, got, found)
            picked[...] = found

        picked[...] = jnp.zeros(picked.shape, F32)
        look(0)

        @pl.when(is_ocean)
        def _():
            for a in range(1, ocean):
                look(a)

        terms = picked[...] * weight[...]
        sums = [jnp.sum(terms[b * rk : (b + 1) * rk], axis=0, keepdims=True) for b in range(blocks + 2)]
        sums[blocks] = jnp.where(row_lane < LANES // 2, sums[blocks], sums[blocks + 1])
        return [
            sums[b] - field[levels - 1 : levels, b * LANES : (b + 1) * LANES] for b in range(blocks + 1)
        ]

    def coupling_step(p):
        product = mixed_spread()
        boundary = boundary_of(p)
        push = jnp.concatenate([gain[...] * row for row in boundary], axis=1)
        push = push + forcing[...]
        field[...] = jnp.where(live, product + push, field[...])
        drive[...] = push

        def substep(_, carry):
            field[...] = jnp.where(live, mixed_spread() + drive[...], field[...])
            return carry

        lax.fori_loop(0, SUBS - 2, substep, 0)
        xx, xh = spread_halves()

        @pl.when(p < STEPS - 1)
        def _():
            low = slice(levels - 8, levels)
            row = mm(mix_a[low, :], xx, NN) + mm(mix_b[low, :], xh, NN) + drive[low, :]
            row = jnp.where(live, row, field[low, :])
            surf[p + 1] = row[7:8, 0:columns]
            surf_each(p + 1, lambda copy: copy.start())

        product = mm(mix_a[...], xx, NN) + mm(mix_b[...], xh, NN)
        field[...] = jnp.where(live, product + drive[...], field[...])

    def column_copy(p, other, source):
        return pltpu.make_async_remote_copy(
            src_ref=chosen_out.at[p, other],
            dst_ref=chosen_in.at[p, source],
            send_sem=col_send.at[p, other],
            recv_sem=col_recv.at[p, source],
            device_id=(s, other),
            device_id_type=MESH,
        )

    def send_columns(p):
        pick = pick_v[p]
        fh, fl = split(field[:, 0:columns])
        taken = mm(pick, fh, NT) + mm(pick, fl, NT)
        projected = dot3(taken, refr_v[...]).reshape(tiles, 8, levels)
        chosen_out[p] = projected
        over_tiles(lambda other: column_copy(p, other, t).start())
        chosen_in[p, t] = chosen_out[p, t]

    own = parts_out.shape[2]

    def part_copy(p, other, source):
        return pltpu.make_async_remote_copy(
            src_ref=parts_out.at[p, other],
            dst_ref=parts_in.at[p, source],
            send_sem=red_send.at[p, other],
            recv_sem=red_recv.at[p, source],
            device_id=(other, t),
            device_id_type=MESH,
        )

    def others():
        return [lax.rem(s + d, sections) for d in range(1, sections)]

    def send_parts(p, w):
        over_tiles(lambda other: column_copy(p, other, other).wait_recv())
        part = dot3(w, chosen_in[p].reshape(rows, levels), TN)
        parts_out[p] = part.reshape(sections, own, levels)
        for other in others():
            part_copy(p, other, s).start()
        parts_in[p, s] = parts_out[p, s]

    def depart(p):
        for other in others():
            part_copy(p, other, other).wait_recv()
        total = parts_in[p, 0]
        for a in range(1, sections):
            total = total + parts_in[p, a]
        dep_v[p] = obs_v[p] - dot3(total, abel_v[...])

    def list_columns(p, carry):
        pick_v[p] = selector(p)
        return carry

    lax.fori_loop(0, STEPS, list_columns, 0)

    for copy in packs:
        copy.wait_recv()
    gap = jnp.zeros((LANES - 2 * HALO, levels), F32)

    def pad(i):
        at = slice(i * HALO, (i + 1) * HALO)
        return jnp.concatenate([pack_in[0, at, :], gap, pack_in[1, at, :]], axis=0).T

    field[:, columns:ext] = pad(0)
    rates[:, columns:ext] = pad(1)
    forcing[:, columns:ext] = pad(2)
    for i in range(2):
        at = slice((blocks + i) * rk, (blocks + i + 1) * rk)
        position[at, :] = pack_in[i, 3 * HALO : 3 * HALO + rk, :].astype(jnp.int32)
        weight[at, :] = pack_in[i, 3 * HALO + rk : PACK, :]

    store = pltpu.make_async_copy(field.at[:, 0:columns], out_state.at[0], store_sem.at[0])

    def period(p, carry):
        coupling_step(p)

        @pl.when(p == STEPS - 1)
        def _():
            store.start()

        send_columns(p)
        return carry

    lax.fori_loop(0, STEPS, period, 0)

    def weigh(p, carry):
        occ_v[p] = occultation_weights(p)
        return carry

    lax.fori_loop(0, STEPS, weigh, 0)

    def gather_parts(p, carry):
        send_parts(p, occ_v[p])

        @pl.when(p == 0)
        def _():
            for copy in packs:
                copy.wait_send()
            for q in range(STEPS):
                surf_each(q, lambda copy: copy.wait_send())

        over_tiles(lambda other: column_copy(p, other, t).wait_send())
        return carry

    lax.fori_loop(0, STEPS, gather_parts, 0)

    def finish(p, carry):
        depart(p)
        for other in others():
            part_copy(p, other, s).wait_send()
        return carry

    lax.fori_loop(0, STEPS, finish, 0)
    last = pltpu.make_async_copy(dep_v, out_departures, store_sem.at[1])
    last.start()
    store.wait()
    last.wait()


def shards(sections, tiles, *args):
    (state, tendency, diffusion, mixing, coupling, remap_index, remap_weight, active_cols, send_cols) = args[:9]
    (occ_slot, occ_weight, occ_count, refraction, abel_matrix, observed) = args[9:]
    send_cols = jnp.swapaxes(send_cols, 3, 4)
    args = args[:8] + (send_cols,) + args[9:]
    levels, columns = state.shape[1:]
    rk = remap_index.shape[1]
    ext = columns + LANES
    slots = (columns // LANES + 2) * rk
    own = observed.shape[1]
    heights = abel_matrix.shape[1]
    dma = pltpu.SemaphoreType.DMA
    any_spec = pl.BlockSpec(memory_space=pltpu.HBM)
    smem = pl.BlockSpec(memory_space=pltpu.SMEM)
    specs = [any_spec] * len(args)
    specs[7] = smem
    scratch = [
        pltpu.VMEM((levels, ext), F32),
        pltpu.VMEM((levels, ext), F32),
        pltpu.VMEM((levels, ext), F32),
        pltpu.VMEM((levels, ext), F32),
        pltpu.VMEM((levels, columns), BF16),
        pltpu.VMEM((levels, columns), BF16),
        pltpu.VMEM((levels, levels), F32),
        pltpu.VMEM(coupling.shape, F32),
        pltpu.VMEM((rk, columns), jnp.int32),
        pltpu.VMEM((rk, columns), F32),
        pltpu.VMEM(send_cols.shape, jnp.int32),
        pltpu.VMEM(occ_slot.shape, jnp.int32),
        pltpu.VMEM(occ_weight.shape, F32),
        pltpu.VMEM(occ_count.shape, jnp.int32),
        pltpu.VMEM((levels, levels), F32),
        pltpu.VMEM(abel_matrix.shape, F32),
        pltpu.VMEM(observed.shape, F32),
        pltpu.VMEM(observed.shape, F32),
        pltpu.VMEM((levels, 2 * levels), BF16),
        pltpu.VMEM((levels, levels), BF16),
        pltpu.VMEM((STEPS, tiles * 8, columns), BF16),
        pltpu.VMEM((STEPS, tiles * 8, occ_slot.shape[3]), F32),
        pltpu.VMEM((levels, LANES), F32),
        pltpu.VMEM((slots, LANES), jnp.int32),
        pltpu.VMEM((slots, LANES), F32),
        pltpu.VMEM((slots, LANES), F32),
        pltpu.VMEM((STEPS, 1, columns), F32),
        pltpu.VMEM((STEPS, 3, sections - 1, 1, columns), F32),
        pltpu.VMEM((2, PACK, LANES), F32),
        pltpu.VMEM((2, PACK, LANES), F32),
        pltpu.VMEM((STEPS, tiles, 8, levels), F32),
        pltpu.VMEM((STEPS, tiles, 8, levels), F32),
        pltpu.VMEM((STEPS, sections, own, levels), F32),
        pltpu.VMEM((STEPS, sections, own, levels), F32),
        dma((14,)),
        dma((2,)),
        dma((2,)),
        dma((2,)),
        dma((STEPS, 3, sections - 1)),
        dma((STEPS, 3, sections - 1)),
        dma((STEPS, tiles)),
        dma((STEPS, tiles)),
        dma((STEPS, sections)),
        dma((STEPS, sections)),
    ]
    return pl.pallas_call(
        functools.partial(kernel, sections, tiles),
        out_shape=(
            jax.ShapeDtypeStruct(state.shape, F32),
            jax.ShapeDtypeStruct((STEPS, own, heights), F32),
        ),
        in_specs=specs,
        out_specs=(any_spec, any_spec),
        scratch_shapes=scratch,
        compiler_params=pltpu.CompilerParams(
            collective_id=0, has_side_effects=True, vmem_limit_bytes=64 * 1024 * 1024 - 64 * 1024
        ),
        cost_estimate=pl.CostEstimate(flops=700_000_000, bytes_accessed=1_500_000, transcendentals=0),
    )(*args)


def solution(mesh):
    return jax.shard_map(
        functools.partial(shards, mesh.shape["sec"], mesh.shape["tile"]),
        mesh=mesh,
        in_specs=(
            P("sec", None, "tile"),
            P("sec", None, "tile"),
            P("sec", None, "tile"),
            P("sec", None, None),
            P("sec", None),
            P("sec", None, "tile"),
            P("sec", None, "tile"),
            P(),
            P(None, "sec", "tile", None, None),
            P(None, "sec", None, "tile"),
            P(None, "sec", None, "tile"),
            P(None, "sec", "tile"),
            P("sec", None, None),
            P(),
            P(None, ("sec", "tile"), None),
        ),
        out_specs=(P("sec", None, "tile"), P(None, ("sec", "tile"), None)),
        check_vma=False,
    )
```

```python
import functools

import jax
import jax.numpy as jnp
from jax import lax
from jax.experimental import pallas as pl
from jax.experimental.pallas import tpu as pltpu
from jax.sharding import PartitionSpec as P

SUBS = 4
STEPS = 2
HALO = SUBS * STEPS
LANES = 128
PACK = 3 * HALO + 8
F32 = jnp.float32
BF16 = jnp.bfloat16
MESH = pl.DeviceIdType.MESH


def split(x):
    high = x.astype(BF16)
    low = (x - high.astype(F32)).astype(BF16)
    return high, low


def mm(a, b, dims):
    return lax.dot_general(a, b, (dims, ((), ())), preferred_element_type=F32)


NN = ((1,), (0,))
NT = ((1,), (1,))
TN = ((0,), (0,))


def dot3(a, b, dims=NN):
    ah, al = split(a)
    bh, bl = split(b)
    return mm(ah, bh, dims) + (mm(ah, bl, dims) + mm(al, bh, dims))


def kernel(
    sections,
    tiles,
    state,
    tendency,
    diffusion,
    mixing,
    coupling,
    remap_index,
    remap_weight,
    active_cols,
    send_cols,
    occ_slot,
    occ_weight,
    occ_count,
    refraction,
    out_state,
    parts_in,
    field,
    rates,
    forcing,
    drive,
    tend_v,
    diff_v,
    mix_v,
    coup_v,
    ridx_v,
    rw_v,
    cols_v,
    slot_v,
    ow_v,
    oc_v,
    refr_v,
    mix_a,
    mix_b,
    pick_v,
    occ_v,
    gain,
    position,
    weight,
    picked,
    surf,
    tab,
    pack_out,
    pack_in,
    chosen_out,
    chosen_in,
    parts_out,
    load_sem,
    store_sem,
    pack_send,
    pack_recv,
    surf_send,
    surf_recv,
    col_send,
    col_recv,
    red_send,
    red_recv,
):
    levels, columns = tend_v.shape
    ext = field.shape[1]
    blocks = columns // LANES
    rk = ridx_v.shape[0]
    s = lax.axis_index("sec")
    t = lax.axis_index("tile")
    ocean = sections - 1
    is_ocean = s == ocean
    right = lax.rem(t + 1, tiles)
    left = lax.rem(t + tiles - 1, tiles)
    near = ((left, 1), (right, 2), (t, 0))

    loads = [
        (state.at[0], field.at[:, 0:columns]),
        (diffusion.at[0], diff_v),
        (tendency.at[0], tend_v),
        (remap_index.at[0], ridx_v),
        (remap_weight.at[0], rw_v),
        (mixing.at[0], mix_v),
        (coupling, coup_v),
        (send_cols, cols_v),
        (occ_slot, slot_v),
        (occ_weight, ow_v),
        (occ_count, oc_v),
        (refraction.at[0], refr_v),
    ]
    loads = [pltpu.make_async_copy(a, b, load_sem.at[i]) for i, (a, b) in enumerate(loads)]
    def over_tiles(body):
        if tiles <= 8:
            for d in range(1, tiles):
                body(lax.rem(t + d, tiles))
        else:
            lax.fori_loop(1, tiles, lambda d, c: (body(lax.rem(t + d, tiles)), c)[1], 0)

    barrier = pltpu.get_barrier_semaphore()

    def greet(sec, tile):
        pl.semaphore_signal(barrier, inc=1, device_id=(sec, tile), device_id_type=MESH)

    over_tiles(lambda other: greet(s, other))
    for d in range(1, sections):
        greet(lax.rem(s + d, sections), t)

    @pl.when(is_ocean)
    def _():
        for a in range(ocean):
            greet(a, left)
            greet(a, right)

    @pl.when(jnp.logical_not(is_ocean))
    def _():
        greet(ocean, left)
        greet(ocean, right)

    for load in loads:
        load.start()

    lane = lax.broadcasted_iota(jnp.int32, (levels, LANES), 1)
    row_lane = lax.broadcasted_iota(jnp.int32, (1, LANES), 1)

    for load in loads[:5]:
        load.wait()
    surf[0] = field[levels - 1 : levels, 0:columns]

    tail = columns - LANES
    idx_f = ridx_v[...].astype(F32)

    def pack(slot, lo, shift):
        a = field[:, lo : lo + LANES]
        b = diff_v[:, lo : lo + LANES].astype(F32)
        c = tend_v[:, lo : lo + LANES].astype(F32)
        if shift:
            a = pltpu.roll(a, shift, 1)
        b = pltpu.roll(b, shift + HALO, 1)
        c = pltpu.roll(c, shift + 2 * HALO, 1)
        mixed = jnp.where(lane < HALO, a, jnp.where(lane < 2 * HALO, b, c))
        pack_out[slot, 0 : 3 * HALO, :] = mixed.T[0 : 3 * HALO]
        pack_out[slot, 3 * HALO : 3 * HALO + rk, :] = idx_f[:, lo : lo + LANES]
        pack_out[slot, 3 * HALO + rk : PACK, :] = rw_v[:, lo : lo + LANES]

    pack(0, 0, 0)
    pack(1, tail, HALO)

    meet = (tiles - 1) + (sections - 1) + jnp.where(is_ocean, 2 * ocean, 2)
    pl.semaphore_wait(barrier, meet)

    def pack_copy(slot, tile):
        return pltpu.make_async_remote_copy(
            src_ref=pack_out.at[slot],
            dst_ref=pack_in.at[slot],
            send_sem=pack_send.at[slot],
            recv_sem=pack_recv.at[slot],
            device_id=(s, tile),
            device_id_type=MESH,
        )

    def surf_copy(p, d, a, sec, tile, mark):
        return pltpu.make_async_remote_copy(
            src_ref=surf.at[p],
            dst_ref=tab.at[p, d, a],
            send_sem=surf_send.at[p, d, mark],
            recv_sem=surf_recv.at[p, d, a],
            device_id=(sec, tile),
            device_id_type=MESH,
        )

    def surf_each(p, act):
        @pl.when(is_ocean)
        def _():
            for tile, d in near:
                for a in range(ocean):
                    act(surf_copy(p, d, 0, a, tile, a))

        @pl.when(jnp.logical_not(is_ocean))
        def _():
            for tile, d in near:
                act(surf_copy(p, d, s, ocean, tile, 0))

    packs = (pack_copy(0, left), pack_copy(1, right))
    for copy in packs:
        copy.start()
    surf_each(0, lambda copy: copy.start())

    for load in loads[5:]:
        load.wait()
    mh, ml = split(mix_v[...])
    mix_a[:, 0:levels] = mh
    mix_a[:, levels : 2 * levels] = mh
    mix_b[...] = ml
    gain[...] = jnp.broadcast_to(coup_v[...], (LANES, levels)).T
    rates[:, 0:columns] = diff_v[...].astype(F32)
    forcing[:, 0:columns] = tend_v[...].astype(F32)
    for b in range(blocks):
        position[b * rk : (b + 1) * rk, :] = ridx_v[:, b * LANES : (b + 1) * LANES]
        weight[b * rk : (b + 1) * rk, :] = rw_v[:, b * LANES : (b + 1) * LANES]

    limit = active_cols[s]
    number = lax.broadcasted_iota(jnp.int32, (1, ext), 1)
    number = jnp.where(
        number < columns, number, jnp.where(number < columns + LANES // 2, number - columns, number - LANES)
    )
    live = number < limit

    cap = cols_v.shape[3]
    rows = tiles * 8

    def selector(p):
        which = lax.broadcasted_iota(jnp.int32, (rows, tiles), 0)
        owner = lax.broadcasted_iota(jnp.int32, (rows, tiles), 1)
        expand = jnp.where(lax.shift_right_logical(which, 3) == owner, 1.0, 0.0)
        listed = lax.dot_general(
            expand,
            cols_v[p, 0, 0].astype(F32),
            (NT, ((), ())),
            precision=lax.Precision.HIGHEST,
            preferred_element_type=F32,
        )
        r = lax.broadcasted_iota(jnp.int32, (rows, cap), 0)
        c = lax.broadcasted_iota(jnp.int32, (rows, cap), 1)
        column = jnp.sum(jnp.where((r & 7) == c, listed, 0.0), axis=1, keepdims=True)
        rr = lax.broadcasted_iota(jnp.int32, (rows, columns), 0)
        cc = lax.broadcasted_iota(jnp.int32, (rows, columns), 1)
        hit = jnp.logical_and(cc == column.astype(jnp.int32), (rr & 7) < cap)
        return jnp.where(hit, 1.0, 0.0).astype(BF16)

    def occultation_weights(p):
        shape = (rows, slot_v.shape[3])
        m = lax.broadcasted_iota(jnp.int32, shape, 0)
        key = jnp.where((m & 7) < cap, lax.shift_right_logical(m, 3) * cap + (m & 7), -1)
        counts = oc_v[p]
        total = jnp.zeros(shape, F32)
        for k in range(slot_v.shape[2]):
            w = jnp.where(counts > k, ow_v[p, 0, k : k + 1, :], 0.0)
            total = total + jnp.where(key == slot_v[p, 0, k : k + 1, :], w, 0.0)
        return total

    def spread_halves():
        f = field[...]
        around = pltpu.roll(f, 1, 1) + pltpu.roll(f, ext - 1, 1)
        spread = f + rates[...] * (around - 2.0 * f)
        xh, xl = split(spread)
        return jnp.concatenate([xh, xl], axis=0), xh

    def mixed_spread():
        xx, xh = spread_halves()
        return mm(mix_a[...], xx, NN) + mm(mix_b[...], xh, NN)

    def boundary_of(p):
        pos = position[...]
        inner = pos & (LANES - 1)
        outer = lax.shift_right_logical(pos, 7)

        def look(a):
            for d in range(3):
                pltpu.make_async_remote_copy(
                    src_ref=surf.at[p],
                    dst_ref=tab.at[p, d, a],
                    send_sem=surf_send.at[p, d, 0],
                    recv_sem=surf_recv.at[p, d, a],
                    device_id=(s, right),
                    device_id_type=MESH,
                ).wait_recv()
            found = picked[...]
            for b in range(blocks):
                at = slice(b * LANES, (b + 1) * LANES)
                table = jnp.concatenate(
                    [
                        jnp.broadcast_to(tab[p, 0, a, :, at], (blocks * rk, LANES)),
                        jnp.broadcast_to(tab[p, 1, a, :, at], (rk, LANES)),
                        jnp.broadcast_to(tab[p, 2, a, :, at], (rk, LANES)),
                    ],
                    axis=0,
                )
                got = jnp.take_along_axis(table, inner, axis=1, mode="promise_in_bounds")
                found = jnp.where(outer == a * blocks + b, got, found)
            picked[...] = found

        picked[...] = jnp.zeros(picked.shape, F32)
        look(0)

        @pl.when(is_ocean)
        def _():
            for a in range(1, ocean):
                look(a)

        terms = picked[...] * weight[...]
        sums = [jnp.sum(terms[b * rk : (b + 1) * rk], axis=0, keepdims=True) for b in range(blocks + 2)]
        sums[blocks] = jnp.where(row_lane < LANES // 2, sums[blocks], sums[blocks + 1])
        return [
            sums[b] - field[levels - 1 : levels, b * LANES : (b + 1) * LANES] for b in range(blocks + 1)
        ]

    def coupling_step(p):
        product = mixed_spread()
        boundary = boundary_of(p)
        push = jnp.concatenate([gain[...] * row for row in boundary], axis=1)
        push = push + forcing[...]
        field[...] = jnp.where(live, product + push, field[...])
        drive[...] = push

        def substep(_, carry):
            field[...] = jnp.where(live, mixed_spread() + drive[...], field[...])
            return carry

        lax.fori_loop(0, SUBS - 2, substep, 0)
        xx, xh = spread_halves()

        @pl.when(p < STEPS - 1)
        def _():
            low = slice(levels - 8, levels)
            row = mm(mix_a[low, :], xx, NN) + mm(mix_b[low, :], xh, NN) + drive[low, :]
            row = jnp.where(live, row, field[low, :])
            surf[p + 1] = row[7:8, 0:columns]
            surf_each(p + 1, lambda copy: copy.start())

        product = mm(mix_a[...], xx, NN) + mm(mix_b[...], xh, NN)
        field[...] = jnp.where(live, product + drive[...], field[...])

    def column_copy(p, other, source):
        return pltpu.make_async_remote_copy(
            src_ref=chosen_out.at[p, other],
            dst_ref=chosen_in.at[p, source],
            send_sem=col_send.at[p, other],
            recv_sem=col_recv.at[p, source],
            device_id=(s, other),
            device_id_type=MESH,
        )

    def send_columns(p):
        pick = pick_v[p]
        fh, fl = split(field[:, 0:columns])
        taken = mm(pick, fh, NT) + mm(pick, fl, NT)
        projected = dot3(taken, refr_v[...]).reshape(tiles, 8, levels)
        chosen_out[p] = projected
        over_tiles(lambda other: column_copy(p, other, t).start())
        chosen_in[p, t] = chosen_out[p, t]

    own = parts_out.shape[2]

    def part_copy(p, other, source):
        return pltpu.make_async_remote_copy(
            src_ref=parts_out.at[p, other],
            dst_ref=parts_in.at[p, source],
            send_sem=red_send.at[p, other],
            recv_sem=red_recv.at[p, source],
            device_id=(other, t),
            device_id_type=MESH,
        )

    def others():
        return [lax.rem(s + d, sections) for d in range(1, sections)]

    def send_parts(p, w):
        over_tiles(lambda other: column_copy(p, other, other).wait_recv())
        part = dot3(w, chosen_in[p].reshape(rows, levels), TN)
        parts_out[p] = part.reshape(sections, own, levels)
        for other in others():
            part_copy(p, other, s).start()
        pltpu.make_async_copy(parts_out.at[p, s], parts_in.at[p, s], red_recv.at[p, s]).start()

    def list_columns(p, carry):
        pick_v[p] = selector(p)
        return carry

    lax.fori_loop(0, STEPS, list_columns, 0)

    for copy in packs:
        copy.wait_recv()
    gap = jnp.zeros((LANES - 2 * HALO, levels), F32)

    def pad(i):
        at = slice(i * HALO, (i + 1) * HALO)
        return jnp.concatenate([pack_in[0, at, :], gap, pack_in[1, at, :]], axis=0).T

    field[:, columns:ext] = pad(0)
    rates[:, columns:ext] = pad(1)
    forcing[:, columns:ext] = pad(2)
    for i in range(2):
        at = slice((blocks + i) * rk, (blocks + i + 1) * rk)
        position[at, :] = pack_in[i, 3 * HALO : 3 * HALO + rk, :].astype(jnp.int32)
        weight[at, :] = pack_in[i, 3 * HALO + rk : PACK, :]

    store = pltpu.make_async_copy(field.at[:, 0:columns], out_state.at[0], store_sem.at[0])

    def period(p, carry):
        coupling_step(p)

        @pl.when(p == STEPS - 1)
        def _():
            store.start()

        send_columns(p)
        return carry

    lax.fori_loop(0, STEPS, period, 0)

    def weigh(p, carry):
        occ_v[p] = occultation_weights(p)
        return carry

    lax.fori_loop(0, STEPS, weigh, 0)

    def gather_parts(p, carry):
        send_parts(p, occ_v[p])

        @pl.when(p == 0)
        def _():
            for copy in packs:
                copy.wait_send()
            for q in range(STEPS):
                surf_each(q, lambda copy: copy.wait_send())

        over_tiles(lambda other: column_copy(p, other, t).wait_send())
        return carry

    lax.fori_loop(0, STEPS, gather_parts, 0)

    def finish(p, carry):
        for other in others():
            part_copy(p, other, other).wait_recv()
        pltpu.make_async_copy(parts_out.at[p, s], parts_in.at[p, s], red_recv.at[p, s]).wait()
        for other in others():
            part_copy(p, other, s).wait_send()
        return carry

    lax.fori_loop(0, STEPS, finish, 0)
    store.wait()


CHUNKS = 4


def departing(state, parts, abel_matrix, observed, out_state, out_departures, state_v, parts_v, abel_v, obs_v, dep_v, sem):
    rows = state.shape[1] // CHUNKS
    loads = [
        pltpu.make_async_copy(parts, parts_v, sem.at[0]),
        pltpu.make_async_copy(abel_matrix, abel_v, sem.at[1]),
        pltpu.make_async_copy(observed, obs_v, sem.at[2]),
    ]
    bring, take = [], []
    for i in range(CHUNKS):
        at = pl.ds(i * rows, rows)
        bring.append(pltpu.make_async_copy(state.at[:, at], state_v.at[:, at], sem.at[3 + i]))
        take.append(pltpu.make_async_copy(state_v.at[:, at], out_state.at[:, at], sem.at[3 + CHUNKS + i]))
    for copy in bring + loads:
        copy.start()
    for i in range(CHUNKS):
        bring[i].wait()
        take[i].start()
    for copy in loads:
        copy.wait()
    for p in range(STEPS):
        total = parts_v[p, 0]
        for a in range(1, parts_v.shape[1]):
            total = total + parts_v[p, a]
        dep_v[p] = obs_v[p] - dot3(total, abel_v[...])
    last = pltpu.make_async_copy(dep_v, out_departures, sem.at[3 + 2 * CHUNKS])
    last.start()
    for copy in take:
        copy.wait()
    last.wait()


def shards(sections, tiles, *args):
    (state, tendency, diffusion, mixing, coupling, remap_index, remap_weight, active_cols, send_cols) = args[:9]
    (occ_slot, occ_weight, occ_count, refraction, abel_matrix, observed) = args[9:]
    send_cols = jnp.swapaxes(send_cols, 3, 4)
    args = args[:8] + (send_cols,) + args[9:]
    levels, columns = state.shape[1:]
    rk = remap_index.shape[1]
    ext = columns + LANES
    slots = (columns // LANES + 2) * rk
    own = observed.shape[1]
    heights = abel_matrix.shape[1]
    dma = pltpu.SemaphoreType.DMA
    any_spec = pl.BlockSpec(memory_space=pltpu.HBM)
    smem = pl.BlockSpec(memory_space=pltpu.SMEM)
    args = args[:13]
    specs = [any_spec] * len(args)
    specs[7] = smem
    scratch = [
        pltpu.VMEM((levels, ext), F32),
        pltpu.VMEM((levels, ext), F32),
        pltpu.VMEM((levels, ext), F32),
        pltpu.VMEM((levels, ext), F32),
        pltpu.VMEM((levels, columns), BF16),
        pltpu.VMEM((levels, columns), BF16),
        pltpu.VMEM((levels, levels), F32),
        pltpu.VMEM(coupling.shape, F32),
        pltpu.VMEM((rk, columns), jnp.int32),
        pltpu.VMEM((rk, columns), F32),
        pltpu.VMEM(send_cols.shape, jnp.int32),
        pltpu.VMEM(occ_slot.shape, jnp.int32),
        pltpu.VMEM(occ_weight.shape, F32),
        pltpu.VMEM(occ_count.shape, jnp.int32),
        pltpu.VMEM((levels, levels), F32),
        pltpu.VMEM((levels, 2 * levels), BF16),
        pltpu.VMEM((levels, levels), BF16),
        pltpu.VMEM((STEPS, tiles * 8, columns), BF16),
        pltpu.VMEM((STEPS, tiles * 8, occ_slot.shape[3]), F32),
        pltpu.VMEM((levels, LANES), F32),
        pltpu.VMEM((slots, LANES), jnp.int32),
        pltpu.VMEM((slots, LANES), F32),
        pltpu.VMEM((slots, LANES), F32),
        pltpu.VMEM((STEPS, 1, columns), F32),
        pltpu.VMEM((STEPS, 3, sections - 1, 1, columns), F32),
        pltpu.VMEM((2, PACK, LANES), F32),
        pltpu.VMEM((2, PACK, LANES), F32),
        pltpu.VMEM((STEPS, tiles, 8, levels), F32),
        pltpu.VMEM((STEPS, tiles, 8, levels), F32),
        pltpu.VMEM((STEPS, sections, own, levels), F32),
        dma((12,)),
        dma((1,)),
        dma((2,)),
        dma((2,)),
        dma((STEPS, 3, sections - 1)),
        dma((STEPS, 3, sections - 1)),
        dma((STEPS, tiles)),
        dma((STEPS, tiles)),
        dma((STEPS, sections)),
        dma((STEPS, sections)),
    ]
    middle, parts = pl.pallas_call(
        functools.partial(kernel, sections, tiles),
        out_shape=(
            jax.ShapeDtypeStruct(state.shape, F32),
            jax.ShapeDtypeStruct((STEPS, sections, own, levels), F32),
        ),
        in_specs=specs,
        out_specs=(any_spec, any_spec),
        scratch_shapes=scratch,
        compiler_params=pltpu.CompilerParams(
            collective_id=0, has_side_effects=True, vmem_limit_bytes=64 * 1024 * 1024 - 64 * 1024
        ),
        cost_estimate=pl.CostEstimate(flops=700_000_000, bytes_accessed=1_500_000, transcendentals=0),
    )(*args)
    return pl.pallas_call(
        departing,
        out_shape=(jax.ShapeDtypeStruct(state.shape, F32), jax.ShapeDtypeStruct((STEPS, own, heights), F32)),
        in_specs=[any_spec] * 4,
        out_specs=(any_spec, any_spec),
        scratch_shapes=[
            pltpu.VMEM(state.shape, F32),
            pltpu.VMEM(parts.shape, F32),
            pltpu.VMEM(abel_matrix.shape, F32),
            pltpu.VMEM(observed.shape, F32),
            pltpu.VMEM(observed.shape, F32),
            dma((4 + 2 * CHUNKS,)),
        ],
        compiler_params=pltpu.CompilerParams(vmem_limit_bytes=64 * 1024 * 1024 - 64 * 1024),
        cost_estimate=pl.CostEstimate(flops=10_000_000, bytes_accessed=800_000, transcendentals=0),
    )(middle, parts, abel_matrix, observed)


def solution(mesh):
    return jax.shard_map(
        functools.partial(shards, mesh.shape["sec"], mesh.shape["tile"]),
        mesh=mesh,
        in_specs=(
            P("sec", None, "tile"),
            P("sec", None, "tile"),
            P("sec", None, "tile"),
            P("sec", None, None),
            P("sec", None),
            P("sec", None, "tile"),
            P("sec", None, "tile"),
            P(),
            P(None, "sec", "tile", None, None),
            P(None, "sec", None, "tile"),
            P(None, "sec", None, "tile"),
            P(None, "sec", "tile"),
            P("sec", None, None),
            P(),
            P(None, ("sec", "tile"), None),
        ),
        out_specs=(P("sec", None, "tile"), P(None, ("sec", "tile"), None)),
        check_vma=False,
    )
```

```python
import functools

import jax
import jax.numpy as jnp
from jax import lax
from jax.experimental import pallas as pl
from jax.experimental.pallas import tpu as pltpu
from jax.sharding import PartitionSpec as P

SUBS = 4
STEPS = 2
HALO = SUBS * STEPS
LANES = 128
PACK = 3 * HALO + 8
F32 = jnp.float32
BF16 = jnp.bfloat16
MESH = pl.DeviceIdType.MESH


def split(x):
    high = x.astype(BF16)
    low = (x - high.astype(F32)).astype(BF16)
    return high, low


def mm(a, b, dims):
    return lax.dot_general(a, b, (dims, ((), ())), preferred_element_type=F32)


NN = ((1,), (0,))
NT = ((1,), (1,))
TN = ((0,), (0,))


def dot3(a, b, dims=NN):
    ah, al = split(a)
    bh, bl = split(b)
    return mm(ah, bh, dims) + (mm(ah, bl, dims) + mm(al, bh, dims))


def kernel(
    sections,
    tiles,
    state,
    tendency,
    diffusion,
    mixing,
    coupling,
    remap_index,
    remap_weight,
    active_cols,
    send_cols,
    occ_slot,
    occ_weight,
    occ_count,
    refraction,
    out_state,
    parts_in,
    cols_in,
    rows_in,
    field,
    rates,
    forcing,
    drive,
    tend_v,
    diff_v,
    mix_v,
    coup_v,
    ridx_v,
    rw_v,
    cols_v,
    slot_v,
    ow_v,
    oc_v,
    refr_v,
    mix_a,
    mix_b,
    pick_v,
    gain,
    position,
    weight,
    picked,
    surf,
    tab,
    pack_out,
    pack_in,
    chosen_out,
    chosen_in,
    parts_out,
    rows_out,
    load_sem,
    store_sem,
    pack_send,
    pack_recv,
    surf_send,
    surf_recv,
    col_send,
    col_recv,
    red_send,
    red_recv,
    last_send,
    last_recv,
    row_send,
    row_recv,
):
    levels, columns = tend_v.shape
    ext = field.shape[1]
    blocks = columns // LANES
    rk = ridx_v.shape[0]
    s = lax.axis_index("sec")
    t = lax.axis_index("tile")
    ocean = sections - 1
    is_ocean = s == ocean
    right = lax.rem(t + 1, tiles)
    left = lax.rem(t + tiles - 1, tiles)
    near = ((left, 1), (right, 2), (t, 0))

    loads = [
        (state.at[0], field.at[:, 0:columns]),
        (diffusion.at[0], diff_v),
        (tendency.at[0], tend_v),
        (remap_index.at[0], ridx_v),
        (remap_weight.at[0], rw_v),
        (mixing.at[0], mix_v),
        (coupling, coup_v),
        (send_cols, cols_v),
        (occ_slot, slot_v),
        (occ_weight, ow_v),
        (occ_count, oc_v),
        (refraction.at[0], refr_v),
    ]
    loads = [pltpu.make_async_copy(a, b, load_sem.at[i]) for i, (a, b) in enumerate(loads)]
    def over_tiles(body):
        if tiles <= 8:
            for d in range(1, tiles):
                body(lax.rem(t + d, tiles))
        else:
            lax.fori_loop(1, tiles, lambda d, c: (body(lax.rem(t + d, tiles)), c)[1], 0)

    barrier = pltpu.get_barrier_semaphore()

    def greet(sec, tile):
        pl.semaphore_signal(barrier, inc=1, device_id=(sec, tile), device_id_type=MESH)

    def beyond(body):
        for q in range(sections):
            over_tiles(lambda other: body(lax.rem(s + q, sections), other))
        for d in range(1, sections):
            body(lax.rem(s + d, sections), t)

    beyond(greet)

    for load in loads:
        load.start()

    lane = lax.broadcasted_iota(jnp.int32, (levels, LANES), 1)
    row_lane = lax.broadcasted_iota(jnp.int32, (1, LANES), 1)

    for load in loads[:5]:
        load.wait()
    surf[0] = field[levels - 1 : levels, 0:columns]

    tail = columns - LANES
    idx_f = ridx_v[...].astype(F32)

    def pack(slot, lo, shift):
        a = field[:, lo : lo + LANES]
        b = diff_v[:, lo : lo + LANES].astype(F32)
        c = tend_v[:, lo : lo + LANES].astype(F32)
        if shift:
            a = pltpu.roll(a, shift, 1)
        b = pltpu.roll(b, shift + HALO, 1)
        c = pltpu.roll(c, shift + 2 * HALO, 1)
        mixed = jnp.where(lane < HALO, a, jnp.where(lane < 2 * HALO, b, c))
        pack_out[slot, 0 : 3 * HALO, :] = mixed.T[0 : 3 * HALO]
        pack_out[slot, 3 * HALO : 3 * HALO + rk, :] = idx_f[:, lo : lo + LANES]
        pack_out[slot, 3 * HALO + rk : PACK, :] = rw_v[:, lo : lo + LANES]

    pack(0, 0, 0)
    pack(1, tail, HALO)

    pl.semaphore_wait(barrier, sections * tiles - 1)

    def pack_copy(slot, tile):
        return pltpu.make_async_remote_copy(
            src_ref=pack_out.at[slot],
            dst_ref=pack_in.at[slot],
            send_sem=pack_send.at[slot],
            recv_sem=pack_recv.at[slot],
            device_id=(s, tile),
            device_id_type=MESH,
        )

    def surf_copy(p, d, a, sec, tile, mark):
        return pltpu.make_async_remote_copy(
            src_ref=surf.at[p],
            dst_ref=tab.at[p, d, a],
            send_sem=surf_send.at[p, d, mark],
            recv_sem=surf_recv.at[p, d, a],
            device_id=(sec, tile),
            device_id_type=MESH,
        )

    def surf_each(p, act):
        @pl.when(is_ocean)
        def _():
            for tile, d in near:
                for a in range(ocean):
                    act(surf_copy(p, d, 0, a, tile, a))

        @pl.when(jnp.logical_not(is_ocean))
        def _():
            for tile, d in near:
                act(surf_copy(p, d, s, ocean, tile, 0))

    packs = (pack_copy(0, left), pack_copy(1, right))
    for copy in packs:
        copy.start()
    surf_each(0, lambda copy: copy.start())

    for load in loads[5:]:
        load.wait()
    mh, ml = split(mix_v[...])
    mix_a[:, 0:levels] = mh
    mix_a[:, levels : 2 * levels] = mh
    mix_b[...] = ml
    gain[...] = jnp.broadcast_to(coup_v[...], (LANES, levels)).T
    rates[:, 0:columns] = diff_v[...].astype(F32)
    forcing[:, 0:columns] = tend_v[...].astype(F32)
    for b in range(blocks):
        position[b * rk : (b + 1) * rk, :] = ridx_v[:, b * LANES : (b + 1) * LANES]
        weight[b * rk : (b + 1) * rk, :] = rw_v[:, b * LANES : (b + 1) * LANES]

    limit = active_cols[s]
    number = lax.broadcasted_iota(jnp.int32, (1, ext), 1)
    number = jnp.where(
        number < columns, number, jnp.where(number < columns + LANES // 2, number - columns, number - LANES)
    )
    live = number < limit

    cap = cols_v.shape[3]
    rows = tiles * 8

    def selector(p):
        which = lax.broadcasted_iota(jnp.int32, (rows, tiles), 0)
        owner = lax.broadcasted_iota(jnp.int32, (rows, tiles), 1)
        expand = jnp.where(lax.shift_right_logical(which, 3) == owner, 1.0, 0.0)
        listed = lax.dot_general(
            expand,
            cols_v[p, 0, 0].astype(F32),
            (NT, ((), ())),
            precision=lax.Precision.HIGHEST,
            preferred_element_type=F32,
        )
        r = lax.broadcasted_iota(jnp.int32, (rows, cap), 0)
        c = lax.broadcasted_iota(jnp.int32, (rows, cap), 1)
        column = jnp.sum(jnp.where((r & 7) == c, listed, 0.0), axis=1, keepdims=True)
        rr = lax.broadcasted_iota(jnp.int32, (rows, columns), 0)
        cc = lax.broadcasted_iota(jnp.int32, (rows, columns), 1)
        hit = jnp.logical_and(cc == column.astype(jnp.int32), (rr & 7) < cap)
        return jnp.where(hit, 1.0, 0.0).astype(BF16)

    def occultation_weights(p):
        shape = (rows, slot_v.shape[3])
        m = lax.broadcasted_iota(jnp.int32, shape, 0)
        key = jnp.where((m & 7) < cap, lax.shift_right_logical(m, 3) * cap + (m & 7), -1)
        counts = oc_v[p]
        total = jnp.zeros(shape, F32)
        for k in range(slot_v.shape[2]):
            w = jnp.where(counts > k, ow_v[p, 0, k : k + 1, :], 0.0)
            total = total + jnp.where(key == slot_v[p, 0, k : k + 1, :], w, 0.0)
        return total

    def spread_halves():
        f = field[...]
        around = pltpu.roll(f, 1, 1) + pltpu.roll(f, ext - 1, 1)
        spread = f + rates[...] * (around - 2.0 * f)
        xh, xl = split(spread)
        return jnp.concatenate([xh, xl], axis=0), xh

    def mixed_spread():
        xx, xh = spread_halves()
        return mm(mix_a[...], xx, NN) + mm(mix_b[...], xh, NN)

    def boundary_of(p):
        pos = position[...]
        inner = pos & (LANES - 1)
        outer = lax.shift_right_logical(pos, 7)

        def look(a):
            for d in range(3):
                pltpu.make_async_remote_copy(
                    src_ref=surf.at[p],
                    dst_ref=tab.at[p, d, a],
                    send_sem=surf_send.at[p, d, 0],
                    recv_sem=surf_recv.at[p, d, a],
                    device_id=(s, right),
                    device_id_type=MESH,
                ).wait_recv()
            found = picked[...]
            for b in range(blocks):
                at = slice(b * LANES, (b + 1) * LANES)
                table = jnp.concatenate(
                    [
                        jnp.broadcast_to(tab[p, 0, a, :, at], (blocks * rk, LANES)),
                        jnp.broadcast_to(tab[p, 1, a, :, at], (rk, LANES)),
                        jnp.broadcast_to(tab[p, 2, a, :, at], (rk, LANES)),
                    ],
                    axis=0,
                )
                got = jnp.take_along_axis(table, inner, axis=1, mode="promise_in_bounds")
                found = jnp.where(outer == a * blocks + b, got, found)
            picked[...] = found

        picked[...] = jnp.zeros(picked.shape, F32)
        look(0)

        @pl.when(is_ocean)
        def _():
            for a in range(1, ocean):
                look(a)

        terms = picked[...] * weight[...]
        sums = [jnp.sum(terms[b * rk : (b + 1) * rk], axis=0, keepdims=True) for b in range(blocks + 2)]
        sums[blocks] = jnp.where(row_lane < LANES // 2, sums[blocks], sums[blocks + 1])
        return [
            sums[b] - field[levels - 1 : levels, b * LANES : (b + 1) * LANES] for b in range(blocks + 1)
        ]

    def coupling_step(p):
        product = mixed_spread()
        boundary = boundary_of(p)
        push = jnp.concatenate([gain[...] * row for row in boundary], axis=1)
        push = push + forcing[...]
        field[...] = jnp.where(live, product + push, field[...])
        drive[...] = push

        def substep(_, carry):
            field[...] = jnp.where(live, mixed_spread() + drive[...], field[...])
            return carry

        lax.fori_loop(0, SUBS - 2, substep, 0)
        xx, xh = spread_halves()

        @pl.when(p < STEPS - 1)
        def _():
            low = slice(levels - 8, levels)
            row = mm(mix_a[low, :], xx, NN) + mm(mix_b[low, :], xh, NN) + drive[low, :]
            row = jnp.where(live, row, field[low, :])
            surf[p + 1] = row[7:8, 0:columns]
            surf_each(p + 1, lambda copy: copy.start())

        product = mm(mix_a[...], xx, NN) + mm(mix_b[...], xh, NN)
        field[...] = jnp.where(live, product + drive[...], field[...])

    def column_copy(p, other, source):
        return pltpu.make_async_remote_copy(
            src_ref=chosen_out.at[p, other],
            dst_ref=chosen_in.at[p, source],
            send_sem=col_send.at[p, other],
            recv_sem=col_recv.at[p, source],
            device_id=(s, other),
            device_id_type=MESH,
        )

    def last_copy(sec, other, from_sec, from_tile):
        return pltpu.make_async_remote_copy(
            src_ref=chosen_out.at[STEPS - 1, other, 0:cap],
            dst_ref=cols_in.at[from_sec, from_tile, 0:cap],
            send_sem=last_send.at[sec, other],
            recv_sem=last_recv.at[from_sec, from_tile],
            device_id=(sec, other),
            device_id_type=MESH,
        )

    own_columns = pltpu.make_async_copy(
        chosen_out.at[STEPS - 1, t, 0:cap], cols_in.at[s, t, 0:cap], last_recv.at[s, t]
    )

    def row_copy(sec, source):
        return pltpu.make_async_remote_copy(
            src_ref=rows_out.at[sec],
            dst_ref=rows_in.at[source],
            send_sem=row_send.at[sec],
            recv_sem=row_recv.at[source],
            device_id=(sec, t),
            device_id_type=MESH,
        )

    own_rows = pltpu.make_async_copy(rows_out.at[s], rows_in.at[s], row_recv.at[s])

    def send_columns(p):
        pick = pick_v[p]
        fh, fl = split(field[:, 0:columns])
        taken = mm(pick, fh, NT) + mm(pick, fl, NT)
        projected = dot3(taken, refr_v[...]).reshape(tiles, 8, levels)
        chosen_out[p] = projected

        @pl.when(p < STEPS - 1)
        def _():
            over_tiles(lambda other: column_copy(p, other, t).start())
            chosen_in[p, t] = chosen_out[p, t]

        @pl.when(p == STEPS - 1)
        def _():
            beyond(lambda sec, other: last_copy(sec, other, s, t).start())
            own_columns.start()

    own = parts_out.shape[2]

    def part_copy(p, other, source):
        return pltpu.make_async_remote_copy(
            src_ref=parts_out.at[p, other],
            dst_ref=parts_in.at[p, source],
            send_sem=red_send.at[p, other],
            recv_sem=red_recv.at[p, source],
            device_id=(other, t),
            device_id_type=MESH,
        )

    def others():
        return [lax.rem(s + d, sections) for d in range(1, sections)]

    def send_parts(p, w):
        over_tiles(lambda other: column_copy(p, other, other).wait_recv())
        part = dot3(w, chosen_in[p].reshape(rows, levels), TN)
        parts_out[p] = part.reshape(sections, own, levels)
        for other in others():
            part_copy(p, other, s).start()
        pltpu.make_async_copy(parts_out.at[p, s], parts_in.at[p, s], red_recv.at[p, s]).start()

    def list_columns(p, carry):
        pick_v[p] = selector(p)
        return carry

    lax.fori_loop(0, STEPS, list_columns, 0)

    for copy in packs:
        copy.wait_recv()
    gap = jnp.zeros((LANES - 2 * HALO, levels), F32)

    def pad(i):
        at = slice(i * HALO, (i + 1) * HALO)
        return jnp.concatenate([pack_in[0, at, :], gap, pack_in[1, at, :]], axis=0).T

    field[:, columns:ext] = pad(0)
    rates[:, columns:ext] = pad(1)
    forcing[:, columns:ext] = pad(2)
    for i in range(2):
        at = slice((blocks + i) * rk, (blocks + i + 1) * rk)
        position[at, :] = pack_in[i, 3 * HALO : 3 * HALO + rk, :].astype(jnp.int32)
        weight[at, :] = pack_in[i, 3 * HALO + rk : PACK, :]

    store = pltpu.make_async_copy(field.at[:, 0:columns], out_state.at[0], store_sem.at[0])

    def period(p, carry):
        coupling_step(p)

        @pl.when(p == STEPS - 1)
        def _():
            store.start()

        send_columns(p)
        return carry

    lax.fori_loop(0, STEPS, period, 0)

    def gather_parts(p, carry):
        send_parts(p, occultation_weights(p))
        over_tiles(lambda other: column_copy(p, other, t).wait_send())
        return carry

    lax.fori_loop(0, STEPS - 1, gather_parts, 0)
    rows_out[...] = occultation_weights(STEPS - 1).T.reshape(rows_out.shape)
    for other in others():
        row_copy(other, s).start()
    own_rows.start()

    for copy in packs:
        copy.wait_send()
    for q in range(STEPS):
        surf_each(q, lambda copy: copy.wait_send())
    store.wait()

    def finish(p, carry):
        for other in others():
            part_copy(p, other, other).wait_recv()
        pltpu.make_async_copy(parts_out.at[p, s], parts_in.at[p, s], red_recv.at[p, s]).wait()
        for other in others():
            part_copy(p, other, s).wait_send()
        return carry

    lax.fori_loop(0, STEPS - 1, finish, 0)
    beyond(lambda sec, other: last_copy(sec, other, s, t).wait_send())
    own_columns.wait()
    for other in others():
        row_copy(other, s).wait_send()
    beyond(lambda sec, other: last_copy(sec, other, sec, other).wait_recv())
    for other in others():
        row_copy(other, other).wait_recv()
    own_rows.wait()


CHUNKS = 4


def departing(
    cap,
    state,
    parts,
    cols,
    weights,
    abel_matrix,
    observed,
    out_state,
    out_departures,
    state_v,
    parts_v,
    cols_v,
    weights_v,
    abel_v,
    obs_v,
    dep_v,
    sem,
):
    rows = state.shape[1] // CHUNKS
    loads = [
        pltpu.make_async_copy(cols, cols_v, sem.at[0]),
        pltpu.make_async_copy(weights, weights_v, sem.at[1]),
        pltpu.make_async_copy(parts, parts_v, sem.at[2]),
        pltpu.make_async_copy(abel_matrix, abel_v, sem.at[3]),
        pltpu.make_async_copy(observed, obs_v, sem.at[4]),
    ]
    bring, take = [], []
    for i in range(CHUNKS):
        at = pl.ds(i * rows, rows)
        bring.append(pltpu.make_async_copy(state.at[:, at], state_v.at[:, at], sem.at[5 + i]))
        take.append(pltpu.make_async_copy(state_v.at[:, at], out_state.at[:, at], sem.at[5 + CHUNKS + i]))
    for copy in loads + bring:
        copy.start()
    for i in range(CHUNKS):
        bring[i].wait()
        take[i].start()
    for copy in loads:
        copy.wait()
    sections, _, columns = weights_v.shape
    levels = cols_v.shape[3]
    sent = (lax.broadcasted_iota(jnp.int32, (columns, levels), 0) & 7) < cap
    totals = []
    for p in range(STEPS - 1):
        totals.append(parts_v[p, 0])
        for a in range(1, sections):
            totals[p] = totals[p] + parts_v[p, a]
    for a in range(sections):
        term = dot3(weights_v[a], jnp.where(sent, cols_v[a].reshape(columns, levels), 0.0))
        totals.append(term) if a == 0 else totals.append(totals.pop() + term)
    for p in range(STEPS):
        dep_v[p] = obs_v[p] - dot3(totals[p], abel_v[...])
    last = pltpu.make_async_copy(dep_v, out_departures, sem.at[5 + 2 * CHUNKS])
    last.start()
    for copy in take:
        copy.wait()
    last.wait()


def shards(sections, tiles, *args):
    (state, tendency, diffusion, mixing, coupling, remap_index, remap_weight, active_cols, send_cols) = args[:9]
    (occ_slot, occ_weight, occ_count, refraction, abel_matrix, observed) = args[9:]
    send_cols = jnp.swapaxes(send_cols, 3, 4)
    args = args[:8] + (send_cols,) + args[9:]
    levels, columns = state.shape[1:]
    rk = remap_index.shape[1]
    ext = columns + LANES
    slots = (columns // LANES + 2) * rk
    own = observed.shape[1]
    heights = abel_matrix.shape[1]
    dma = pltpu.SemaphoreType.DMA
    any_spec = pl.BlockSpec(memory_space=pltpu.HBM)
    smem = pl.BlockSpec(memory_space=pltpu.SMEM)
    args = args[:13]
    specs = [any_spec] * len(args)
    specs[7] = smem
    scratch = [
        pltpu.VMEM((levels, ext), F32),
        pltpu.VMEM((levels, ext), F32),
        pltpu.VMEM((levels, ext), F32),
        pltpu.VMEM((levels, ext), F32),
        pltpu.VMEM((levels, columns), BF16),
        pltpu.VMEM((levels, columns), BF16),
        pltpu.VMEM((levels, levels), F32),
        pltpu.VMEM(coupling.shape, F32),
        pltpu.VMEM((rk, columns), jnp.int32),
        pltpu.VMEM((rk, columns), F32),
        pltpu.VMEM(send_cols.shape, jnp.int32),
        pltpu.VMEM(occ_slot.shape, jnp.int32),
        pltpu.VMEM(occ_weight.shape, F32),
        pltpu.VMEM(occ_count.shape, jnp.int32),
        pltpu.VMEM((levels, levels), F32),
        pltpu.VMEM((levels, 2 * levels), BF16),
        pltpu.VMEM((levels, levels), BF16),
        pltpu.VMEM((STEPS, tiles * 8, columns), BF16),
        pltpu.VMEM((levels, LANES), F32),
        pltpu.VMEM((slots, LANES), jnp.int32),
        pltpu.VMEM((slots, LANES), F32),
        pltpu.VMEM((slots, LANES), F32),
        pltpu.VMEM((STEPS, 1, columns), F32),
        pltpu.VMEM((STEPS, 3, sections - 1, 1, columns), F32),
        pltpu.VMEM((2, PACK, LANES), F32),
        pltpu.VMEM((2, PACK, LANES), F32),
        pltpu.VMEM((STEPS, tiles, 8, levels), F32),
        pltpu.VMEM((STEPS, tiles, 8, levels), F32),
        pltpu.VMEM((STEPS - 1, sections, own, levels), F32),
        pltpu.VMEM((sections, own, tiles * 8), F32),
        dma((12,)),
        dma((1,)),
        dma((2,)),
        dma((2,)),
        dma((STEPS, 3, sections - 1)),
        dma((STEPS, 3, sections - 1)),
        dma((STEPS, tiles)),
        dma((STEPS, tiles)),
        dma((STEPS, sections)),
        dma((STEPS, sections)),
        dma((sections, tiles)),
        dma((sections, tiles)),
        dma((sections,)),
        dma((sections,)),
    ]
    middle, parts, cols, weights = pl.pallas_call(
        functools.partial(kernel, sections, tiles),
        out_shape=(
            jax.ShapeDtypeStruct(state.shape, F32),
            jax.ShapeDtypeStruct((STEPS - 1, sections, own, levels), F32),
            jax.ShapeDtypeStruct((sections, tiles, 8, levels), F32),
            jax.ShapeDtypeStruct((sections, own, tiles * 8), F32),
        ),
        in_specs=specs,
        out_specs=(any_spec,) * 4,
        scratch_shapes=scratch,
        compiler_params=pltpu.CompilerParams(
            collective_id=0, has_side_effects=True, vmem_limit_bytes=64 * 1024 * 1024 - 64 * 1024
        ),
        cost_estimate=pl.CostEstimate(flops=700_000_000, bytes_accessed=1_500_000, transcendentals=0),
    )(*args)
    return pl.pallas_call(
        functools.partial(departing, send_cols.shape[3]),
        out_shape=(jax.ShapeDtypeStruct(state.shape, F32), jax.ShapeDtypeStruct((STEPS, own, heights), F32)),
        in_specs=[any_spec] * 6,
        out_specs=(any_spec, any_spec),
        scratch_shapes=[
            pltpu.VMEM(state.shape, F32),
            pltpu.VMEM(parts.shape, F32),
            pltpu.VMEM(cols.shape, F32),
            pltpu.VMEM(weights.shape, F32),
            pltpu.VMEM(abel_matrix.shape, F32),
            pltpu.VMEM(observed.shape, F32),
            pltpu.VMEM(observed.shape, F32),
            dma((6 + 2 * CHUNKS,)),
        ],
        compiler_params=pltpu.CompilerParams(vmem_limit_bytes=64 * 1024 * 1024 - 64 * 1024),
        cost_estimate=pl.CostEstimate(flops=10_000_000, bytes_accessed=800_000, transcendentals=0),
    )(middle, parts, cols, weights, abel_matrix, observed)


def solution(mesh):
    return jax.shard_map(
        functools.partial(shards, mesh.shape["sec"], mesh.shape["tile"]),
        mesh=mesh,
        in_specs=(
            P("sec", None, "tile"),
            P("sec", None, "tile"),
            P("sec", None, "tile"),
            P("sec", None, None),
            P("sec", None),
            P("sec", None, "tile"),
            P("sec", None, "tile"),
            P(),
            P(None, "sec", "tile", None, None),
            P(None, "sec", None, "tile"),
            P(None, "sec", None, "tile"),
            P(None, "sec", "tile"),
            P("sec", None, None),
            P(),
            P(None, ("sec", "tile"), None),
        ),
        out_specs=(P("sec", None, "tile"), P(None, ("sec", "tile"), None)),
        check_vma=False,
    )
```

```python
import functools

import jax
import jax.numpy as jnp
from jax import lax
from jax.experimental import pallas as pl
from jax.experimental.pallas import tpu as pltpu
from jax.sharding import PartitionSpec as P

SUBS = 4
STEPS = 2
HALO = SUBS * STEPS
LANES = 128
PACK = 3 * HALO + 8
F32 = jnp.float32
BF16 = jnp.bfloat16
MESH = pl.DeviceIdType.MESH


def split(x):
    high = x.astype(BF16)
    low = (x - high.astype(F32)).astype(BF16)
    return high, low


def mm(a, b, dims):
    return lax.dot_general(a, b, (dims, ((), ())), preferred_element_type=F32)


NN = ((1,), (0,))
NT = ((1,), (1,))
TN = ((0,), (0,))


def dot3(a, b, dims=NN):
    ah, al = split(a)
    bh, bl = split(b)
    return mm(ah, bh, dims) + (mm(ah, bl, dims) + mm(al, bh, dims))


def kernel(
    sections,
    tiles,
    state,
    tendency,
    diffusion,
    mixing,
    coupling,
    remap_index,
    remap_weight,
    active_cols,
    send_cols,
    occ_slot,
    occ_weight,
    occ_count,
    refraction,
    out_state,
    parts_in,
    cols_in,
    rows_in,
    field,
    rates,
    forcing,
    drive,
    tend_v,
    diff_v,
    mix_v,
    coup_v,
    ridx_v,
    rw_v,
    cols_v,
    slot_v,
    ow_v,
    oc_v,
    refr_v,
    mix_a,
    mix_b,
    pick_v,
    gain,
    position,
    weight,
    picked,
    surf,
    tab,
    pack_out,
    pack_in,
    chosen_out,
    chosen_in,
    parts_out,
    rows_out,
    spare,
    load_sem,
    store_sem,
    pack_send,
    pack_recv,
    surf_send,
    surf_recv,
    col_send,
    col_recv,
    red_send,
    red_recv,
    last_send,
    last_recv,
    row_send,
    row_recv,
):
    levels, columns = tend_v.shape
    ext = field.shape[1]
    blocks = columns // LANES
    rk = ridx_v.shape[0]
    s = lax.axis_index("sec")
    t = lax.axis_index("tile")
    ocean = sections - 1
    is_ocean = s == ocean
    right = lax.rem(t + 1, tiles)
    left = lax.rem(t + tiles - 1, tiles)
    near = ((left, 1), (right, 2), (t, 0))

    loads = [
        (state.at[0], field.at[:, 0:columns]),
        (diffusion.at[0], diff_v),
        (tendency.at[0], tend_v),
        (remap_index.at[0], ridx_v),
        (remap_weight.at[0], rw_v),
        (mixing.at[0], mix_v),
        (coupling, coup_v),
        (send_cols, cols_v),
        (occ_slot, slot_v),
        (occ_weight, ow_v),
        (occ_count, oc_v),
        (refraction.at[0], refr_v),
    ]
    loads = [pltpu.make_async_copy(a, b, load_sem.at[i]) for i, (a, b) in enumerate(loads)]
    for load in loads[:5]:
        load.start()

    def drain(ref, sem):
        pltpu.make_async_copy(ref, ref, sem).wait()

    def over_tiles(body):
        if tiles <= 8:
            for d in range(1, tiles):
                body(lax.rem(t + d, tiles))
        else:
            lax.fori_loop(1, tiles, lambda d, c: (body(lax.rem(t + d, tiles)), c)[1], 0)

    barrier = pltpu.get_barrier_semaphore()

    def greet(sec, tile):
        pl.semaphore_signal(barrier, inc=1, device_id=(sec, tile), device_id_type=MESH)

    def beyond(body):
        for q in range(sections):
            over_tiles(lambda other: body(lax.rem(s + q, sections), other))
        for d in range(1, sections):
            body(lax.rem(s + d, sections), t)

    beyond(greet)

    for load in loads[5:]:
        load.start()

    lane = lax.broadcasted_iota(jnp.int32, (levels, LANES), 1)
    row_lane = lax.broadcasted_iota(jnp.int32, (1, LANES), 1)

    for load in loads[:5]:
        load.wait()
    surf[0] = field[levels - 1 : levels, 0:columns]

    tail = columns - LANES
    idx_f = ridx_v[...].astype(F32)

    def pack(slot, lo, shift):
        a = field[:, lo : lo + LANES]
        b = diff_v[:, lo : lo + LANES].astype(F32)
        c = tend_v[:, lo : lo + LANES].astype(F32)
        if shift:
            a = pltpu.roll(a, shift, 1)
        b = pltpu.roll(b, shift + HALO, 1)
        c = pltpu.roll(c, shift + 2 * HALO, 1)
        mixed = jnp.where(lane < HALO, a, jnp.where(lane < 2 * HALO, b, c))
        pack_out[slot, 0 : 3 * HALO, :] = mixed.T[0 : 3 * HALO]
        pack_out[slot, 3 * HALO : 3 * HALO + rk, :] = idx_f[:, lo : lo + LANES]
        pack_out[slot, 3 * HALO + rk : PACK, :] = rw_v[:, lo : lo + LANES]

    pack(0, 0, 0)
    pack(1, tail, HALO)

    pl.semaphore_wait(barrier, sections * tiles - 1)

    def pack_copy(slot, tile):
        return pltpu.make_async_remote_copy(
            src_ref=pack_out.at[slot],
            dst_ref=pack_in.at[slot],
            send_sem=pack_send.at[slot],
            recv_sem=pack_recv.at[slot],
            device_id=(s, tile),
            device_id_type=MESH,
        )

    def surf_copy(p, d, a, sec, tile, mark):
        return pltpu.make_async_remote_copy(
            src_ref=surf.at[p],
            dst_ref=tab.at[p, d, a],
            send_sem=surf_send.at[p, mark],
            recv_sem=surf_recv.at[p, a],
            device_id=(sec, tile),
            device_id_type=MESH,
        )

    def surf_sent(p):
        @pl.when(is_ocean)
        def _():
            for a in range(ocean):
                drain(tab.at[p, :, a], surf_send.at[p, a])

        @pl.when(jnp.logical_not(is_ocean))
        def _():
            drain(tab.at[p, :, 0], surf_send.at[p, 0])

    def surf_each(p, act):
        @pl.when(is_ocean)
        def _():
            for tile, d in near:
                for a in range(ocean):
                    act(surf_copy(p, d, 0, a, tile, a))

        @pl.when(jnp.logical_not(is_ocean))
        def _():
            for tile, d in near:
                act(surf_copy(p, d, s, ocean, tile, 0))

    packs = (pack_copy(0, left), pack_copy(1, right))
    for copy in packs:
        copy.start()
    surf_each(0, lambda copy: copy.start())

    for load in loads[5:]:
        load.wait()
    mh, ml = split(mix_v[...])
    mix_a[:, 0:levels] = mh
    mix_a[:, levels : 2 * levels] = mh
    mix_b[...] = ml
    gain[...] = jnp.broadcast_to(coup_v[...], (LANES, levels)).T
    rates[:, 0:columns] = diff_v[...].astype(F32)
    forcing[:, 0:columns] = tend_v[...].astype(F32)
    for b in range(blocks):
        position[b * rk : (b + 1) * rk, :] = ridx_v[:, b * LANES : (b + 1) * LANES]
        weight[b * rk : (b + 1) * rk, :] = rw_v[:, b * LANES : (b + 1) * LANES]

    limit = active_cols[s]
    number = lax.broadcasted_iota(jnp.int32, (1, ext), 1)
    number = jnp.where(
        number < columns, number, jnp.where(number < columns + LANES // 2, number - columns, number - LANES)
    )
    live = number < limit

    cap = cols_v.shape[3]
    rows = tiles * 8

    def selector(p):
        which = lax.broadcasted_iota(jnp.int32, (rows, tiles), 0)
        owner = lax.broadcasted_iota(jnp.int32, (rows, tiles), 1)
        expand = jnp.where(lax.shift_right_logical(which, 3) == owner, 1.0, 0.0)
        listed = lax.dot_general(
            expand,
            cols_v[p, 0, 0].astype(F32),
            (NT, ((), ())),
            precision=lax.Precision.HIGHEST,
            preferred_element_type=F32,
        )
        r = lax.broadcasted_iota(jnp.int32, (rows, cap), 0)
        c = lax.broadcasted_iota(jnp.int32, (rows, cap), 1)
        column = jnp.sum(jnp.where((r & 7) == c, listed, 0.0), axis=1, keepdims=True)
        rr = lax.broadcasted_iota(jnp.int32, (rows, columns), 0)
        cc = lax.broadcasted_iota(jnp.int32, (rows, columns), 1)
        hit = jnp.logical_and(cc == column.astype(jnp.int32), (rr & 7) < cap)
        return jnp.where(hit, 1.0, 0.0).astype(BF16)

    def occultation_weights(p):
        shape = (rows, slot_v.shape[3])
        m = lax.broadcasted_iota(jnp.int32, shape, 0)
        key = jnp.where((m & 7) < cap, lax.shift_right_logical(m, 3) * cap + (m & 7), -1)
        counts = oc_v[p]
        total = jnp.zeros(shape, F32)
        for k in range(slot_v.shape[2]):
            w = jnp.where(counts > k, ow_v[p, 0, k : k + 1, :], 0.0)
            total = total + jnp.where(key == slot_v[p, 0, k : k + 1, :], w, 0.0)
        return total

    def spread_halves():
        f = field[...]
        around = pltpu.roll(f, 1, 1) + pltpu.roll(f, ext - 1, 1)
        spread = f + rates[...] * (around - 2.0 * f)
        xh, xl = split(spread)
        return jnp.concatenate([xh, xl], axis=0), xh

    def mixed_spread():
        xx, xh = spread_halves()
        return mm(mix_a[...], xx, NN) + mm(mix_b[...], xh, NN)

    def boundary_of(p):
        pos = position[...]
        inner = pos & (LANES - 1)
        outer = lax.shift_right_logical(pos, 7)

        def look(a):
            drain(tab.at[p, :, a], surf_recv.at[p, a])
            found = picked[...]
            for b in range(blocks):
                at = slice(b * LANES, (b + 1) * LANES)
                table = jnp.concatenate(
                    [
                        jnp.broadcast_to(tab[p, 0, a, :, at], (blocks * rk, LANES)),
                        jnp.broadcast_to(tab[p, 1, a, :, at], (rk, LANES)),
                        jnp.broadcast_to(tab[p, 2, a, :, at], (rk, LANES)),
                    ],
                    axis=0,
                )
                got = jnp.take_along_axis(table, inner, axis=1, mode="promise_in_bounds")
                found = jnp.where(outer == a * blocks + b, got, found)
            picked[...] = found

        picked[...] = jnp.zeros(picked.shape, F32)
        look(0)

        @pl.when(is_ocean)
        def _():
            for a in range(1, ocean):
                look(a)

        terms = picked[...] * weight[...]
        sums = [jnp.sum(terms[b * rk : (b + 1) * rk], axis=0, keepdims=True) for b in range(blocks + 2)]
        sums[blocks] = jnp.where(row_lane < LANES // 2, sums[blocks], sums[blocks + 1])
        return [
            sums[b] - field[levels - 1 : levels, b * LANES : (b + 1) * LANES] for b in range(blocks + 1)
        ]

    def coupling_step(p):
        product = mixed_spread()
        boundary = boundary_of(p)
        push = jnp.concatenate([gain[...] * row for row in boundary], axis=1)
        push = push + forcing[...]
        field[...] = jnp.where(live, product + push, field[...])
        drive[...] = push

        def substep(_, carry):
            field[...] = jnp.where(live, mixed_spread() + drive[...], field[...])
            return carry

        lax.fori_loop(0, SUBS - 2, substep, 0)
        xx, xh = spread_halves()

        @pl.when(p < STEPS - 1)
        def _():
            low = slice(levels - 8, levels)
            row = mm(mix_a[low, :], xx, NN) + mm(mix_b[low, :], xh, NN) + drive[low, :]
            row = jnp.where(live, row, field[low, :])
            surf[p + 1] = row[7:8, 0:columns]
            surf_each(p + 1, lambda copy: copy.start())

        product = mm(mix_a[...], xx, NN) + mm(mix_b[...], xh, NN)
        field[...] = jnp.where(live, product + drive[...], field[...])

    def column_copy(p, other, source):
        return pltpu.make_async_remote_copy(
            src_ref=chosen_out.at[p, other],
            dst_ref=chosen_in.at[p, source],
            send_sem=col_send.at[p],
            recv_sem=col_recv.at[p],
            device_id=(s, other),
            device_id_type=MESH,
        )

    def last_copy(sec, other, from_sec, from_tile):
        return pltpu.make_async_remote_copy(
            src_ref=chosen_out.at[STEPS - 1, other, 0:cap],
            dst_ref=cols_in.at[from_sec, from_tile, 0:cap],
            send_sem=last_send.at[0],
            recv_sem=last_recv.at[0],
            device_id=(sec, other),
            device_id_type=MESH,
        )

    own_columns = pltpu.make_async_copy(
        chosen_out.at[STEPS - 1, t, 0:cap], cols_in.at[s, t, 0:cap], last_recv.at[0]
    )

    def row_copy(sec, source):
        return pltpu.make_async_remote_copy(
            src_ref=rows_out.at[sec],
            dst_ref=rows_in.at[source],
            send_sem=row_send.at[0],
            recv_sem=row_recv.at[0],
            device_id=(sec, t),
            device_id_type=MESH,
        )

    own_rows = pltpu.make_async_copy(rows_out.at[s], rows_in.at[s], row_recv.at[0])

    def send_columns(p):
        pick = pick_v[p]
        fh, fl = split(field[:, 0:columns])
        taken = mm(pick, fh, NT) + mm(pick, fl, NT)
        projected = dot3(taken, refr_v[...]).reshape(tiles, 8, levels)
        chosen_out[p] = projected

        @pl.when(p < STEPS - 1)
        def _():
            over_tiles(lambda other: column_copy(p, other, t).start())
            pltpu.make_async_copy(chosen_out.at[p, t], chosen_in.at[p, t], col_recv.at[p]).start()

        @pl.when(p == STEPS - 1)
        def _():
            beyond(lambda sec, other: last_copy(sec, other, s, t).start())
            own_columns.start()

    own = parts_out.shape[2]

    def part_copy(p, other, source):
        return pltpu.make_async_remote_copy(
            src_ref=parts_out.at[p, other],
            dst_ref=parts_in.at[p, source],
            send_sem=red_send.at[p],
            recv_sem=red_recv.at[p],
            device_id=(other, t),
            device_id_type=MESH,
        )

    def others():
        return [lax.rem(s + d, sections) for d in range(1, sections)]

    def send_parts(p, w):
        drain(chosen_in.at[p], col_recv.at[p])
        part = dot3(w, chosen_in[p].reshape(rows, levels), TN)
        parts_out[p] = part.reshape(sections, own, levels)
        for other in others():
            part_copy(p, other, s).start()
        pltpu.make_async_copy(parts_out.at[p, s], parts_in.at[p, s], red_recv.at[p]).start()

    def list_columns(p, carry):
        pick_v[p] = selector(p)
        return carry

    lax.fori_loop(0, STEPS, list_columns, 0)

    for copy in packs:
        copy.wait_recv()
    gap = jnp.zeros((LANES - 2 * HALO, levels), F32)

    def pad(i):
        at = slice(i * HALO, (i + 1) * HALO)
        return jnp.concatenate([pack_in[0, at, :], gap, pack_in[1, at, :]], axis=0).T

    field[:, columns:ext] = pad(0)
    rates[:, columns:ext] = pad(1)
    forcing[:, columns:ext] = pad(2)
    for i in range(2):
        at = slice((blocks + i) * rk, (blocks + i + 1) * rk)
        position[at, :] = pack_in[i, 3 * HALO : 3 * HALO + rk, :].astype(jnp.int32)
        weight[at, :] = pack_in[i, 3 * HALO + rk : PACK, :]

    store = pltpu.make_async_copy(field.at[:, 0:columns], out_state.at[0], store_sem.at[0])

    def period(p, carry):
        coupling_step(p)

        @pl.when(p == STEPS - 1)
        def _():
            store.start()

        send_columns(p)
        return carry

    lax.fori_loop(0, STEPS, period, 0)

    def gather_parts(p, carry):
        send_parts(p, occultation_weights(p))
        drain(chosen_out.at[p, 0 : tiles - 1], col_send.at[p])
        return carry

    lax.fori_loop(0, STEPS - 1, gather_parts, 0)
    rows_out[...] = occultation_weights(STEPS - 1).T.reshape(rows_out.shape)
    for other in others():
        row_copy(other, s).start()
    own_rows.start()

    for copy in packs:
        copy.wait_send()
    for q in range(STEPS):
        surf_sent(q)
    store.wait()

    drain(spare, last_send.at[0])
    drain(rows_out.at[0 : sections - 1], row_send.at[0])
    for p in range(STEPS - 1):
        drain(parts_out.at[p, 0 : sections - 1], red_send.at[p])
        drain(parts_in.at[p], red_recv.at[p])
    drain(rows_in, row_recv.at[0])
    drain(cols_in.at[:, :, 0:cap], last_recv.at[0])


CHUNKS = 4


def departing(
    cap,
    state,
    parts,
    cols,
    weights,
    abel_matrix,
    observed,
    out_state,
    out_departures,
    state_v,
    parts_v,
    cols_v,
    weights_v,
    abel_v,
    obs_v,
    dep_v,
    sem,
):
    rows = state.shape[1] // CHUNKS
    loads = [
        pltpu.make_async_copy(cols, cols_v, sem.at[0]),
        pltpu.make_async_copy(weights, weights_v, sem.at[1]),
        pltpu.make_async_copy(parts, parts_v, sem.at[2]),
        pltpu.make_async_copy(abel_matrix, abel_v, sem.at[3]),
        pltpu.make_async_copy(observed, obs_v, sem.at[4]),
    ]
    bring, take = [], []
    for i in range(CHUNKS):
        at = pl.ds(i * rows, rows)
        bring.append(pltpu.make_async_copy(state.at[:, at], state_v.at[:, at], sem.at[5 + i]))
        take.append(pltpu.make_async_copy(state_v.at[:, at], out_state.at[:, at], sem.at[5 + CHUNKS + i]))
    for copy in loads + bring:
        copy.start()
    for i in range(CHUNKS):
        bring[i].wait()
        take[i].start()
    for copy in loads:
        copy.wait()
    sections, _, columns = weights_v.shape
    levels = cols_v.shape[3]
    sent = (lax.broadcasted_iota(jnp.int32, (columns, levels), 0) & 7) < cap
    totals = []
    for p in range(STEPS - 1):
        totals.append(parts_v[p, 0])
        for a in range(1, sections):
            totals[p] = totals[p] + parts_v[p, a]
    for a in range(sections):
        term = dot3(weights_v[a], jnp.where(sent, cols_v[a].reshape(columns, levels), 0.0))
        totals.append(term) if a == 0 else totals.append(totals.pop() + term)
    for p in range(STEPS):
        dep_v[p] = obs_v[p] - dot3(totals[p], abel_v[...])
    last = pltpu.make_async_copy(dep_v, out_departures, sem.at[5 + 2 * CHUNKS])
    last.start()
    for copy in take:
        copy.wait()
    last.wait()


def shards(sections, tiles, *args):
    (state, tendency, diffusion, mixing, coupling, remap_index, remap_weight, active_cols, send_cols) = args[:9]
    (occ_slot, occ_weight, occ_count, refraction, abel_matrix, observed) = args[9:]
    send_cols = jnp.swapaxes(send_cols, 3, 4)
    args = args[:8] + (send_cols,) + args[9:]
    levels, columns = state.shape[1:]
    rk = remap_index.shape[1]
    ext = columns + LANES
    slots = (columns // LANES + 2) * rk
    own = observed.shape[1]
    heights = abel_matrix.shape[1]
    dma = pltpu.SemaphoreType.DMA
    any_spec = pl.BlockSpec(memory_space=pltpu.HBM)
    smem = pl.BlockSpec(memory_space=pltpu.SMEM)
    args = args[:13]
    specs = [any_spec] * len(args)
    specs[7] = smem
    scratch = [
        pltpu.VMEM((levels, ext), F32),
        pltpu.VMEM((levels, ext), F32),
        pltpu.VMEM((levels, ext), F32),
        pltpu.VMEM((levels, ext), F32),
        pltpu.VMEM((levels, columns), BF16),
        pltpu.VMEM((levels, columns), BF16),
        pltpu.VMEM((levels, levels), F32),
        pltpu.VMEM(coupling.shape, F32),
        pltpu.VMEM((rk, columns), jnp.int32),
        pltpu.VMEM((rk, columns), F32),
        pltpu.VMEM(send_cols.shape, jnp.int32),
        pltpu.VMEM(occ_slot.shape, jnp.int32),
        pltpu.VMEM(occ_weight.shape, F32),
        pltpu.VMEM(occ_count.shape, jnp.int32),
        pltpu.VMEM((levels, levels), F32),
        pltpu.VMEM((levels, 2 * levels), BF16),
        pltpu.VMEM((levels, levels), BF16),
        pltpu.VMEM((STEPS, tiles * 8, columns), BF16),
        pltpu.VMEM((levels, LANES), F32),
        pltpu.VMEM((slots, LANES), jnp.int32),
        pltpu.VMEM((slots, LANES), F32),
        pltpu.VMEM((slots, LANES), F32),
        pltpu.VMEM((STEPS, 1, columns), F32),
        pltpu.VMEM((STEPS, 3, sections - 1, 1, columns), F32),
        pltpu.VMEM((2, PACK, LANES), F32),
        pltpu.VMEM((2, PACK, LANES), F32),
        pltpu.VMEM((STEPS, tiles, 8, levels), F32),
        pltpu.VMEM((STEPS, tiles, 8, levels), F32),
        pltpu.VMEM((STEPS - 1, sections, own, levels), F32),
        pltpu.VMEM((sections, own, tiles * 8), F32),
        pltpu.VMEM((sections * tiles - 1, send_cols.shape[3], levels), F32),
        dma((12,)),
        dma((1,)),
        dma((2,)),
        dma((2,)),
        dma((STEPS, sections - 1)),
        dma((STEPS, sections - 1)),
        dma((STEPS,)),
        dma((STEPS,)),
        dma((STEPS,)),
        dma((STEPS,)),
        dma((1,)),
        dma((1,)),
        dma((1,)),
        dma((1,)),
    ]
    middle, parts, cols, weights = pl.pallas_call(
        functools.partial(kernel, sections, tiles),
        out_shape=(
            jax.ShapeDtypeStruct(state.shape, F32),
            jax.ShapeDtypeStruct((STEPS - 1, sections, own, levels), F32),
            jax.ShapeDtypeStruct((sections, tiles, 8, levels), F32),
            jax.ShapeDtypeStruct((sections, own, tiles * 8), F32),
        ),
        in_specs=specs,
        out_specs=(any_spec,) * 4,
        scratch_shapes=scratch,
        compiler_params=pltpu.CompilerParams(
            collective_id=0, has_side_effects=True, vmem_limit_bytes=64 * 1024 * 1024 - 64 * 1024
        ),
        cost_estimate=pl.CostEstimate(flops=700_000_000, bytes_accessed=1_500_000, transcendentals=0),
    )(*args)
    return pl.pallas_call(
        functools.partial(departing, send_cols.shape[3]),
        out_shape=(jax.ShapeDtypeStruct(state.shape, F32), jax.ShapeDtypeStruct((STEPS, own, heights), F32)),
        in_specs=[any_spec] * 6,
        out_specs=(any_spec, any_spec),
        scratch_shapes=[
            pltpu.VMEM(state.shape, F32),
            pltpu.VMEM(parts.shape, F32),
            pltpu.VMEM(cols.shape, F32),
            pltpu.VMEM(weights.shape, F32),
            pltpu.VMEM(abel_matrix.shape, F32),
            pltpu.VMEM(observed.shape, F32),
            pltpu.VMEM(observed.shape, F32),
            dma((6 + 2 * CHUNKS,)),
        ],
        compiler_params=pltpu.CompilerParams(vmem_limit_bytes=64 * 1024 * 1024 - 64 * 1024),
        cost_estimate=pl.CostEstimate(flops=10_000_000, bytes_accessed=800_000, transcendentals=0),
    )(middle, parts, cols, weights, abel_matrix, observed)


def solution(mesh):
    return jax.shard_map(
        functools.partial(shards, mesh.shape["sec"], mesh.shape["tile"]),
        mesh=mesh,
        in_specs=(
            P("sec", None, "tile"),
            P("sec", None, "tile"),
            P("sec", None, "tile"),
            P("sec", None, None),
            P("sec", None),
            P("sec", None, "tile"),
            P("sec", None, "tile"),
            P(),
            P(None, "sec", "tile", None, None),
            P(None, "sec", None, "tile"),
            P(None, "sec", None, "tile"),
            P(None, "sec", "tile"),
            P("sec", None, None),
            P(),
            P(None, ("sec", "tile"), None),
        ),
        out_specs=(P("sec", None, "tile"), P(None, ("sec", "tile"), None)),
        check_vma=False,
    )
```

```python
import functools

import jax
import jax.numpy as jnp
from jax import lax
from jax.experimental import pallas as pl
from jax.experimental.pallas import tpu as pltpu
from jax.sharding import PartitionSpec as P

SUBS = 4
STEPS = 2
HALO = SUBS * STEPS
LANES = 128
PACK = 3 * HALO + 8
F32 = jnp.float32
BF16 = jnp.bfloat16
MESH = pl.DeviceIdType.MESH


def split(x):
    high = x.astype(BF16)
    low = (x - high.astype(F32)).astype(BF16)
    return high, low


def mm(a, b, dims):
    return lax.dot_general(a, b, (dims, ((), ())), preferred_element_type=F32)


NN = ((1,), (0,))
NT = ((1,), (1,))
TN = ((0,), (0,))


def dot3(a, b, dims=NN):
    ah, al = split(a)
    bh, bl = split(b)
    return mm(ah, bh, dims) + (mm(ah, bl, dims) + mm(al, bh, dims))


def kernel(
    sections,
    tiles,
    state,
    tendency,
    diffusion,
    mixing,
    coupling,
    remap_index,
    remap_weight,
    active_cols,
    send_cols,
    occ_slot,
    occ_weight,
    occ_count,
    refraction,
    out_state,
    parts_in,
    cols_in,
    rows_in,
    field,
    rates,
    forcing,
    drive,
    tend_v,
    diff_v,
    mix_v,
    coup_v,
    ridx_v,
    rw_v,
    cols_v,
    slot_v,
    ow_v,
    oc_v,
    refr_v,
    mix,
    pick_v,
    gain,
    position,
    weight,
    picked,
    surf,
    tab,
    pack_out,
    pack_in,
    chosen_out,
    chosen_in,
    parts_out,
    rows_out,
    spare,
    load_sem,
    store_sem,
    pack_send,
    pack_recv,
    surf_send,
    surf_recv,
    col_send,
    col_recv,
    red_send,
    red_recv,
    last_send,
    last_recv,
    row_send,
    row_recv,
):
    levels, columns = tend_v.shape
    ext = field.shape[1]
    blocks = columns // LANES
    rk = ridx_v.shape[0]
    s = lax.axis_index("sec")
    t = lax.axis_index("tile")
    ocean = sections - 1
    is_ocean = s == ocean
    right = lax.rem(t + 1, tiles)
    left = lax.rem(t + tiles - 1, tiles)
    near = ((left, 1), (right, 2), (t, 0))

    loads = [
        (state.at[0], field.at[:, 0:columns]),
        (diffusion.at[0], diff_v),
        (tendency.at[0], tend_v),
        (remap_index.at[0], ridx_v),
        (remap_weight.at[0], rw_v),
        (mixing.at[0], mix_v),
        (coupling, coup_v),
        (send_cols, cols_v),
        (occ_slot, slot_v),
        (occ_weight, ow_v),
        (occ_count, oc_v),
        (refraction.at[0], refr_v),
    ]
    loads = [pltpu.make_async_copy(a, b, load_sem.at[i]) for i, (a, b) in enumerate(loads)]
    for load in loads[:5]:
        load.start()

    def drain(ref, sem):
        pltpu.make_async_copy(ref, ref, sem).wait()

    def over_tiles(body):
        if tiles <= 8:
            for d in range(1, tiles):
                body(lax.rem(t + d, tiles))
        else:
            lax.fori_loop(1, tiles, lambda d, c: (body(lax.rem(t + d, tiles)), c)[1], 0)

    barrier = pltpu.get_barrier_semaphore()

    def greet(sec, tile):
        pl.semaphore_signal(barrier, inc=1, device_id=(sec, tile), device_id_type=MESH)

    def beyond(body):
        for q in range(sections):
            over_tiles(lambda other: body(lax.rem(s + q, sections), other))
        for d in range(1, sections):
            body(lax.rem(s + d, sections), t)

    beyond(greet)

    for load in loads[5:]:
        load.start()

    lane = lax.broadcasted_iota(jnp.int32, (levels, LANES), 1)
    row_lane = lax.broadcasted_iota(jnp.int32, (1, LANES), 1)

    for load in loads[:5]:
        load.wait()
    surf[0] = field[levels - 1 : levels, 0:columns]

    tail = columns - LANES
    idx_f = ridx_v[...].astype(F32)

    def pack(slot, lo, shift):
        a = field[:, lo : lo + LANES]
        b = diff_v[:, lo : lo + LANES].astype(F32)
        c = tend_v[:, lo : lo + LANES].astype(F32)
        if shift:
            a = pltpu.roll(a, shift, 1)
        b = pltpu.roll(b, shift + HALO, 1)
        c = pltpu.roll(c, shift + 2 * HALO, 1)
        mixed = jnp.where(lane < HALO, a, jnp.where(lane < 2 * HALO, b, c))
        pack_out[slot, 0 : 3 * HALO, :] = mixed.T[0 : 3 * HALO]
        pack_out[slot, 3 * HALO : 3 * HALO + rk, :] = idx_f[:, lo : lo + LANES]
        pack_out[slot, 3 * HALO + rk : PACK, :] = rw_v[:, lo : lo + LANES]

    pack(0, 0, 0)
    pack(1, tail, HALO)

    pl.semaphore_wait(barrier, sections * tiles - 1)

    def pack_copy(slot, tile):
        return pltpu.make_async_remote_copy(
            src_ref=pack_out.at[slot],
            dst_ref=pack_in.at[slot],
            send_sem=pack_send.at[slot],
            recv_sem=pack_recv.at[slot],
            device_id=(s, tile),
            device_id_type=MESH,
        )

    def surf_copy(p, d, a, sec, tile, mark):
        return pltpu.make_async_remote_copy(
            src_ref=surf.at[p],
            dst_ref=tab.at[p, d, a],
            send_sem=surf_send.at[p, mark],
            recv_sem=surf_recv.at[p, a],
            device_id=(sec, tile),
            device_id_type=MESH,
        )

    def surf_sent(p):
        @pl.when(is_ocean)
        def _():
            for a in range(ocean):
                drain(tab.at[p, :, a], surf_send.at[p, a])

        @pl.when(jnp.logical_not(is_ocean))
        def _():
            drain(tab.at[p, :, 0], surf_send.at[p, 0])

    def surf_each(p, act):
        @pl.when(is_ocean)
        def _():
            for tile, d in near:
                for a in range(ocean):
                    act(surf_copy(p, d, 0, a, tile, a))

        @pl.when(jnp.logical_not(is_ocean))
        def _():
            for tile, d in near:
                act(surf_copy(p, d, s, ocean, tile, 0))

    packs = (pack_copy(0, left), pack_copy(1, right))
    for copy in packs:
        copy.start()
    surf_each(0, lambda copy: copy.start())

    for load in loads[5:]:
        load.wait()
    mh, ml = split(mix_v[...])
    mix[0:levels, 0:levels] = mh
    mix[0:levels, levels : 2 * levels] = mh
    mix[levels : 2 * levels, 0:levels] = ml
    mix[levels : 2 * levels, levels : 2 * levels] = jnp.zeros_like(ml)
    gain[...] = jnp.broadcast_to(coup_v[...], (LANES, levels)).T
    rates[:, 0:columns] = diff_v[...].astype(F32)
    forcing[:, 0:columns] = tend_v[...].astype(F32)
    for b in range(blocks):
        position[b * rk : (b + 1) * rk, :] = ridx_v[:, b * LANES : (b + 1) * LANES]
        weight[b * rk : (b + 1) * rk, :] = rw_v[:, b * LANES : (b + 1) * LANES]

    limit = active_cols[s]
    number = lax.broadcasted_iota(jnp.int32, (1, ext), 1)
    number = jnp.where(
        number < columns, number, jnp.where(number < columns + LANES // 2, number - columns, number - LANES)
    )
    live = number < limit

    cap = cols_v.shape[3]
    rows = tiles * 8

    def selector(p):
        which = lax.broadcasted_iota(jnp.int32, (rows, tiles), 0)
        owner = lax.broadcasted_iota(jnp.int32, (rows, tiles), 1)
        expand = jnp.where(lax.shift_right_logical(which, 3) == owner, 1.0, 0.0)
        listed = lax.dot_general(
            expand,
            cols_v[p, 0, 0].astype(F32),
            (NT, ((), ())),
            precision=lax.Precision.HIGHEST,
            preferred_element_type=F32,
        )
        r = lax.broadcasted_iota(jnp.int32, (rows, cap), 0)
        c = lax.broadcasted_iota(jnp.int32, (rows, cap), 1)
        column = jnp.sum(jnp.where((r & 7) == c, listed, 0.0), axis=1, keepdims=True)
        rr = lax.broadcasted_iota(jnp.int32, (rows, columns), 0)
        cc = lax.broadcasted_iota(jnp.int32, (rows, columns), 1)
        hit = jnp.logical_and(cc == column.astype(jnp.int32), (rr & 7) < cap)
        return jnp.where(hit, 1.0, 0.0).astype(BF16)

    def occultation_weights(p):
        shape = (rows, slot_v.shape[3])
        m = lax.broadcasted_iota(jnp.int32, shape, 0)
        key = jnp.where((m & 7) < cap, lax.shift_right_logical(m, 3) * cap + (m & 7), -1)
        counts = oc_v[p]
        total = jnp.zeros(shape, F32)
        for k in range(slot_v.shape[2]):
            w = jnp.where(counts > k, ow_v[p, 0, k : k + 1, :], 0.0)
            total = total + jnp.where(key == slot_v[p, 0, k : k + 1, :], w, 0.0)
        return total

    def spread_halves():
        f = field[...]
        around = pltpu.roll(f, 1, 1) + pltpu.roll(f, ext - 1, 1)
        spread = f + rates[...] * (around - 2.0 * f)
        xh, xl = split(spread)
        return jnp.concatenate([xh, xl], axis=0)

    def mixed(halves):
        both = mm(mix[...], halves, NN)
        return both[0:levels] + both[levels : 2 * levels]

    def mixed_spread():
        return mixed(spread_halves())

    def boundary_of(p):
        pos = position[...]
        inner = pos & (LANES - 1)
        outer = lax.shift_right_logical(pos, 7)

        def look(a):
            drain(tab.at[p, :, a], surf_recv.at[p, a])
            found = picked[...]
            for b in range(blocks):
                at = slice(b * LANES, (b + 1) * LANES)
                table = jnp.concatenate(
                    [
                        jnp.broadcast_to(tab[p, 0, a, :, at], (blocks * rk, LANES)),
                        jnp.broadcast_to(tab[p, 1, a, :, at], (rk, LANES)),
                        jnp.broadcast_to(tab[p, 2, a, :, at], (rk, LANES)),
                    ],
                    axis=0,
                )
                got = jnp.take_along_axis(table, inner, axis=1, mode="promise_in_bounds")
                found = jnp.where(outer == a * blocks + b, got, found)
            picked[...] = found

        picked[...] = jnp.zeros(picked.shape, F32)
        look(0)

        @pl.when(is_ocean)
        def _():
            for a in range(1, ocean):
                look(a)

        terms = picked[...] * weight[...]
        sums = [jnp.sum(terms[b * rk : (b + 1) * rk], axis=0, keepdims=True) for b in range(blocks + 2)]
        sums[blocks] = jnp.where(row_lane < LANES // 2, sums[blocks], sums[blocks + 1])
        return [
            sums[b] - field[levels - 1 : levels, b * LANES : (b + 1) * LANES] for b in range(blocks + 1)
        ]

    def coupling_step(p):
        product = mixed_spread()
        boundary = boundary_of(p)
        push = jnp.concatenate([gain[...] * row for row in boundary], axis=1)
        push = push + forcing[...]
        field[...] = jnp.where(live, product + push, field[...])
        drive[...] = push

        def substep(_, carry):
            field[...] = jnp.where(live, mixed_spread() + drive[...], field[...])
            return carry

        lax.fori_loop(0, SUBS - 2, substep, 0)
        halves = spread_halves()

        @pl.when(p < STEPS - 1)
        def _():
            low = slice(levels - 8, levels)
            ends = jnp.concatenate([mix[levels - 16 : levels, :], mix[2 * levels - 16 : 2 * levels, :]], axis=0)
            both = mm(ends, halves, NN)
            row = both[8:16] + both[24:32] + drive[low, :]
            row = jnp.where(live, row, field[low, :])
            surf[p + 1] = row[7:8, 0:columns]
            surf_each(p + 1, lambda copy: copy.start())

        product = mixed(halves)
        field[...] = jnp.where(live, product + drive[...], field[...])

    def column_copy(p, other, source):
        return pltpu.make_async_remote_copy(
            src_ref=chosen_out.at[p, other],
            dst_ref=chosen_in.at[p, source],
            send_sem=col_send.at[p],
            recv_sem=col_recv.at[p],
            device_id=(s, other),
            device_id_type=MESH,
        )

    def last_copy(sec, other, from_sec, from_tile):
        return pltpu.make_async_remote_copy(
            src_ref=chosen_out.at[STEPS - 1, other, 0:cap],
            dst_ref=cols_in.at[from_sec, from_tile, 0:cap],
            send_sem=last_send.at[0],
            recv_sem=last_recv.at[0],
            device_id=(sec, other),
            device_id_type=MESH,
        )

    own_columns = pltpu.make_async_copy(
        chosen_out.at[STEPS - 1, t, 0:cap], cols_in.at[s, t, 0:cap], last_recv.at[0]
    )

    def row_copy(sec, source):
        return pltpu.make_async_remote_copy(
            src_ref=rows_out.at[sec],
            dst_ref=rows_in.at[source],
            send_sem=row_send.at[0],
            recv_sem=row_recv.at[0],
            device_id=(sec, t),
            device_id_type=MESH,
        )

    own_rows = pltpu.make_async_copy(rows_out.at[s], rows_in.at[s], row_recv.at[0])

    def send_columns(p):
        pick = pick_v[p]
        fh, fl = split(field[:, 0:columns])
        taken = mm(pick, fh, NT) + mm(pick, fl, NT)
        projected = dot3(taken, refr_v[...]).reshape(tiles, 8, levels)
        chosen_out[p] = projected

        @pl.when(p < STEPS - 1)
        def _():
            over_tiles(lambda other: column_copy(p, other, t).start())
            pltpu.make_async_copy(chosen_out.at[p, t], chosen_in.at[p, t], col_recv.at[p]).start()

        @pl.when(p == STEPS - 1)
        def _():
            beyond(lambda sec, other: last_copy(sec, other, s, t).start())
            own_columns.start()

    own = parts_out.shape[2]

    def part_copy(p, other, source):
        return pltpu.make_async_remote_copy(
            src_ref=parts_out.at[p, other],
            dst_ref=parts_in.at[p, source],
            send_sem=red_send.at[p],
            recv_sem=red_recv.at[p],
            device_id=(other, t),
            device_id_type=MESH,
        )

    def others():
        return [lax.rem(s + d, sections) for d in range(1, sections)]

    def send_parts(p, w):
        drain(chosen_in.at[p], col_recv.at[p])
        part = dot3(w, chosen_in[p].reshape(rows, levels), TN)
        parts_out[p] = part.reshape(sections, own, levels)
        for other in others():
            part_copy(p, other, s).start()
        pltpu.make_async_copy(parts_out.at[p, s], parts_in.at[p, s], red_recv.at[p]).start()

    def list_columns(p, carry):
        pick_v[p] = selector(p)
        return carry

    lax.fori_loop(0, STEPS, list_columns, 0)

    for copy in packs:
        copy.wait_recv()
    gap = jnp.zeros((LANES - 2 * HALO, levels), F32)

    def pad(i):
        at = slice(i * HALO, (i + 1) * HALO)
        return jnp.concatenate([pack_in[0, at, :], gap, pack_in[1, at, :]], axis=0).T

    field[:, columns:ext] = pad(0)
    rates[:, columns:ext] = pad(1)
    forcing[:, columns:ext] = pad(2)
    for i in range(2):
        at = slice((blocks + i) * rk, (blocks + i + 1) * rk)
        position[at, :] = pack_in[i, 3 * HALO : 3 * HALO + rk, :].astype(jnp.int32)
        weight[at, :] = pack_in[i, 3 * HALO + rk : PACK, :]

    store = pltpu.make_async_copy(field.at[:, 0:columns], out_state.at[0], store_sem.at[0])

    def period(p, carry):
        coupling_step(p)

        @pl.when(p == STEPS - 1)
        def _():
            store.start()

        send_columns(p)
        return carry

    lax.fori_loop(0, STEPS, period, 0)

    def gather_parts(p, carry):
        send_parts(p, occultation_weights(p))
        drain(chosen_out.at[p, 0 : tiles - 1], col_send.at[p])
        return carry

    lax.fori_loop(0, STEPS - 1, gather_parts, 0)
    rows_out[...] = occultation_weights(STEPS - 1).T.reshape(rows_out.shape)
    for other in others():
        row_copy(other, s).start()
    own_rows.start()

    for copy in packs:
        copy.wait_send()
    for q in range(STEPS):
        surf_sent(q)
    store.wait()

    drain(spare, last_send.at[0])
    drain(rows_out.at[0 : sections - 1], row_send.at[0])
    for p in range(STEPS - 1):
        drain(parts_out.at[p, 0 : sections - 1], red_send.at[p])
        drain(parts_in.at[p], red_recv.at[p])
    drain(rows_in, row_recv.at[0])
    drain(cols_in.at[:, :, 0:cap], last_recv.at[0])


CHUNKS = 4


def departing(
    cap,
    state,
    parts,
    cols,
    weights,
    abel_matrix,
    observed,
    out_state,
    out_departures,
    state_v,
    parts_v,
    cols_v,
    weights_v,
    abel_v,
    obs_v,
    dep_v,
    sem,
):
    rows = state.shape[1] // CHUNKS
    loads = [
        pltpu.make_async_copy(cols, cols_v, sem.at[0]),
        pltpu.make_async_copy(weights, weights_v, sem.at[1]),
        pltpu.make_async_copy(parts, parts_v, sem.at[2]),
        pltpu.make_async_copy(abel_matrix, abel_v, sem.at[3]),
        pltpu.make_async_copy(observed, obs_v, sem.at[4]),
    ]
    bring, take = [], []
    for i in range(CHUNKS):
        at = pl.ds(i * rows, rows)
        bring.append(pltpu.make_async_copy(state.at[:, at], state_v.at[:, at], sem.at[5 + i]))
        take.append(pltpu.make_async_copy(state_v.at[:, at], out_state.at[:, at], sem.at[5 + CHUNKS + i]))
    for copy in loads + bring:
        copy.start()
    for i in range(CHUNKS):
        bring[i].wait()
        take[i].start()
    for copy in loads:
        copy.wait()
    sections, _, columns = weights_v.shape
    levels = cols_v.shape[3]
    sent = (lax.broadcasted_iota(jnp.int32, (columns, levels), 0) & 7) < cap
    totals = []
    for p in range(STEPS - 1):
        totals.append(parts_v[p, 0])
        for a in range(1, sections):
            totals[p] = totals[p] + parts_v[p, a]
    for a in range(sections):
        term = dot3(weights_v[a], jnp.where(sent, cols_v[a].reshape(columns, levels), 0.0))
        totals.append(term) if a == 0 else totals.append(totals.pop() + term)
    for p in range(STEPS):
        dep_v[p] = obs_v[p] - dot3(totals[p], abel_v[...])
    last = pltpu.make_async_copy(dep_v, out_departures, sem.at[5 + 2 * CHUNKS])
    last.start()
    for copy in take:
        copy.wait()
    last.wait()


def shards(sections, tiles, *args):
    (state, tendency, diffusion, mixing, coupling, remap_index, remap_weight, active_cols, send_cols) = args[:9]
    (occ_slot, occ_weight, occ_count, refraction, abel_matrix, observed) = args[9:]
    send_cols = jnp.swapaxes(send_cols, 3, 4)
    args = args[:8] + (send_cols,) + args[9:]
    levels, columns = state.shape[1:]
    rk = remap_index.shape[1]
    ext = columns + LANES
    slots = (columns // LANES + 2) * rk
    own = observed.shape[1]
    heights = abel_matrix.shape[1]
    dma = pltpu.SemaphoreType.DMA
    any_spec = pl.BlockSpec(memory_space=pltpu.HBM)
    smem = pl.BlockSpec(memory_space=pltpu.SMEM)
    args = args[:13]
    specs = [any_spec] * len(args)
    specs[7] = smem
    scratch = [
        pltpu.VMEM((levels, ext), F32),
        pltpu.VMEM((levels, ext), F32),
        pltpu.VMEM((levels, ext), F32),
        pltpu.VMEM((levels, ext), F32),
        pltpu.VMEM((levels, columns), BF16),
        pltpu.VMEM((levels, columns), BF16),
        pltpu.VMEM((levels, levels), F32),
        pltpu.VMEM(coupling.shape, F32),
        pltpu.VMEM((rk, columns), jnp.int32),
        pltpu.VMEM((rk, columns), F32),
        pltpu.VMEM(send_cols.shape, jnp.int32),
        pltpu.VMEM(occ_slot.shape, jnp.int32),
        pltpu.VMEM(occ_weight.shape, F32),
        pltpu.VMEM(occ_count.shape, jnp.int32),
        pltpu.VMEM((levels, levels), F32),
        pltpu.VMEM((2 * levels, 2 * levels), BF16),
        pltpu.VMEM((STEPS, tiles * 8, columns), BF16),
        pltpu.VMEM((levels, LANES), F32),
        pltpu.VMEM((slots, LANES), jnp.int32),
        pltpu.VMEM((slots, LANES), F32),
        pltpu.VMEM((slots, LANES), F32),
        pltpu.VMEM((STEPS, 1, columns), F32),
        pltpu.VMEM((STEPS, 3, sections - 1, 1, columns), F32),
        pltpu.VMEM((2, PACK, LANES), F32),
        pltpu.VMEM((2, PACK, LANES), F32),
        pltpu.VMEM((STEPS, tiles, 8, levels), F32),
        pltpu.VMEM((STEPS, tiles, 8, levels), F32),
        pltpu.VMEM((STEPS - 1, sections, own, levels), F32),
        pltpu.VMEM((sections, own, tiles * 8), F32),
        pltpu.VMEM((sections * tiles - 1, send_cols.shape[3], levels), F32),
        dma((12,)),
        dma((1,)),
        dma((2,)),
        dma((2,)),
        dma((STEPS, sections - 1)),
        dma((STEPS, sections - 1)),
        dma((STEPS,)),
        dma((STEPS,)),
        dma((STEPS,)),
        dma((STEPS,)),
        dma((1,)),
        dma((1,)),
        dma((1,)),
        dma((1,)),
    ]
    middle, parts, cols, weights = pl.pallas_call(
        functools.partial(kernel, sections, tiles),
        out_shape=(
            jax.ShapeDtypeStruct(state.shape, F32),
            jax.ShapeDtypeStruct((STEPS - 1, sections, own, levels), F32),
            jax.ShapeDtypeStruct((sections, tiles, 8, levels), F32),
            jax.ShapeDtypeStruct((sections, own, tiles * 8), F32),
        ),
        in_specs=specs,
        out_specs=(any_spec,) * 4,
        scratch_shapes=scratch,
        compiler_params=pltpu.CompilerParams(
            collective_id=0, has_side_effects=True, vmem_limit_bytes=64 * 1024 * 1024 - 64 * 1024
        ),
        cost_estimate=pl.CostEstimate(flops=700_000_000, bytes_accessed=1_500_000, transcendentals=0),
    )(*args)
    return pl.pallas_call(
        functools.partial(departing, send_cols.shape[3]),
        out_shape=(jax.ShapeDtypeStruct(state.shape, F32), jax.ShapeDtypeStruct((STEPS, own, heights), F32)),
        in_specs=[any_spec] * 6,
        out_specs=(any_spec, any_spec),
        scratch_shapes=[
            pltpu.VMEM(state.shape, F32),
            pltpu.VMEM(parts.shape, F32),
            pltpu.VMEM(cols.shape, F32),
            pltpu.VMEM(weights.shape, F32),
            pltpu.VMEM(abel_matrix.shape, F32),
            pltpu.VMEM(observed.shape, F32),
            pltpu.VMEM(observed.shape, F32),
            dma((6 + 2 * CHUNKS,)),
        ],
        compiler_params=pltpu.CompilerParams(vmem_limit_bytes=64 * 1024 * 1024 - 64 * 1024),
        cost_estimate=pl.CostEstimate(flops=10_000_000, bytes_accessed=800_000, transcendentals=0),
    )(middle, parts, cols, weights, abel_matrix, observed)


def solution(mesh):
    return jax.shard_map(
        functools.partial(shards, mesh.shape["sec"], mesh.shape["tile"]),
        mesh=mesh,
        in_specs=(
            P("sec", None, "tile"),
            P("sec", None, "tile"),
            P("sec", None, "tile"),
            P("sec", None, None),
            P("sec", None),
            P("sec", None, "tile"),
            P("sec", None, "tile"),
            P(),
            P(None, "sec", "tile", None, None),
            P(None, "sec", None, "tile"),
            P(None, "sec", None, "tile"),
            P(None, "sec", "tile"),
            P("sec", None, None),
            P(),
            P(None, ("sec", "tile"), None),
        ),
        out_specs=(P("sec", None, "tile"), P(None, ("sec", "tile"), None)),
        check_vma=False,
    )
```

```python
import functools

import jax
import jax.numpy as jnp
from jax import lax
from jax.experimental import pallas as pl
from jax.experimental.pallas import tpu as pltpu
from jax.sharding import PartitionSpec as P

SUBS = 4
STEPS = 2
HALO = SUBS * STEPS
LANES = 128
PACK = 3 * HALO + 8
F32 = jnp.float32
BF16 = jnp.bfloat16
MESH = pl.DeviceIdType.MESH


def split(x):
    high = x.astype(BF16)
    low = (x - high.astype(F32)).astype(BF16)
    return high, low


def mm(a, b, dims):
    return lax.dot_general(a, b, (dims, ((), ())), preferred_element_type=F32)


NN = ((1,), (0,))
NT = ((1,), (1,))
TN = ((0,), (0,))


def dot3(a, b, dims=NN):
    ah, al = split(a)
    bh, bl = split(b)
    return mm(ah, bh, dims) + (mm(ah, bl, dims) + mm(al, bh, dims))


def kernel(
    sections,
    tiles,
    state,
    tendency,
    diffusion,
    mixing,
    coupling,
    remap_index,
    remap_weight,
    active_cols,
    send_cols,
    occ_slot,
    occ_weight,
    occ_count,
    refraction,
    out_state,
    parts_in,
    cols_in,
    rows_in,
    field,
    rates,
    forcing,
    drive,
    tend_v,
    diff_v,
    mix_v,
    coup_v,
    ridx_v,
    rw_v,
    cols_v,
    slot_v,
    ow_v,
    oc_v,
    refr_v,
    mix,
    pick_v,
    gain,
    position,
    weight,
    picked,
    surf,
    tab,
    pack_out,
    pack_in,
    chosen_out,
    chosen_in,
    parts_out,
    rows_out,
    spare,
    load_sem,
    store_sem,
    pack_send,
    pack_recv,
    surf_send,
    surf_recv,
    col_send,
    col_recv,
    red_send,
    red_recv,
    last_send,
    last_recv,
    row_send,
    row_recv,
):
    levels, columns = tend_v.shape
    ext = field.shape[1]
    blocks = columns // LANES
    rk = ridx_v.shape[0]
    s = lax.axis_index("sec")
    t = lax.axis_index("tile")
    ocean = sections - 1
    is_ocean = s == ocean
    right = lax.rem(t + 1, tiles)
    left = lax.rem(t + tiles - 1, tiles)
    near = ((left, 1), (right, 2), (t, 0))

    loads = [
        (state.at[0], field.at[:, 0:columns]),
        (diffusion.at[0], diff_v),
        (tendency.at[0], tend_v),
        (remap_index.at[0], ridx_v),
        (remap_weight.at[0], rw_v),
        (mixing.at[0], mix_v),
        (coupling, coup_v),
        (send_cols, cols_v),
        (occ_slot, slot_v),
        (occ_weight, ow_v),
        (occ_count, oc_v),
        (refraction.at[0], refr_v),
    ]
    loads = [pltpu.make_async_copy(a, b, load_sem.at[i]) for i, (a, b) in enumerate(loads)]
    for load in loads[:5]:
        load.start()

    def drain(ref, sem):
        pltpu.make_async_copy(ref, ref, sem).wait()

    def over_tiles(body):
        if tiles <= 8:
            for d in range(1, tiles):
                body(lax.rem(t + d, tiles))
        else:
            lax.fori_loop(1, tiles, lambda d, c: (body(lax.rem(t + d, tiles)), c)[1], 0)

    barrier = pltpu.get_barrier_semaphore()

    def greet(sec, tile):
        pl.semaphore_signal(barrier, inc=1, device_id=(sec, tile), device_id_type=MESH)

    def beyond(body):
        for q in range(sections):
            over_tiles(lambda other: body(lax.rem(s + q, sections), other))
        for d in range(1, sections):
            body(lax.rem(s + d, sections), t)

    beyond(greet)

    for load in loads[5:]:
        load.start()

    lane = lax.broadcasted_iota(jnp.int32, (levels, LANES), 1)
    row_lane = lax.broadcasted_iota(jnp.int32, (1, LANES), 1)

    for load in loads[:5]:
        load.wait()
    surf[0] = field[levels - 1 : levels, 0:columns]

    tail = columns - LANES
    idx_f = ridx_v[...].astype(F32)

    def pack(slot, lo, shift):
        a = field[:, lo : lo + LANES]
        b = diff_v[:, lo : lo + LANES].astype(F32)
        c = tend_v[:, lo : lo + LANES].astype(F32)
        if shift:
            a = pltpu.roll(a, shift, 1)
        b = pltpu.roll(b, shift + HALO, 1)
        c = pltpu.roll(c, shift + 2 * HALO, 1)
        mixed = jnp.where(lane < HALO, a, jnp.where(lane < 2 * HALO, b, c))
        pack_out[slot, 0 : 3 * HALO, :] = mixed.T[0 : 3 * HALO]
        pack_out[slot, 3 * HALO : 3 * HALO + rk, :] = idx_f[:, lo : lo + LANES]
        pack_out[slot, 3 * HALO + rk : PACK, :] = rw_v[:, lo : lo + LANES]

    pack(0, 0, 0)
    pack(1, tail, HALO)

    pl.semaphore_wait(barrier, sections * tiles - 1)

    def pack_copy(slot, tile):
        return pltpu.make_async_remote_copy(
            src_ref=pack_out.at[slot],
            dst_ref=pack_in.at[slot],
            send_sem=pack_send.at[slot],
            recv_sem=pack_recv.at[slot],
            device_id=(s, tile),
            device_id_type=MESH,
        )

    def surf_copy(p, d, a, sec, tile, mark):
        return pltpu.make_async_remote_copy(
            src_ref=surf.at[p],
            dst_ref=tab.at[p, d, a],
            send_sem=surf_send.at[p, mark],
            recv_sem=surf_recv.at[p, a],
            device_id=(sec, tile),
            device_id_type=MESH,
        )

    def surf_sent(p):
        @pl.when(is_ocean)
        def _():
            for a in range(ocean):
                drain(tab.at[p, :, a], surf_send.at[p, a])

        @pl.when(jnp.logical_not(is_ocean))
        def _():
            drain(tab.at[p, :, 0], surf_send.at[p, 0])

    def surf_each(p, act):
        @pl.when(is_ocean)
        def _():
            for tile, d in near:
                for a in range(ocean):
                    act(surf_copy(p, d, 0, a, tile, a))

        @pl.when(jnp.logical_not(is_ocean))
        def _():
            for tile, d in near:
                act(surf_copy(p, d, s, ocean, tile, 0))

    packs = (pack_copy(0, left), pack_copy(1, right))
    for copy in packs:
        copy.start()
    surf_each(0, lambda copy: copy.start())

    for load in loads[5:]:
        load.wait()
    mh, ml = split(mix_v[...])
    mix[0:levels, 0:levels] = mh
    mix[0:levels, levels : 2 * levels] = mh
    mix[levels : 2 * levels, 0:levels] = ml
    mix[levels : 2 * levels, levels : 2 * levels] = jnp.zeros_like(ml)
    gain[...] = jnp.broadcast_to(coup_v[...], (LANES, levels)).T
    rates[:, 0:columns] = diff_v[...].astype(F32)
    forcing[:, 0:columns] = tend_v[...].astype(F32)
    for b in range(blocks):
        position[b * rk : (b + 1) * rk, :] = ridx_v[:, b * LANES : (b + 1) * LANES]
        weight[b * rk : (b + 1) * rk, :] = rw_v[:, b * LANES : (b + 1) * LANES]

    limit = active_cols[s]
    number = lax.broadcasted_iota(jnp.int32, (1, ext), 1)
    number = jnp.where(
        number < columns, number, jnp.where(number < columns + LANES // 2, number - columns, number - LANES)
    )
    live = number < limit

    cap = cols_v.shape[3]
    rows = tiles * 8

    def selector(p):
        which = lax.broadcasted_iota(jnp.int32, (rows, tiles), 0)
        owner = lax.broadcasted_iota(jnp.int32, (rows, tiles), 1)
        expand = jnp.where(lax.shift_right_logical(which, 3) == owner, 1.0, 0.0).astype(BF16)
        high, low = split(cols_v[p, 0, 0].astype(F32))
        listed = mm(expand, high, NT) + mm(expand, low, NT)
        r = lax.broadcasted_iota(jnp.int32, (rows, cap), 0)
        c = lax.broadcasted_iota(jnp.int32, (rows, cap), 1)
        column = jnp.sum(jnp.where((r & 7) == c, listed, 0.0), axis=1, keepdims=True)
        rr = lax.broadcasted_iota(jnp.int32, (rows, columns), 0)
        cc = lax.broadcasted_iota(jnp.int32, (rows, columns), 1)
        hit = jnp.logical_and(cc == column.astype(jnp.int32), (rr & 7) < cap)
        return jnp.where(hit, 1.0, 0.0).astype(BF16)

    def occultation_weights(p):
        shape = (rows, slot_v.shape[3])
        m = lax.broadcasted_iota(jnp.int32, shape, 0)
        key = jnp.where((m & 7) < cap, lax.shift_right_logical(m, 3) * cap + (m & 7), -1)
        counts = oc_v[p]
        total = jnp.zeros(shape, F32)
        for k in range(slot_v.shape[2]):
            w = jnp.where(counts > k, ow_v[p, 0, k : k + 1, :], 0.0)
            total = total + jnp.where(key == slot_v[p, 0, k : k + 1, :], w, 0.0)
        return total

    def spread_halves():
        f = field[...]
        around = pltpu.roll(f, 1, 1) + pltpu.roll(f, ext - 1, 1)
        spread = f + rates[...] * (around - 2.0 * f)
        xh, xl = split(spread)
        return jnp.concatenate([xh, xl], axis=0)

    def mixed(halves):
        both = mm(mix[...], halves, NN)
        return both[0:levels] + both[levels : 2 * levels]

    def mixed_spread():
        return mixed(spread_halves())

    def boundary_of(p):
        pos = position[...]
        inner = pos & (LANES - 1)
        outer = lax.shift_right_logical(pos, 7)

        def look(a):
            drain(tab.at[p, :, a], surf_recv.at[p, a])
            found = picked[...]
            for b in range(blocks):
                at = slice(b * LANES, (b + 1) * LANES)
                table = jnp.concatenate(
                    [
                        jnp.broadcast_to(tab[p, 0, a, :, at], (blocks * rk, LANES)),
                        jnp.broadcast_to(tab[p, 1, a, :, at], (rk, LANES)),
                        jnp.broadcast_to(tab[p, 2, a, :, at], (rk, LANES)),
                    ],
                    axis=0,
                )
                got = jnp.take_along_axis(table, inner, axis=1, mode="promise_in_bounds")
                found = jnp.where(outer == a * blocks + b, got, found)
            picked[...] = found

        picked[...] = jnp.zeros(picked.shape, F32)
        look(0)

        @pl.when(is_ocean)
        def _():
            for a in range(1, ocean):
                look(a)

        terms = picked[...] * weight[...]
        sums = [jnp.sum(terms[b * rk : (b + 1) * rk], axis=0, keepdims=True) for b in range(blocks + 2)]
        sums[blocks] = jnp.where(row_lane < LANES // 2, sums[blocks], sums[blocks + 1])
        return [
            sums[b] - field[levels - 1 : levels, b * LANES : (b + 1) * LANES] for b in range(blocks + 1)
        ]

    def coupling_step(p):
        product = mixed_spread()
        boundary = boundary_of(p)
        push = jnp.concatenate([gain[...] * row for row in boundary], axis=1)
        push = push + forcing[...]
        field[...] = jnp.where(live, product + push, field[...])
        drive[...] = push

        def substep(_, carry):
            field[...] = jnp.where(live, mixed_spread() + drive[...], field[...])
            return carry

        lax.fori_loop(0, SUBS - 2, substep, 0)
        halves = spread_halves()

        @pl.when(p < STEPS - 1)
        def _():
            low = slice(levels - 8, levels)
            ends = jnp.concatenate([mix[levels - 16 : levels, :], mix[2 * levels - 16 : 2 * levels, :]], axis=0)
            both = mm(ends, halves, NN)
            row = both[8:16] + both[24:32] + drive[low, :]
            row = jnp.where(live, row, field[low, :])
            surf[p + 1] = row[7:8, 0:columns]
            surf_each(p + 1, lambda copy: copy.start())

        product = mixed(halves)
        field[...] = jnp.where(live, product + drive[...], field[...])

    def column_copy(p, other, source):
        return pltpu.make_async_remote_copy(
            src_ref=chosen_out.at[p, other],
            dst_ref=chosen_in.at[p, source],
            send_sem=col_send.at[p],
            recv_sem=col_recv.at[p],
            device_id=(s, other),
            device_id_type=MESH,
        )

    def last_copy(sec, other, from_sec, from_tile):
        return pltpu.make_async_remote_copy(
            src_ref=chosen_out.at[STEPS - 1, other, 0:cap],
            dst_ref=cols_in.at[from_sec, from_tile, 0:cap],
            send_sem=last_send.at[0],
            recv_sem=last_recv.at[0],
            device_id=(sec, other),
            device_id_type=MESH,
        )

    own_columns = pltpu.make_async_copy(
        chosen_out.at[STEPS - 1, t, 0:cap], cols_in.at[s, t, 0:cap], last_recv.at[0]
    )

    def row_copy(sec, source):
        return pltpu.make_async_remote_copy(
            src_ref=rows_out.at[sec],
            dst_ref=rows_in.at[source],
            send_sem=row_send.at[0],
            recv_sem=row_recv.at[0],
            device_id=(sec, t),
            device_id_type=MESH,
        )

    own_rows = pltpu.make_async_copy(rows_out.at[s], rows_in.at[s], row_recv.at[0])

    def send_columns(p):
        pick = pick_v[p]
        fh, fl = split(field[:, 0:columns])
        taken = mm(pick, fh, NT) + mm(pick, fl, NT)
        projected = dot3(taken, refr_v[...]).reshape(tiles, 8, levels)
        chosen_out[p] = projected

        @pl.when(p < STEPS - 1)
        def _():
            over_tiles(lambda other: column_copy(p, other, t).start())
            pltpu.make_async_copy(chosen_out.at[p, t], chosen_in.at[p, t], col_recv.at[p]).start()

        @pl.when(p == STEPS - 1)
        def _():
            beyond(lambda sec, other: last_copy(sec, other, s, t).start())
            own_columns.start()

    own = parts_out.shape[2]

    def part_copy(p, other, source):
        return pltpu.make_async_remote_copy(
            src_ref=parts_out.at[p, other],
            dst_ref=parts_in.at[p, source],
            send_sem=red_send.at[p],
            recv_sem=red_recv.at[p],
            device_id=(other, t),
            device_id_type=MESH,
        )

    def others():
        return [lax.rem(s + d, sections) for d in range(1, sections)]

    def send_parts(p, w):
        drain(chosen_in.at[p], col_recv.at[p])
        part = dot3(w, chosen_in[p].reshape(rows, levels), TN)
        parts_out[p] = part.reshape(sections, own, levels)
        for other in others():
            part_copy(p, other, s).start()
        pltpu.make_async_copy(parts_out.at[p, s], parts_in.at[p, s], red_recv.at[p]).start()

    def list_columns(p, carry):
        pick_v[p] = selector(p)
        return carry

    lax.fori_loop(0, STEPS, list_columns, 0)

    for copy in packs:
        copy.wait_recv()
    gap = jnp.zeros((LANES - 2 * HALO, levels), F32)

    def pad(i):
        at = slice(i * HALO, (i + 1) * HALO)
        return jnp.concatenate([pack_in[0, at, :], gap, pack_in[1, at, :]], axis=0).T

    field[:, columns:ext] = pad(0)
    rates[:, columns:ext] = pad(1)
    forcing[:, columns:ext] = pad(2)
    for i in range(2):
        at = slice((blocks + i) * rk, (blocks + i + 1) * rk)
        position[at, :] = pack_in[i, 3 * HALO : 3 * HALO + rk, :].astype(jnp.int32)
        weight[at, :] = pack_in[i, 3 * HALO + rk : PACK, :]

    store = pltpu.make_async_copy(field.at[:, 0:columns], out_state.at[0], store_sem.at[0])

    def period(p, carry):
        coupling_step(p)

        @pl.when(p == STEPS - 1)
        def _():
            store.start()

        send_columns(p)
        return carry

    lax.fori_loop(0, STEPS, period, 0)

    def gather_parts(p, carry):
        send_parts(p, occultation_weights(p))
        drain(chosen_out.at[p, 0 : tiles - 1], col_send.at[p])
        return carry

    lax.fori_loop(0, STEPS - 1, gather_parts, 0)
    rows_out[...] = occultation_weights(STEPS - 1).T.reshape(rows_out.shape)
    for other in others():
        row_copy(other, s).start()
    own_rows.start()

    for copy in packs:
        copy.wait_send()
    for q in range(STEPS):
        surf_sent(q)
    store.wait()

    drain(spare, last_send.at[0])
    drain(rows_out.at[0 : sections - 1], row_send.at[0])
    for p in range(STEPS - 1):
        drain(parts_out.at[p, 0 : sections - 1], red_send.at[p])
        drain(parts_in.at[p], red_recv.at[p])
    drain(rows_in, row_recv.at[0])
    drain(cols_in.at[:, :, 0:cap], last_recv.at[0])


CHUNKS = 4


def departing(
    cap,
    state,
    parts,
    cols,
    weights,
    abel_matrix,
    observed,
    out_state,
    out_departures,
    state_v,
    parts_v,
    cols_v,
    weights_v,
    abel_v,
    obs_v,
    dep_v,
    sem,
):
    rows = state.shape[1] // CHUNKS
    loads = [
        pltpu.make_async_copy(cols, cols_v, sem.at[0]),
        pltpu.make_async_copy(weights, weights_v, sem.at[1]),
        pltpu.make_async_copy(parts, parts_v, sem.at[2]),
        pltpu.make_async_copy(abel_matrix, abel_v, sem.at[3]),
        pltpu.make_async_copy(observed, obs_v, sem.at[4]),
    ]
    bring, take = [], []
    for i in range(CHUNKS):
        at = pl.ds(i * rows, rows)
        bring.append(pltpu.make_async_copy(state.at[:, at], state_v.at[:, at], sem.at[5 + i]))
        take.append(pltpu.make_async_copy(state_v.at[:, at], out_state.at[:, at], sem.at[5 + CHUNKS + i]))
    for copy in loads + bring:
        copy.start()
    for i in range(CHUNKS):
        bring[i].wait()
        take[i].start()
    for copy in loads:
        copy.wait()
    sections, _, columns = weights_v.shape
    levels = cols_v.shape[3]
    sent = (lax.broadcasted_iota(jnp.int32, (columns, levels), 0) & 7) < cap
    totals = []
    for p in range(STEPS - 1):
        totals.append(parts_v[p, 0])
        for a in range(1, sections):
            totals[p] = totals[p] + parts_v[p, a]
    for a in range(sections):
        term = dot3(weights_v[a], jnp.where(sent, cols_v[a].reshape(columns, levels), 0.0))
        totals.append(term) if a == 0 else totals.append(totals.pop() + term)
    for p in range(STEPS):
        dep_v[p] = obs_v[p] - dot3(totals[p], abel_v[...])
    last = pltpu.make_async_copy(dep_v, out_departures, sem.at[5 + 2 * CHUNKS])
    last.start()
    for copy in take:
        copy.wait()
    last.wait()


def shards(sections, tiles, *args):
    (state, tendency, diffusion, mixing, coupling, remap_index, remap_weight, active_cols, send_cols) = args[:9]
    (occ_slot, occ_weight, occ_count, refraction, abel_matrix, observed) = args[9:]
    send_cols = jnp.swapaxes(send_cols, 3, 4)
    args = args[:8] + (send_cols,) + args[9:]
    levels, columns = state.shape[1:]
    rk = remap_index.shape[1]
    ext = columns + LANES
    slots = (columns // LANES + 2) * rk
    own = observed.shape[1]
    heights = abel_matrix.shape[1]
    dma = pltpu.SemaphoreType.DMA
    any_spec = pl.BlockSpec(memory_space=pltpu.HBM)
    smem = pl.BlockSpec(memory_space=pltpu.SMEM)
    args = args[:13]
    specs = [any_spec] * len(args)
    specs[7] = smem
    scratch = [
        pltpu.VMEM((levels, ext), F32),
        pltpu.VMEM((levels, ext), F32),
        pltpu.VMEM((levels, ext), F32),
        pltpu.VMEM((levels, ext), F32),
        pltpu.VMEM((levels, columns), BF16),
        pltpu.VMEM((levels, columns), BF16),
        pltpu.VMEM((levels, levels), F32),
        pltpu.VMEM(coupling.shape, F32),
        pltpu.VMEM((rk, columns), jnp.int32),
        pltpu.VMEM((rk, columns), F32),
        pltpu.VMEM(send_cols.shape, jnp.int32),
        pltpu.VMEM(occ_slot.shape, jnp.int32),
        pltpu.VMEM(occ_weight.shape, F32),
        pltpu.VMEM(occ_count.shape, jnp.int32),
        pltpu.VMEM((levels, levels), F32),
        pltpu.VMEM((2 * levels, 2 * levels), BF16),
        pltpu.VMEM((STEPS, tiles * 8, columns), BF16),
        pltpu.VMEM((levels, LANES), F32),
        pltpu.VMEM((slots, LANES), jnp.int32),
        pltpu.VMEM((slots, LANES), F32),
        pltpu.VMEM((slots, LANES), F32),
        pltpu.VMEM((STEPS, 1, columns), F32),
        pltpu.VMEM((STEPS, 3, sections - 1, 1, columns), F32),
        pltpu.VMEM((2, PACK, LANES), F32),
        pltpu.VMEM((2, PACK, LANES), F32),
        pltpu.VMEM((STEPS, tiles, 8, levels), F32),
        pltpu.VMEM((STEPS, tiles, 8, levels), F32),
        pltpu.VMEM((STEPS - 1, sections, own, levels), F32),
        pltpu.VMEM((sections, own, tiles * 8), F32),
        pltpu.VMEM((sections * tiles - 1, send_cols.shape[3], levels), F32),
        dma((12,)),
        dma((1,)),
        dma((2,)),
        dma((2,)),
        dma((STEPS, sections - 1)),
        dma((STEPS, sections - 1)),
        dma((STEPS,)),
        dma((STEPS,)),
        dma((STEPS,)),
        dma((STEPS,)),
        dma((1,)),
        dma((1,)),
        dma((1,)),
        dma((1,)),
    ]
    middle, parts, cols, weights = pl.pallas_call(
        functools.partial(kernel, sections, tiles),
        out_shape=(
            jax.ShapeDtypeStruct(state.shape, F32),
            jax.ShapeDtypeStruct((STEPS - 1, sections, own, levels), F32),
            jax.ShapeDtypeStruct((sections, tiles, 8, levels), F32),
            jax.ShapeDtypeStruct((sections, own, tiles * 8), F32),
        ),
        in_specs=specs,
        out_specs=(any_spec,) * 4,
        scratch_shapes=scratch,
        compiler_params=pltpu.CompilerParams(
            collective_id=0, has_side_effects=True, vmem_limit_bytes=64 * 1024 * 1024 - 64 * 1024
        ),
        cost_estimate=pl.CostEstimate(flops=700_000_000, bytes_accessed=1_500_000, transcendentals=0),
    )(*args)
    return pl.pallas_call(
        functools.partial(departing, send_cols.shape[3]),
        out_shape=(jax.ShapeDtypeStruct(state.shape, F32), jax.ShapeDtypeStruct((STEPS, own, heights), F32)),
        in_specs=[any_spec] * 6,
        out_specs=(any_spec, any_spec),
        scratch_shapes=[
            pltpu.VMEM(state.shape, F32),
            pltpu.VMEM(parts.shape, F32),
            pltpu.VMEM(cols.shape, F32),
            pltpu.VMEM(weights.shape, F32),
            pltpu.VMEM(abel_matrix.shape, F32),
            pltpu.VMEM(observed.shape, F32),
            pltpu.VMEM(observed.shape, F32),
            dma((6 + 2 * CHUNKS,)),
        ],
        compiler_params=pltpu.CompilerParams(vmem_limit_bytes=64 * 1024 * 1024 - 64 * 1024),
        cost_estimate=pl.CostEstimate(flops=10_000_000, bytes_accessed=800_000, transcendentals=0),
    )(middle, parts, cols, weights, abel_matrix, observed)


def solution(mesh):
    return jax.shard_map(
        functools.partial(shards, mesh.shape["sec"], mesh.shape["tile"]),
        mesh=mesh,
        in_specs=(
            P("sec", None, "tile"),
            P("sec", None, "tile"),
            P("sec", None, "tile"),
            P("sec", None, None),
            P("sec", None),
            P("sec", None, "tile"),
            P("sec", None, "tile"),
            P(),
            P(None, "sec", "tile", None, None),
            P(None, "sec", None, "tile"),
            P(None, "sec", None, "tile"),
            P(None, "sec", "tile"),
            P("sec", None, None),
            P(),
            P(None, ("sec", "tile"), None),
        ),
        out_specs=(P("sec", None, "tile"), P(None, ("sec", "tile"), None)),
        check_vma=False,
    )
```
